32 devices in a mesh: wide: 8 (over z, x), narrow: 4 (over y, core).
Axes of the slice: x: 2, y: 2, z: 4, core: 2. Of those that a mesh axis runs over, the one named last changes fastest.
Arguments:
- tokens: bfloat16 [12288, 768], P(('wide', 'narrow')), may hold values from -6 to 6
- type_ids: int32 [12288], P(('wide', 'narrow')), may hold values from 0 to 1
- segment_ids: int32 [24, 512], P('wide'), may hold values from 0 to 2, as said below
- cotangent: bfloat16 [12288, 768], P(('wide', 'narrow')), may hold values from -6 to 6
- type_table: float32 [2, 768], replicated, may hold values from -3 to 3
- type_first: float32 [2, 768], replicated, may hold values from -448 to 448
- type_second: float32 [2, 768], replicated, may hold values from 6144 to 24576
- norm_gains: float32 [2, 768], replicated, may hold values from 0.5 to 1.5
- gains_first: float32 [2, 768], replicated, may hold values from -640 to 640
- gains_second: float32 [2, 768], replicated, may hold values from 12288 to 49152
- biases: float32 [6, 768], replicated, may hold values from -1.25 to 1.25
- biases_first: float32 [6, 768], replicated, may hold values from -640 to 640
- biases_second: float32 [6, 768], replicated, may hold values from 12288 to 49152
- qkv_weight: float32 [3, 768, 768], P(None, 'wide', 'narrow'), may hold values from -0.21875 to 0.21875
- qkv_first: float32 [3, 768, 768], P(None, 'wide', 'narrow'), may hold values from -640 to 640
- qkv_second: float32 [3, 768, 768], P(None, 'wide', 'narrow'), may hold values from 12288 to 49152
- out_weight: float32 [768, 768], P('narrow', 'wide'), may hold values from -0.875 to 0.875
- out_first: float32 [768, 768], P('narrow', 'wide'), may hold values from -192 to 192
- out_second: float32 [768, 768], P('narrow', 'wide'), may hold values from 1105.92 to 4423.68
- up_weight: float32 [768, 3072], P(None, ('wide', 'narrow')), may hold values from -0.21875 to 0.21875
- up_first: float32 [768, 3072], P(None, ('wide', 'narrow')), may hold values from -224 to 224
- up_second: float32 [768, 3072], P(None, ('wide', 'narrow')), may hold values from 1474.56 to 6144
- up_bias: float32 [3072], P(('wide', 'narrow')), may hold values from -1.25 to 1.25
- up_bias_first: float32 [3072], P(('wide', 'narrow')), may hold values from -224 to 224
- up_bias_second: float32 [3072], P(('wide', 'narrow')), may hold values from 1474.56 to 6144
- down_weight: float32 [3072, 768], P(('wide', 'narrow')), may hold values from -0.109375 to 0.109375
- down_first: float32 [3072, 768], P(('wide', 'narrow')), may hold values from -448 to 448
- down_second: float32 [3072, 768], P(('wide', 'narrow')), may hold values from 4915.2 to 19660.8
Outputs:
- activations: bfloat16 [12288, 768], P(('wide', 'narrow'))
- input_grad: float32 [12288, 768], P(('wide', 'narrow'))
- type_new: float32 [2, 768], replicated
- type_first_new: float32 [2, 768], replicated
- type_second_new: float32 [2, 768], replicated
- gains_new: float32 [2, 768], replicated
- gains_first_new: float32 [2, 768], replicated
- gains_second_new: float32 [2, 768], replicated
- biases_new: float32 [6, 768], replicated
- biases_first_new: float32 [6, 768], replicated
- biases_second_new: float32 [6, 768], replicated
- qkv_new: float32 [3, 768, 768], P(None, 'wide', 'narrow')
- qkv_first_new: float32 [3, 768, 768], P(None, 'wide', 'narrow')
- qkv_second_new: float32 [3, 768, 768], P(None, 'wide', 'narrow')
- out_new: float32 [768, 768], P('narrow', 'wide')
- out_first_new: float32 [768, 768], P('narrow', 'wide')
- out_second_new: float32 [768, 768], P('narrow', 'wide')
- up_new: float32 [768, 3072], P(None, ('wide', 'narrow'))
- up_first_new: float32 [768, 3072], P(None, ('wide', 'narrow'))
- up_second_new: float32 [768, 3072], P(None, ('wide', 'narrow'))
- up_bias_new: float32 [3072], P(('wide', 'narrow'))
- up_bias_first_new: float32 [3072], P(('wide', 'narrow'))
- up_bias_second_new: float32 [3072], P(('wide', 'narrow'))
- down_new: float32 [3072, 768], P(('wide', 'narrow'))
- down_first_new: float32 [3072, 768], P(('wide', 'narrow'))
- down_second_new: float32 [3072, 768], P(('wide', 'narrow'))
The draws below stay inside these ranges and needn't reach their ends.
Inputs may be any that keep to these rules, and one draw needn't show every extreme that they name: `segment_ids`: each packed sequence holds exactly three documents, numbered 0, 1, 2 in order along its 512 rows, each of one row or more; the ids never fall.
All inputs are finite; a program needn't handle non-finite values.
Results may differ from the reference program's by a relative error of at most 0.012.
Values may be sent and summed in bfloat16 or wider, within the bound.
A program may use at most 192 MiB of HBM per device.

```python
import math
import jax
import jax.numpy as jnp
from jax import lax

D = 768
HEADS = 12
HD = 64
FF = 3072
PACK_LEN = 512
STEP = 5
PACKS_ALL = 24
TOKENS = 12288


def draw_segment_ids(key, part):
    key = jax.random.fold_in(key, 7)
    key_marks = jax.random.fold_in(key, 1)
    key_early = jax.random.fold_in(key, 2)
    key_late = jax.random.fold_in(key, 3)
    mark_draws = jax.random.randint(key_marks, (PACKS_ALL, PACK_LEN), 0, max(PACK_LEN // 4, 2))
    early = jax.random.randint(key_early, (PACKS_ALL, 1), 1, PACK_LEN // 2)
    late = jax.random.randint(key_late, (PACKS_ALL, 1), PACK_LEN // 2, PACK_LEN)
    position = jnp.arange(PACK_LEN)[None, :]
    forced = (position == early) | (position == late)
    opening = jnp.where(position == 0, 0, ((mark_draws == 0) | forced).astype(jnp.int32))
    return jnp.minimum(jnp.cumsum(opening, axis=1), 2).astype(jnp.int32)


def place_ends(values, stream_key, smallest, largest):
    shape = values.shape
    place = [jax.random.randint(jax.random.fold_in(stream_key, axis), (), 0, shape[axis]) for axis in range(len(shape))]
    values = values.at[tuple(place)].set(smallest)
    longest = shape.index(max(shape))
    place[longest] = (place[longest] + 1) % shape[longest]
    return values.at[tuple(place)].set(largest)


def strengthened(values, rng, source, target, parts, factor):
    def block_of(dim):
        return (jnp.arange(values.shape[dim]) // (values.shape[dim] // parts)).reshape((-1,) + (1,) * (values.ndim - 1 - dim))

    near = jax.random.permutation(rng, parts)[block_of(target)]
    far = (block_of(target) + parts // 2) % parts
    return jnp.where((block_of(source) == near) | (block_of(source) == far), factor * values, values)


def steps_of(key, shape, split, low, top_value):
    level, own = 1.0, jax.random.fold_in(key, 6)
    for dim, parts in split:
        heights = jnp.exp(jax.random.uniform(jax.random.fold_in(own, dim), (parts,), jnp.float32, low / len(split), top_value / len(split)))
        level = level * jnp.repeat(heights, shape[dim] // parts).reshape([-1 if axis == dim else 1 for axis in range(len(shape))])
    return level


def centred(stream_key, extent, scale, most, split=(), kind=jnp.bfloat16):
    result = scale * jax.random.normal(stream_key, extent, jnp.float32)
    if split:
        result = result * steps_of(stream_key, extent, split, -0.22, 0.18)
    return jnp.clip(result, -most, most).astype(kind)


def bell_draw_with(own_key, extent, deviation, limit, cuts, heavy, held_as=jnp.bfloat16):
    result = deviation * jax.random.normal(own_key, extent, jnp.float32)
    if cuts:
        result = result * steps_of(own_key, extent, cuts, -0.22, 0.18)
    return jnp.clip(strengthened(result, jax.random.fold_in(own_key, 3), *heavy), -limit, limit).astype(held_as)


def setup_inputs(seed: int = 0) -> dict:
    keys = jax.random.split(jax.random.key(seed), 29)
    tokens = bell_draw_with(keys[0], (TOKENS, D), 1.0, 6.0, ((0, 32),), (0, 1, 32, 2.75))
    type_ids = place_ends(jax.random.randint(keys[1], (TOKENS,), 0, 2), jax.random.fold_in(keys[1], 1), 0, 1).astype(jnp.int32)
    segment_ids = draw_segment_ids(jax.random.fold_in(keys[28], 71), 0)
    cotangent = centred(keys[3], (TOKENS, D), 1.0, 6.0, ((0, 32),))
    type_table = centred(keys[4], (2, D), 0.5, 3.0, (), jnp.float32)
    type_first = centred(keys[5], (2, D), (0.7 * TOKENS ** 0.5), 448.0, (), jnp.float32)
    type_second = jnp.clip(jnp.exp(jax.random.uniform(keys[6], (2, D), jnp.float32, math.log(6144.0), math.log(24576.0))), 6144.0, 24576.0)
    norm_gains = jnp.clip(1.0 + 0.1 * jax.random.normal(keys[7], (2, D), jnp.float32), 0.5, 1.5)
    gains_first = centred(keys[8], (2, D), (TOKENS ** 0.5), 640.0, (), jnp.float32)
    gains_second = jnp.clip(jnp.exp(jax.random.uniform(keys[9], (2, D), jnp.float32, math.log(12288.0), math.log(49152.0))), 12288.0, 49152.0)
    biases = centred(keys[10], (6, D), 0.2, 1.25, (), jnp.float32)
    biases_first = centred(keys[11], (6, D), (TOKENS ** 0.5), 640.0, (), jnp.float32)
    biases_second = jnp.clip(jnp.exp(jax.random.uniform(keys[12], (6, D), jnp.float32, math.log(12288.0), math.log(49152.0))), 12288.0, 49152.0)
    qkv_weight = centred(keys[13], (3, D, D), D ** -0.5, 0.21875, ((1, 8), (2, 4)), jnp.float32)
    qkv_first = centred(keys[14], (3, D, D), (TOKENS ** 0.5), 640.0, ((1, 8), (2, 4)), jnp.float32)
    qkv_second = jnp.clip(jnp.exp(math.log(49152.0) - 1.3862944 * jax.random.uniform(keys[15], (3, D, D), jnp.float32) ** steps_of(keys[15], (3, D, D), ((1, 8), (2, 4)), -0.2, 0.2)), 12288.0, 49152.0)
    out_weight = centred(keys[16], (D, D), (D // 16) ** -0.5, 0.875, ((0, 4), (1, 8)), jnp.float32)
    out_first = centred(keys[17], (D, D), (0.3 * TOKENS ** 0.5), 192.0, ((0, 4), (1, 8)), jnp.float32)
    out_second = jnp.clip(jnp.exp(math.log(4423.68) - 1.3862944 * jax.random.uniform(keys[18], (D, D), jnp.float32) ** steps_of(keys[18], (D, D), ((0, 4), (1, 8)), -0.2, 0.2)), 1105.92, 4423.68)
    up_weight = centred(keys[19], (D, FF), D ** -0.5, 0.21875, ((1, 32),), jnp.float32)
    up_first = centred(keys[20], (D, FF), (0.35 * TOKENS ** 0.5), 224.0, ((1, 32),), jnp.float32)
    up_second = jnp.clip(jnp.exp(math.log(6144.0) - 1.4271163 * jax.random.uniform(keys[21], (D, FF), jnp.float32) ** steps_of(keys[21], (D, FF), ((1, 32),), -0.2, 0.2)), 1474.56, 6144.0)
    up_bias = centred(keys[22], (FF,), 0.2, 1.25, ((0, 32),), jnp.float32)
    up_bias_first = centred(keys[23], (FF,), (0.35 * TOKENS ** 0.5), 224.0, ((0, 32),), jnp.float32)
    up_bias_second = jnp.clip(jnp.exp(math.log(6144.0) - 1.4271163 * jax.random.uniform(keys[24], (FF,), jnp.float32) ** steps_of(keys[24], (FF,), ((0, 32),), -0.2, 0.2)), 1474.56, 6144.0)
    down_weight = centred(keys[25], (FF, D), FF ** -0.5, 0.109375, ((0, 32),), jnp.float32)
    down_first = centred(keys[26], (FF, D), (0.65 * TOKENS ** 0.5), 448.0, ((0, 32),), jnp.float32)
    down_second = jnp.clip(jnp.exp(math.log(19660.8) - 1.3862944 * jax.random.uniform(keys[27], (FF, D), jnp.float32) ** steps_of(keys[27], (FF, D), ((0, 32),), -0.2, 0.2)), 4915.2, 19660.8)
    return {"tokens": tokens, "type_ids": type_ids, "segment_ids": segment_ids, "cotangent": cotangent, "type_table": type_table, "type_first": type_first, "type_second": type_second, "norm_gains": norm_gains, "gains_first": gains_first, "gains_second": gains_second, "biases": biases, "biases_first": biases_first, "biases_second": biases_second, "qkv_weight": qkv_weight, "qkv_first": qkv_first, "qkv_second": qkv_second, "out_weight": out_weight, "out_first": out_first, "out_second": out_second, "up_weight": up_weight, "up_first": up_first, "up_second": up_second, "up_bias": up_bias, "up_bias_first": up_bias_first, "up_bias_second": up_bias_second, "down_weight": down_weight, "down_first": down_first, "down_second": down_second}


@jax.custom_vjp
def low(v):
    return lax.optimization_barrier(v.astype(jnp.bfloat16)).astype(jnp.float32)

@jax.custom_vjp
def low_back(v):
    return v

def low_keep(v):
    return (low(v), None)

def low_pass(kept, grad):
    return (grad,)

def back_keep(v):
    return (v, None)

def back_low(kept, grad):
    return (low(grad),)
low.defvjp(low_keep, low_pass)
low_back.defvjp(back_keep, back_low)
norm_eps = 1e-06
masked_score = -1e+30

def norm_rows(values, gain, shift):
    center = lax.optimization_barrier(jnp.mean(values, axis=-1, keepdims=True))
    spread = values - center
    variance = lax.optimization_barrier(jnp.mean(spread * spread, axis=-1, keepdims=True))
    return spread * lax.rsqrt(variance + norm_eps) * gain + shift

def product(left_mat, right_mat):
    return jnp.dot(left_mat, right_mat, precision=lax.Precision.HIGHEST, preferred_element_type=jnp.float32)

def gelu_exact(values):
    return jax.nn.gelu(values, approximate=False)

def pack_attend(pack_item):
    queries, key_rows, values, segment = pack_item
    raw_scores = jnp.einsum('qhd,khd->hqk', queries, key_rows, precision=lax.Precision.HIGHEST)
    scores = low_back(raw_scores * HD ** (-0.5))
    same_doc = segment[:, None] == segment[None, :]
    scores = jnp.where(same_doc[None, :, :], scores, masked_score)
    weights = jax.nn.softmax(scores, axis=-1)
    return jnp.einsum('hqk,khd->qhd', low(weights), values, precision=lax.Precision.HIGHEST)

def layer_forward(inputs, type_rows, segments, params):
    type_table, norm_gains, biases, qkv_weight, out_weight, up_weight, up_bias, down_weight = params
    embedded = inputs + type_table[type_rows]
    normed1 = low(norm_rows(embedded, norm_gains[0], biases[0]))
    qkv_low = low(qkv_weight)
    queries = low(low_back(product(normed1, qkv_low[0]) + biases[1]))
    keys_all = low(low_back(product(normed1, qkv_low[1])))
    values = low(low_back(product(normed1, qkv_low[2]) + biases[2]))
    row_count = normed1.shape[0]
    pack_shape = (row_count // PACK_LEN, PACK_LEN, HEADS, HD)
    attended = lax.map(jax.checkpoint(pack_attend), (queries.reshape(pack_shape), keys_all.reshape(pack_shape), values.reshape(pack_shape), segments))
    attended = low(low_back(attended.reshape(row_count, D)))
    hidden1 = embedded + low_back(product(attended, low(out_weight))) + biases[3]
    normed2 = low(norm_rows(hidden1, norm_gains[1], biases[4]))
    before = low_back(product(normed2, low(up_weight)) + low(up_bias))
    active = low(gelu_exact(before))
    return hidden1 + product(active, low(down_weight)) + biases[5]

def adam_update(weight_in, moment_one, moment_two, gradient, step_rate):
    moment_one = 0.5 * moment_one + 0.5 * gradient
    moment_two = 0.5 * moment_two + 0.5 * gradient * gradient
    correction = 1.0 - 0.5 ** STEP
    direction = moment_one / correction / (jnp.sqrt(moment_two / correction) + 1e-08)
    return (weight_in - step_rate * (direction + 0.01 * weight_in), moment_one, moment_two)

def step_rates():
    return (0.5, 0.4, 0.4, D ** (-0.5), 4.0 * D ** (-0.5), D ** (-0.5), 0.4, FF ** (-0.5))

def add_pair(first_term, second_term):
    return first_term + second_term

def reference(tokens, type_ids, segment_ids, cotangent, type_table, type_first, type_second, norm_gains, gains_first, gains_second, biases, biases_first, biases_second, qkv_weight, qkv_first, qkv_second, out_weight, out_first, out_second, up_weight, up_first, up_second, up_bias, up_bias_first, up_bias_second, down_weight, down_first, down_second):
    params = (type_table, norm_gains, biases, qkv_weight, out_weight, up_weight, up_bias, down_weight)
    moments_one = (type_first, gains_first, biases_first, qkv_first, out_first, up_first, up_bias_first, down_first)
    moments_two = (type_second, gains_second, biases_second, qkv_second, out_second, up_second, up_bias_second, down_second)
    block_rows = 8 * PACK_LEN
    blocks = TOKENS // block_rows
    inputs = tokens.astype(jnp.float32).reshape(blocks, block_rows, D)
    type_blocks = type_ids.reshape(blocks, block_rows)
    segment_blocks = segment_ids.reshape(blocks, 8, PACK_LEN)
    back_blocks = cotangent.astype(jnp.float32).reshape(blocks, block_rows, D)

    def block_step(totals, block_item):
        block_in, block_types, block_segments, block_back = block_item

        def forward(values_in, params_in):
            return layer_forward(values_in, block_types, block_segments, params_in)
        output, pullback = jax.vjp(forward, block_in, params)
        grad_in, grad_params = pullback(block_back)
        totals = jax.tree.map(add_pair, totals, grad_params)
        return (totals, (output.astype(jnp.bfloat16), grad_in))
    zero_grads = jax.tree.map(jnp.zeros_like, params)
    gradients, (outputs, input_grads) = lax.scan(block_step, zero_grads, (inputs, type_blocks, segment_blocks, back_blocks))
    step_sizes = step_rates()
    updated = [adam_update(params[position], moments_one[position], moments_two[position], gradients[position], step_sizes[position]) for position in range(8)]
    return (outputs.reshape(TOKENS, D), input_grads.reshape(TOKENS, D), updated[0][0], updated[0][1], updated[0][2], updated[1][0], updated[1][1], updated[1][2], updated[2][0], updated[2][1], updated[2][2], updated[3][0], updated[3][1], updated[3][2], updated[4][0], updated[4][1], updated[4][2], updated[5][0], updated[5][1], updated[5][2], updated[6][0], updated[6][1], updated[6][2], updated[7][0], updated[7][1], updated[7][2])
```

```python
import math

import jax
import jax.numpy as jnp
from jax import lax
from jax.experimental import pallas as pl
from jax.experimental.pallas import tpu as pltpu
from jax.sharding import PartitionSpec as P

D = 768
HD = 64
FF = 3072
STEP = 5


norm_eps = 1e-06
masked_score = -1e30


def in_blocks(value, dim, size):
    shape = value.shape
    tiles = value.reshape(*shape[:dim], size, shape[dim] // size, *shape[dim + 1 :])
    return jnp.moveaxis(tiles, dim, 0)


def sent_and_summed(value, axis, dim):
    tiles = in_blocks(value, dim, lax.axis_size(axis))
    arrived = lax.all_to_all(tiles, axis, split_axis=0, concat_axis=0, tiled=True)
    return arrived.astype(jnp.float32).sum(axis=0)


def norm_rows(values, gain, shift):
    center = jnp.mean(values, axis=-1, keepdims=True)
    spread = values - center
    variance = jnp.mean(spread * spread, axis=-1, keepdims=True)
    return spread * lax.rsqrt(variance + norm_eps) * gain + shift


def gelu_exact(values):
    return jax.nn.gelu(values, approximate=False)


def times_transposed(left_mat, right_mat):
    return lax.dot_general(
        left_mat, right_mat, (((1,), (1,)), ((), ())), preferred_element_type=jnp.float32
    )


def transposed_times(left_mat, right_mat):
    return lax.dot_general(
        left_mat, right_mat, (((0,), (0,)), ((), ())), preferred_element_type=jnp.float32
    )


def adam_update(weight_in, moment_one, moment_two, gradient, step_rate):
    moment_one = 0.5 * moment_one + 0.5 * gradient
    moment_two = 0.5 * moment_two + 0.5 * gradient * gradient
    correction = 1.0 - 0.5**STEP
    direction = moment_one / correction / (jnp.sqrt(moment_two / correction) + 1e-08)
    return (weight_in - step_rate * (direction + 0.01 * weight_in), moment_one, moment_two)


def step_rates():
    return (0.5, 0.4, 0.4, D ** (-0.5), 4.0 * D ** (-0.5), D ** (-0.5), 0.4, FF ** (-0.5))


def group_rows(values):
    return lax.all_gather(values, "narrow", axis=0, tiled=True)


def group_sums(term_fn, local_rows):
    return lax.psum_scatter(
        term_fn(jnp.int32(0), lax.axis_size("narrow") * local_rows).astype(jnp.bfloat16),
        "narrow",
        scatter_dimension=0,
        tiled=True,
    ).astype(jnp.float32)


def masked_scores(queries, key_rows, segment):
    raw_scores = jnp.einsum(
        "qhd,khd->hqk", queries, key_rows, preferred_element_type=jnp.float32
    ) * HD ** (-0.5)
    same_doc = segment[:, None] == segment[None, :]
    return jnp.where(same_doc[None, :, :], raw_scores, masked_score)


def pack_forward(pack_item):
    queries, key_rows, values, segment = pack_item
    scores = masked_scores(queries, key_rows, segment)
    highest = jnp.max(scores, axis=-1, keepdims=True)
    exponentials = jnp.exp(scores - highest)
    totals = jnp.sum(exponentials, axis=-1, keepdims=True)
    weights = exponentials / totals
    attended = jnp.einsum(
        "hqk,khd->qhd", weights.astype(jnp.bfloat16), values, preferred_element_type=jnp.float32
    )
    return (attended.astype(jnp.bfloat16), (highest + jnp.log(totals))[:, :, 0])


def pack_backward(pack_item):
    queries, key_rows, values, segment, log_totals, grad_attended = pack_item
    scores = masked_scores(queries, key_rows, segment)
    weights = jnp.exp(scores - log_totals[:, :, None])
    grad_values = jnp.einsum(
        "hqk,qhd->khd",
        weights.astype(jnp.bfloat16),
        grad_attended,
        preferred_element_type=jnp.float32,
    )
    grad_weights = jnp.einsum(
        "qhd,khd->hqk", grad_attended, values, preferred_element_type=jnp.float32
    )
    center = jnp.sum(weights * grad_weights, axis=-1, keepdims=True)
    grad_scores = (weights * (grad_weights - center)).astype(jnp.bfloat16)
    grad_queries = jnp.einsum(
        "hqk,khd->qhd", grad_scores, key_rows, preferred_element_type=jnp.float32
    ) * HD ** (-0.5)
    grad_keys = jnp.einsum(
        "hqk,qhd->khd", grad_scores, queries, preferred_element_type=jnp.float32
    ) * HD ** (-0.5)
    return (
        grad_queries.astype(jnp.bfloat16),
        grad_keys.astype(jnp.bfloat16),
        grad_values.astype(jnp.bfloat16),
    )


def shards(
    tokens,
    type_ids,
    segment_ids,
    cotangent,
    type_table,
    type_first,
    type_second,
    norm_gains,
    gains_first,
    gains_second,
    biases,
    biases_first,
    biases_second,
    qkv_weight,
    qkv_first,
    qkv_second,
    out_weight,
    out_first,
    out_second,
    up_weight,
    up_first,
    up_second,
    up_bias,
    up_bias_first,
    up_bias_second,
    down_weight,
    down_first,
    down_second,
):
    local_rows = tokens.shape[0]
    model_width = tokens.shape[1]
    head_cols = qkv_weight.shape[2]
    heads_here = head_cols // HD
    pack_count = segment_ids.shape[0]
    pack_rows = segment_ids.shape[1]
    group_count = pack_count * pack_rows
    narrow_index = lax.axis_index("narrow")
    qkv_low = qkv_weight.astype(jnp.bfloat16)
    out_low = out_weight.astype(jnp.bfloat16)
    up_low = up_weight.astype(jnp.bfloat16)
    up_bias_low = up_bias.astype(jnp.bfloat16)
    down_low = down_weight.astype(jnp.bfloat16)
    qkv_full, out_rows = (
        lax.all_gather(qkv_low, "wide", axis=1, tiled=True),
        lax.all_gather(out_low, "wide", axis=1, tiled=True),
    )
    up_cols, up_bias_cols, down_rows = (
        lax.all_gather(up_low, ("wide", "narrow"), axis=1, tiled=True),
        lax.all_gather(up_bias_low, ("wide", "narrow"), axis=0, tiled=True),
        lax.all_gather(down_low, ("wide", "narrow"), axis=0, tiled=True),
    )
    is_image = (type_ids == 1)[:, None]
    embedded = tokens.astype(jnp.float32) + jnp.where(
        is_image, type_table[1][None, :], type_table[0][None, :]
    )
    normed1_full, norm1_pull = jax.vjp(norm_rows, embedded, norm_gains[0], biases[0])
    normed1 = normed1_full.astype(jnp.bfloat16)
    group_normed = group_rows(normed1)
    head_offset = narrow_index * head_cols
    bias_query = lax.dynamic_slice_in_dim(biases[1], head_offset, head_cols)
    bias_value = lax.dynamic_slice_in_dim(biases[2], head_offset, head_cols)
    bias_stack = jnp.stack([bias_query, jnp.zeros_like(bias_query), bias_value])
    projected = jnp.einsum(
        "rd,sde->sre", group_normed, qkv_full, preferred_element_type=jnp.float32
    )
    qkv_rows = (projected + bias_stack[:, None, :]).astype(jnp.bfloat16)
    qkv_packs = qkv_rows.reshape(3, pack_count, pack_rows, heads_here, HD)
    attended, log_totals = lax.map(
        pack_forward, (qkv_packs[0], qkv_packs[1], qkv_packs[2], segment_ids)
    )
    attended = attended.reshape(group_count, head_cols)

    def out_term(first_row, row_span):
        return jnp.dot(attended, out_rows, preferred_element_type=jnp.float32)

    attn_proj = group_sums(out_term, local_rows)
    hidden1 = embedded + attn_proj + biases[3]
    normed2_full, norm2_pull = jax.vjp(norm_rows, hidden1, norm_gains[1], biases[4])
    normed2 = normed2_full.astype(jnp.bfloat16)
    mlp_input, mlp_back = (normed2, cotangent)
    pre_act = jnp.dot(mlp_input, up_cols, preferred_element_type=jnp.float32) + up_bias_cols.astype(
        jnp.float32
    )
    activated, gelu_pull = jax.vjp(gelu_exact, pre_act)
    act_low = activated.astype(jnp.bfloat16)
    mlp_out = jnp.dot(act_low, down_rows, preferred_element_type=jnp.float32)
    activations = (hidden1 + mlp_out + biases[5]).astype(jnp.bfloat16)
    grad_act = times_transposed(mlp_back, down_rows)
    (grad_pre,) = gelu_pull(grad_act)
    grad_pre_low = grad_pre.astype(jnp.bfloat16)
    grad_down = transposed_times(act_low, mlp_back)
    grad_up = transposed_times(mlp_input, grad_pre_low)
    grad_up_bias = jnp.sum(grad_pre_low.astype(jnp.float32), axis=0)
    grad_normed2 = times_transposed(grad_pre_low, up_cols)
    grad_hidden_part, grad_gain2, grad_shift2 = norm2_pull(grad_normed2)
    cotangent_full = cotangent.astype(jnp.float32)
    grad_hidden = cotangent_full + grad_hidden_part
    grad_hidden_low = grad_hidden.astype(jnp.bfloat16)
    group_back = group_rows(grad_hidden_low)
    grad_attended = times_transposed(group_back, out_rows).astype(jnp.bfloat16)
    grad_out_weight = transposed_times(attended, group_back)
    back_packs = grad_attended.reshape(pack_count, pack_rows, heads_here, HD)
    grad_queries, grad_keys, grad_values = lax.map(
        pack_backward,
        (qkv_packs[0], qkv_packs[1], qkv_packs[2], segment_ids, log_totals, back_packs),
    )
    grad_qkv_rows = jnp.stack([grad_queries, grad_keys, grad_values]).reshape(
        3, group_count, head_cols
    )
    grad_qkv_weight = jnp.einsum(
        "rd,sre->sde", group_normed, grad_qkv_rows, preferred_element_type=jnp.float32
    )
    head_sums = jnp.sum(grad_qkv_rows.astype(jnp.float32), axis=1)

    def in_term(first_row, row_span):
        return jnp.einsum(
            "sre,sde->rd", grad_qkv_rows, qkv_full, preferred_element_type=jnp.float32
        )

    grad_normed1 = group_sums(in_term, local_rows)
    grad_embed_part, grad_gain1, grad_shift1 = norm1_pull(grad_normed1)
    input_grad = grad_hidden + grad_embed_part
    zero_row = jnp.zeros((model_width,), jnp.float32)
    query_sums = lax.dynamic_update_slice_in_dim(zero_row, head_sums[0], head_offset, 0)
    value_sums = lax.dynamic_update_slice_in_dim(zero_row, head_sums[2], head_offset, 0)
    gain_part = jnp.stack([grad_gain1, grad_gain2])
    shift_part = jnp.stack(
        [
            grad_shift1,
            query_sums,
            value_sums,
            jnp.sum(grad_hidden, axis=0),
            grad_shift2,
            jnp.sum(cotangent_full, axis=0),
        ]
    )
    type_part = jnp.stack(
        [
            jnp.sum(jnp.where(is_image, 0.0, input_grad), axis=0),
            jnp.sum(jnp.where(is_image, input_grad, 0.0), axis=0),
        ]
    )
    grad_gains, grad_biases, grad_types = lax.psum(
        (gain_part, shift_part, type_part), ("wide", "narrow")
    )
    owned_qkv, owned_out = (
        sent_and_summed(grad_qkv_weight.astype(jnp.bfloat16), "wide", 1),
        sent_and_summed(grad_out_weight.astype(jnp.bfloat16), "wide", 1),
    )
    owned_up, owned_up_bias, owned_down = (
        lax.psum_scatter(grad_up, ("wide", "narrow"), scatter_dimension=1, tiled=True),
        lax.psum_scatter(grad_up_bias, ("wide", "narrow"), scatter_dimension=0, tiled=True),
        lax.psum_scatter(grad_down, ("wide", "narrow"), scatter_dimension=0, tiled=True),
    )
    step_sizes = step_rates()
    new_type = adam_update(type_table, type_first, type_second, grad_types, step_sizes[0])
    new_gains = adam_update(norm_gains, gains_first, gains_second, grad_gains, step_sizes[1])
    new_biases = adam_update(biases, biases_first, biases_second, grad_biases, step_sizes[2])
    new_qkv = adam_update(qkv_weight, qkv_first, qkv_second, owned_qkv, step_sizes[3])
    new_out = adam_update(out_weight, out_first, out_second, owned_out, step_sizes[4])
    new_up = adam_update(up_weight, up_first, up_second, owned_up, step_sizes[5])
    new_up_bias = adam_update(up_bias, up_bias_first, up_bias_second, owned_up_bias, step_sizes[6])
    new_down = adam_update(down_weight, down_first, down_second, owned_down, step_sizes[7])
    return (
        activations,
        input_grad,
        new_type[0],
        new_type[1],
        new_type[2],
        new_gains[0],
        new_gains[1],
        new_gains[2],
        new_biases[0],
        new_biases[1],
        new_biases[2],
        new_qkv[0],
        new_qkv[1],
        new_qkv[2],
        new_out[0],
        new_out[1],
        new_out[2],
        new_up[0],
        new_up[1],
        new_up[2],
        new_up_bias[0],
        new_up_bias[1],
        new_up_bias[2],
        new_down[0],
        new_down[1],
        new_down[2],
    )


def dot_nn(left_mat, right_mat):
    return lax.dot_general(
        left_mat, right_mat, (((1,), (0,)), ((), ())), preferred_element_type=jnp.float32
    )


def dot_nt(left_mat, right_mat):
    return lax.dot_general(
        left_mat, right_mat, (((1,), (1,)), ((), ())), preferred_element_type=jnp.float32
    )


def dot_tn(left_mat, right_mat):
    return lax.dot_general(
        left_mat, right_mat, (((0,), (0,)), ((), ())), preferred_element_type=jnp.float32
    )


def rows_at(block, size):
    return pl.ds(pl.multiple_of(block * size, size), size)


def row_stats(values):
    center = jnp.mean(values, axis=-1, keepdims=True)
    spread = values - center
    variance = jnp.mean(spread * spread, axis=-1, keepdims=True)
    scale = lax.rsqrt(variance + norm_eps)
    return spread * scale, scale


def column_sums(values):
    return jnp.sum(values, axis=0, keepdims=True)


ROW = 128
OWN = 384
CHIP = 768
HALF_PACK = 256
PACK = 512
BLK = 96
HALF_BLK = 48
ATTN, UP, DOWN = 0, 1, 2
GAIN_ROW, BIAS_ROW, TYPE_ROW, UP_BIAS_ROW, SMALL_ROWS = 0, 2, 8, 10, 16


def layer_kernel(
    own, unit_bias, tokens, is_image, cotangent, query_doc, key_doc, type_table, gains, biases, qkv_bias,
    act_out, input_grad, grad_out, small_out,
    full, part, g_all, n1_all, n2_all, dh_all, qkv, att, dkv_far, probs, mask, act, slope, datt,
    key_acc, value_acc, embedded, hidden1, own_sum, swap_send, swap_recv, bias_slots, bias_row, small,
    small_recv, rx, ry, rdx, rdy, rz,
    gz_s, gz_r, gx_s, gx_r, gy_s, gy_r, gfx_s, gfx_r, gfy_s, gfy_r,
    sz_s, sz_r, sx_s, sx_r, sy_s, sy_r, sdx_s, sdx_r, sdy_s, sdy_r,
    spread_s, spread_r, swap_s, swap_r, far_s, far_r, bias_s, bias_r, small_s, small_r,
):
    f32, bf16 = jnp.float32, jnp.bfloat16
    wide = lax.axis_index("wide")
    narrow = lax.axis_index("narrow")
    z, x = wide // 2, wide % 2
    y, core = narrow // 2, narrow % 2
    z_of = [z, z + 1 - 2 * (z % 2), (z + 2) % 4, 3 - z]
    sibling = (wide, y * 2 + (1 - core))
    x_side = (z * 2 + (1 - x), narrow)
    y_side = (wide, (1 - y) * 2 + core)
    z_side = [None] + [(z_of[j] * 2 + x, narrow) for j in (1, 2, 3)]

    def copy(src, dst, send, recv, to):
        return pltpu.make_async_remote_copy(
            src_ref=src, dst_ref=dst, send_sem=send, recv_sem=recv, device_id=to,
            device_id_type=pl.DeviceIdType.MESH,
        )

    pending = []

    def start(*args):
        one = copy(*args)
        one.start()
        pending.append(one)
        return one

    barrier = pltpu.get_barrier_semaphore()
    for to in (sibling, x_side, y_side, z_side[1], z_side[2], z_side[3]):
        pl.semaphore_signal(barrier, inc=1, device_id=to, device_id_type=pl.DeviceIdType.MESH)
    pl.semaphore_wait(barrier, 6)

    def slot(ref, kind, yy, zz, xx, first=0, size=BLK):
        row = pl.multiple_of((zz * 2 + xx) * BLK + first, 16)
        return ref.at[kind, yy, pl.ds(row, size)]

    def gather_z(kind):
        mine = slot(full, kind, y, z, x)
        for j in (1, 2, 3):
            start(mine, mine, gz_s.at[kind, j], gz_r.at[kind, j], z_side[j])

    def gather_on(kind, j):
        block = slot(full, kind, y, z_of[j], x)
        if j:
            copy(block, block, gz_s.at[kind, j], gz_r.at[kind, j], z_side[j]).wait_recv()
        start(block, block, gx_s.at[kind, j], gx_r.at[kind, j], x_side)
        start(block, block, gy_s.at[kind, j], gy_r.at[kind, j], y_side)

    def gather_far(kind, j):
        zz = z_of[j]
        block = slot(full, kind, y, zz, 1 - x)
        copy(block, block, gx_s.at[kind, j], gx_r.at[kind, j], x_side).wait_recv()
        half = slot(full, kind, y, zz, 1 - x, 0, HALF_BLK)
        start(half, half, gfy_s.at[kind, j], gfy_r.at[kind, j], y_side)
        block = slot(full, kind, 1 - y, zz, x)
        copy(block, block, gy_s.at[kind, j], gy_r.at[kind, j], y_side).wait_recv()
        half = slot(full, kind, 1 - y, zz, x, HALF_BLK, HALF_BLK)
        start(half, half, gfx_s.at[kind, j], gfx_r.at[kind, j], x_side)

    def gather_done(kind):
        for j in range(4):
            half = slot(full, kind, 1 - y, z_of[j], 1 - x, 0, HALF_BLK)
            copy(half, half, gfy_s.at[kind, j], gfy_r.at[kind, j], y_side).wait_recv()
            half = slot(full, kind, 1 - y, z_of[j], 1 - x, HALF_BLK, HALF_BLK)
            copy(half, half, gfx_s.at[kind, j], gfx_r.at[kind, j], x_side).wait_recv()

    def scatter_far(kind, j):
        half = slot(part, kind, 1 - y, z_of[j], 1 - x, 0, HALF_BLK)
        start(half, rdy.at[kind, j], sdy_s.at[kind, j], sdy_r.at[kind, j], y_side)
        half = slot(part, kind, 1 - y, z_of[j], 1 - x, HALF_BLK, HALF_BLK)
        start(half, rdx.at[kind, j], sdx_s.at[kind, j], sdx_r.at[kind, j], x_side)

    def add_in(ref, arrived):
        ref[...] = (ref[...].astype(f32) + arrived[...].astype(f32)).astype(bf16)

    def scatter_near(kind, j):
        zz = z_of[j]
        half = slot(part, kind, y, zz, 1 - x, 0, HALF_BLK)
        copy(half, rdy.at[kind, j], sdy_s.at[kind, j], sdy_r.at[kind, j], y_side).wait_recv()
        add_in(half, rdy.at[kind, j])
        start(slot(part, kind, y, zz, 1 - x), rx.at[kind, j], sx_s.at[kind, j], sx_r.at[kind, j], x_side)
        half = slot(part, kind, 1 - y, zz, x, HALF_BLK, HALF_BLK)
        copy(half, rdx.at[kind, j], sdx_s.at[kind, j], sdx_r.at[kind, j], x_side).wait_recv()
        add_in(half, rdx.at[kind, j])
        start(slot(part, kind, 1 - y, zz, x), ry.at[kind, j], sy_s.at[kind, j], sy_r.at[kind, j], y_side)

    def scatter_z(kind, j):
        block = slot(part, kind, y, z_of[j], x)
        copy(block, rx.at[kind, j], sx_s.at[kind, j], sx_r.at[kind, j], x_side).wait_recv()
        copy(block, ry.at[kind, j], sy_s.at[kind, j], sy_r.at[kind, j], y_side).wait_recv()
        total = block[...].astype(f32) + rx[kind, j].astype(f32) + ry[kind, j].astype(f32)
        if j:
            block[...] = total.astype(bf16)
            start(block, rz.at[kind, j], sz_s.at[kind, j], sz_r.at[kind, j], z_side[j])
        else:
            grad_out[kind] = total

    def scatter_done(kind):
        for j in (1, 2, 3):
            copy(rz.at[kind, j], rz.at[kind, j], sz_s.at[kind, j], sz_r.at[kind, j], z_side[j]).wait_recv()
        grad_out[kind] = grad_out[kind] + (
            rz[kind, 1].astype(f32) + rz[kind, 2].astype(f32) + rz[kind, 3].astype(f32)
        )

    def place(which, block):
        return rows_at((3 * which + block + 4 * y) % 6, ROW)

    def hand_over(ref, use, block):
        here = ref.at[place(core, block)]
        return copy(here, here, spread_s.at[use, block], spread_r.at[use, block], sibling)

    def spread_done(ref, use):
        for block in range(3):
            there = ref.at[place(1 - core, block)]
            copy(there, there, spread_s.at[use, block], spread_r.at[use, block], sibling).wait_recv()
            pending.append(hand_over(ref, use, block))

    def swap_sums(use, term):
        def for_sibling(block, carry):
            rows = rows_at(block, ROW)
            swap_send[use, rows] = term(place(1 - core, block)).astype(bf16)
            copy(
                swap_send.at[use, rows], swap_recv.at[use, rows], swap_s.at[use, block],
                swap_r.at[use, block], sibling,
            ).start()
            return carry

        def for_self(block, carry):
            own_sum[rows_at(block, ROW)] = term(place(core, block))
            return carry

        lax.fori_loop(0, 3, for_sibling, 0)
        lax.fori_loop(0, 3, for_self, 0)

    def swap_done(use):
        for block in range(3):
            rows = pl.ds(block * ROW, ROW)
            one = copy(
                swap_send.at[use, rows], swap_recv.at[use, rows], swap_s.at[use, block],
                swap_r.at[use, block], sibling,
            )
            one.wait_recv()
            pending.append(one)

    def swapped(use, rows):
        return own_sum[rows] + swap_recv[use, rows].astype(f32)

    for kind in (ATTN, UP, DOWN):
        slot(full, kind, y, z, x)[...] = own[kind]
    gather_z(ATTN)
    gather_on(ATTN, 0)

    def give_cotangent(block, carry):
        g_all[place(core, block)] = cotangent[rows_at(block, ROW)]
        hand_over(g_all, 0, block).start()
        return carry

    def first_norm(block, carry):
        rows = rows_at(block, ROW)
        values = tokens[rows].astype(f32) + jnp.where(
            is_image[rows] > 0, type_table[1:2, :], type_table[0:1, :]
        )
        embedded[rows] = values
        xhat, _ = row_stats(values)
        n1_all[place(core, block)] = (xhat * gains[0:1, :] + biases[0:1, :]).astype(bf16)
        hand_over(n1_all, 1, block).start()
        return carry

    lax.fori_loop(0, 3, first_norm, 0)

    half_rows = pl.ds(PACK, HALF_PACK)
    far_rows = pl.ds(CHIP, HALF_PACK)
    over_y = copy(n1_all.at[half_rows], n1_all.at[far_rows], far_s.at[0], far_r.at[0], y_side)
    relay = copy(n1_all.at[far_rows], n1_all.at[far_rows], far_s.at[1], far_r.at[1], sibling)
    holds_half = (core + y) == 1

    @pl.when(holds_half)
    def _():
        over_y.start()

    def bias_hop(first, size, index, to):
        ref = bias_slots.at[pl.ds(first, size)]
        return start(ref, ref, bias_s.at[index], bias_r.at[index], to)

    def bias_wait(first, size, index, to):
        ref = bias_slots.at[pl.ds(first, size)]
        copy(ref, ref, bias_s.at[index], bias_r.at[index], to).wait_recv()

    bias_first = (y * 2 + x) * 4
    bias_slots[bias_first + z] = unit_bias[...]
    for j in (1, 2, 3):
        bias_hop(bias_first + z, 1, j, z_side[j])

    lax.fori_loop(0, 3, give_cotangent, 0)
    gather_z(UP)

    for tile in range(3):
        rows = pl.ds(tile * 256, 256)
        mask[rows] = jnp.where(
            query_doc[rows] == key_doc[tile // 2 : tile // 2 + 1, :], 0.0, masked_score
        ).astype(bf16)
    small[...] = jnp.zeros_like(small)
    for yy in (0, 1):
        att[yy, :, 0:HD] = jnp.zeros((CHIP, HD), bf16)
        qkv[yy, :, 576:768] = jnp.zeros((CHIP + HALF_PACK, 192), bf16)

    gather_on(ATTN, 1)
    gather_far(ATTN, 0)
    gather_on(ATTN, 2)
    gather_far(ATTN, 1)

    @pl.when(jnp.logical_not(holds_half))
    def _():
        over_y.wait_recv()
        relay.start()

    for j in (1, 2, 3):
        bias_wait(bias_first + z_of[j], 1, j, z_side[j])
    bias_hop(bias_first, 4, 4, x_side)
    gather_on(ATTN, 3)
    gather_far(ATTN, 2)
    bias_wait((y * 2 + 1 - x) * 4, 4, 4, x_side)
    bias_hop(y * 8, 8, 5, y_side)
    gather_on(UP, 0)
    gather_far(ATTN, 3)
    gather_on(UP, 1)
    gather_z(DOWN)

    spread_done(n1_all, 1)

    @pl.when(holds_half)
    def _():
        relay.wait_recv()

    gather_done(ATTN)
    gather_far(UP, 0)

    lane = lax.broadcasted_iota(jnp.int32, (1, 640), 1)
    shrink = jnp.where(lane >= 384, HD ** (-0.5), 1.0).astype(f32)

    def project(yy):
        def body(tile, carry):
            rows = rows_at(tile, 256)
            found = dot_nn(n1_all[rows], full[ATTN, yy, :, 0:640]) + qkv_bias[yy]
            qkv[yy, rows, 0:576] = (found * shrink)[:, 0:576].astype(bf16)
            return carry

        lax.fori_loop(0, 4, body, 0)

    def attend(yy, head):
        def body(tile, carry):
            rows = rows_at(tile, 256)
            keys = rows_at(tile // 2, PACK)
            queries = qkv[yy, rows, 384 + HD * head : 448 + HD * head]
            key_rows = qkv[yy, keys, HD * head : HD * head + HD]
            values = qkv[yy, keys, 192 + HD * head : 256 + HD * head]
            scores = dot_nt(queries, key_rows) + mask[rows].astype(f32)
            exponentials = jnp.exp(scores - jnp.max(scores, axis=-1, keepdims=True))
            totals = jnp.sum(exponentials, axis=-1, keepdims=True)
            weights = (exponentials * (1.0 / totals)).astype(bf16)
            probs[yy * 3 + head, rows] = weights
            att[yy, rows, HD + HD * head : 2 * HD + HD * head] = dot_nn(weights, values).astype(bf16)
            return carry

        lax.fori_loop(0, 3, body, 0)

    project(0)
    gather_on(UP, 2)
    project(1)
    gather_far(UP, 1)
    attend(0, 0)
    gather_on(UP, 3)
    attend(0, 1)
    gather_far(UP, 2)
    attend(0, 2)
    gather_on(DOWN, 0)
    attend(1, 0)
    gather_far(UP, 3)
    gather_on(DOWN, 1)
    attend(1, 1)
    gather_far(DOWN, 0)
    attend(1, 2)
    gather_on(DOWN, 2)

    def out_term(rows):
        return dot_nt(att[0, rows], full[ATTN, 0, :, 512:768]) + dot_nt(
            att[1, rows], full[ATTN, 1, :, 512:768]
        )

    swap_sums(0, out_term)
    gather_far(DOWN, 1)
    bias_wait((1 - y) * 8, 8, 5, y_side)
    for yy in (0, 1):
        for xx in (0, 1):
            for zz in range(4):
                first = yy * 768 + (zz * 2 + xx) * BLK
                bias_row[:, first : first + BLK] = bias_slots[(yy * 2 + xx) * 4 + zz, :, 0:BLK]
    swap_done(0)

    def second_norm(block, carry):
        rows = rows_at(block, ROW)
        values = embedded[rows] + swapped(0, rows) + biases[3:4, :]
        hidden1[rows] = values
        xhat, _ = row_stats(values)
        n2_all[place(core, block)] = (xhat * gains[1:2, :] + biases[4:5, :]).astype(bf16)
        hand_over(n2_all, 2, block).start()
        return carry

    lax.fori_loop(0, 3, second_norm, 0)
    gather_on(DOWN, 3)
    spread_done(n2_all, 2)
    gather_done(UP)
    gather_far(DOWN, 2)

    def up_chunk(yy, chunk):
        lanes = slice(chunk * 256, chunk * 256 + 256)
        shift = bias_row[0:1, yy * 768 + chunk * 256 : yy * 768 + chunk * 256 + 256]

        def body(tile, carry):
            rows = rows_at(tile, 256)
            before = dot_nt(n2_all[rows], full[UP, yy, lanes]) + shift
            normal = 0.5 + 0.5 * lax.erf(before * (0.5**0.5))
            act[yy, rows, lanes] = (before * normal).astype(bf16)
            bell = jnp.exp(-0.5 * before * before) * ((2.0 * math.pi) ** -0.5)
            slope[yy, rows, lanes] = (normal + before * bell).astype(bf16)
            return carry

        lax.fori_loop(0, 3, body, 0)

    for yy in (0, 1):
        for chunk in range(3):
            up_chunk(yy, chunk)
            if (yy, chunk) == (0, 1):
                gather_far(DOWN, 3)
    spread_done(g_all, 0)

    def down_grad(yy):
        for chunk in range(3):
            lanes = slice(chunk * 256, chunk * 256 + 256)
            part[DOWN, yy, lanes] = dot_tn(act[yy, :, lanes], g_all[...]).astype(bf16)

    down_grad(1 - y)
    gather_done(DOWN)
    for j in (1, 2, 3, 0):
        scatter_far(DOWN, j)
    down_grad(y)

    def du_chunk(yy, chunk):
        lanes = slice(chunk * 256, chunk * 256 + 256)

        def body(tile, carry):
            rows = rows_at(tile, 256)
            grad = dot_nt(g_all[rows], full[DOWN, yy, lanes]) * slope[yy, rows, lanes].astype(f32)
            grad = grad.astype(bf16)
            slope[yy, rows, lanes] = grad
            return carry + column_sums(grad.astype(f32))

        total = lax.fori_loop(0, 3, body, jnp.zeros((1, 256), f32))
        for cc in (0, 1):
            small[UP_BIAS_ROW + 2 * cc + yy : UP_BIAS_ROW + 2 * cc + yy + 1, lanes] = jnp.where(
                core == cc, total, 0.0
            )

    def mlp_term(rows):
        return dot_nn(act[0, rows], full[DOWN, 0]) + dot_nn(act[1, rows], full[DOWN, 1])

    def du_term(rows):
        return dot_nn(slope[0, rows], full[UP, 0]) + dot_nn(slope[1, rows], full[UP, 1])

    def up_grad(yy):
        for chunk in range(3):
            lanes = slice(chunk * 256, chunk * 256 + 256)
            part[UP, yy, lanes] = dot_tn(slope[yy, :, lanes], n2_all[...]).astype(bf16)

    for yy in (0, 1):
        for chunk in range(3):
            du_chunk(yy, chunk)
        scatter_near(DOWN, 1 + yy)
    swap_sums(2, du_term)
    scatter_near(DOWN, 3)
    scatter_near(DOWN, 0)
    up_grad(1 - y)
    scatter_z(DOWN, 1)
    for j in (1, 2, 3, 0):
        scatter_far(UP, j)
    scatter_z(DOWN, 2)
    up_grad(y)
    scatter_z(DOWN, 3)
    swap_done(2)

    def second_norm_back(block, carry):
        rows = rows_at(block, ROW)
        grad = swapped(2, rows)
        xhat, scale = row_stats(hidden1[rows])
        scaled = grad * gains[1:2, :]
        back = (
            scaled
            - jnp.mean(scaled, axis=-1, keepdims=True)
            - xhat * jnp.mean(scaled * xhat, axis=-1, keepdims=True)
        ) * scale
        given = cotangent[rows].astype(f32)
        total = given + back
        input_grad[rows] = total
        dh_all[place(core, block)] = total.astype(bf16)
        hand_over(dh_all, 3, block).start()
        small[1:2, :] += column_sums(grad * xhat)
        small[6:7, :] += column_sums(grad)
        small[5:6, :] += column_sums(total)
        small[7:8, :] += column_sums(given)
        return carry

    lax.fori_loop(0, 3, second_norm_back, 0)
    scatter_z(DOWN, 0)
    scatter_near(UP, 1)
    scatter_near(UP, 2)
    swap_sums(1, mlp_term)
    spread_done(dh_all, 3)

    def project_back(yy):
        def body(tile, carry):
            rows = rows_at(tile, 256)
            datt[yy, rows] = dot_nn(dh_all[rows], full[ATTN, yy, :, 512:768]).astype(bf16)
            return carry

        lax.fori_loop(0, 3, body, 0)

    def attend_back(yy, head):
        key_acc[...] = jnp.zeros_like(key_acc)
        value_acc[...] = jnp.zeros_like(value_acc)

        def body(tile, carry):
            rows = rows_at(tile, 256)
            keys = rows_at(tile // 2, PACK)
            queries = qkv[yy, rows, 384 + HD * head : 448 + HD * head]
            key_rows = qkv[yy, keys, HD * head : HD * head + HD]
            values = qkv[yy, keys, 192 + HD * head : 256 + HD * head]
            grad = datt[yy, rows, HD + HD * head : 2 * HD + HD * head]
            weights = probs[yy * 3 + head, rows]
            weights_full = weights.astype(f32)
            back = dot_nt(grad, values)
            center = jnp.sum(weights_full * back, axis=-1, keepdims=True)
            grad_scores = (weights_full * (back - center)).astype(bf16)
            qkv[yy, rows, 384 + HD * head : 448 + HD * head] = (
                dot_nn(grad_scores, key_rows) * HD ** (-0.5)
            ).astype(bf16)
            value_acc[keys] += dot_tn(weights, grad)
            key_acc[keys] += dot_tn(grad_scores, queries)
            return carry

        lax.fori_loop(0, 3, body, 0)
        qkv[yy, :, HD * head : HD * head + HD] = key_acc[...].astype(bf16)
        qkv[yy, :, 192 + HD * head : 256 + HD * head] = value_acc[...].astype(bf16)

    project_back(0)
    project_back(1)
    scatter_near(UP, 3)
    scatter_done(DOWN)
    attend_back(0, 0)
    scatter_near(UP, 0)
    attend_back(0, 1)
    scatter_z(UP, 1)
    attend_back(0, 2)
    scatter_z(UP, 2)
    attend_back(1, 0)
    scatter_z(UP, 3)
    attend_back(1, 1)
    scatter_z(UP, 0)
    attend_back(1, 2)

    for yy in (0, 1):
        start(qkv.at[yy, far_rows, 0:384], dkv_far.at[yy], far_s.at[2 + yy], far_r.at[2 + yy], y_side)
    swap_done(1)

    def finish_act(block, carry):
        rows = rows_at(block, ROW)
        act_out[rows] = (hidden1[rows] + swapped(1, rows) + biases[5:6, :]).astype(bf16)
        return carry

    lax.fori_loop(0, 3, finish_act, 0)
    scatter_done(UP)
    for yy in (0, 1):
        copy(
            qkv.at[yy, far_rows, 0:384], dkv_far.at[yy], far_s.at[2 + yy], far_r.at[2 + yy], y_side
        ).wait_recv()
        qkv[yy, half_rows, 0:384] = (
            qkv[yy, half_rows, 0:384].astype(f32) + dkv_far[yy].astype(f32)
        ).astype(bf16)

    def attn_grad(yy):
        for chunk in range(3):
            lanes = slice(chunk * 256, chunk * 256 + 256)
            n1_part = n1_all[0:CHIP, lanes]
            part[ATTN, yy, lanes, 0:512] = dot_tn(n1_part, qkv[yy, 0:CHIP, 0:512]).astype(bf16)
            part[ATTN, yy, lanes, 512:768] = (
                dot_tn(n1_part, qkv[yy, 0:CHIP, 512:768]) + dot_tn(dh_all[:, lanes], att[yy])
            ).astype(bf16)

    attn_grad(1 - y)
    for j in (1, 2, 3, 0):
        scatter_far(ATTN, j)
    attn_grad(y)

    def in_term(rows):
        return dot_nt(qkv[0, rows], full[ATTN, 0]) + dot_nt(qkv[1, rows], full[ATTN, 1])

    scatter_near(ATTN, 1)
    swap_sums(3, in_term)
    scatter_near(ATTN, 2)
    for yy in (0, 1):
        sums = column_sums(qkv[yy, 0:CHIP, 192:576].astype(f32))
        for cc in (0, 1):
            first = yy * 384 + cc * 192
            small[4:5, first : first + 192] = jnp.where(core == cc, sums[:, 0:192], 0.0)
            small[3:4, first : first + 192] = jnp.where(core == cc, sums[:, 192:384], 0.0)
    swap_done(3)
    scatter_near(ATTN, 3)

    def first_norm_back(block, carry):
        rows = rows_at(block, ROW)
        grad = swapped(3, rows)
        xhat, scale = row_stats(embedded[rows])
        scaled = grad * gains[0:1, :]
        back = (
            scaled
            - jnp.mean(scaled, axis=-1, keepdims=True)
            - xhat * jnp.mean(scaled * xhat, axis=-1, keepdims=True)
        ) * scale
        total = input_grad[rows] + back
        input_grad[rows] = total
        small[0:1, :] += column_sums(grad * xhat)
        small[2:3, :] += column_sums(grad)
        image = is_image[rows] > 0
        small[8:9, :] += column_sums(jnp.where(image, 0.0, total))
        small[9:10, :] += column_sums(jnp.where(image, total, 0.0))
        return carry

    lax.fori_loop(0, 3, first_norm_back, 0)

    start(small, small_recv.at[4], small_s.at[4], small_r.at[4], sibling)
    scatter_near(ATTN, 0)
    copy(small, small_recv.at[4], small_s.at[4], small_r.at[4], sibling).wait_recv()
    small_recv[5] = small[...] + small_recv[4]
    start(small_recv.at[5], small_recv.at[6], small_s.at[5], small_r.at[5], x_side)
    scatter_z(ATTN, 1)
    copy(small_recv.at[5], small_recv.at[6], small_s.at[5], small_r.at[5], x_side).wait_recv()
    small_recv[7] = small_recv[5] + small_recv[6]
    start(small_recv.at[7], small_recv.at[8], small_s.at[6], small_r.at[6], y_side)
    scatter_z(ATTN, 2)
    copy(small_recv.at[7], small_recv.at[8], small_s.at[6], small_r.at[6], y_side).wait_recv()
    small_recv[z] = small_recv[7] + small_recv[8]
    for j in (1, 2, 3):
        start(small_recv.at[z], small_recv.at[z], small_s.at[j], small_r.at[j], z_side[j])
    scatter_z(ATTN, 3)
    scatter_z(ATTN, 0)
    for j in (1, 2, 3):
        there = small_recv.at[z_of[j]]
        copy(there, there, small_s.at[j], small_r.at[j], z_side[j]).wait_recv()
    small_out[...] = (small_recv[0] + small_recv[1]) + (small_recv[2] + small_recv[3])
    scatter_done(ATTN)

    for one in pending:
        one.wait_send()

    @pl.when(holds_half)
    def _():
        over_y.wait_send()

    @pl.when(jnp.logical_not(holds_half))
    def _():
        relay.wait_send()


def run_layer(*operands):
    f32, bf16 = jnp.float32, jnp.bfloat16
    vmem, dma = pltpu.VMEM, pltpu.SemaphoreType.DMA
    scratch = [
        vmem((3, 2, 768, 768), bf16),
        vmem((3, 2, 768, 768), bf16),
        vmem((CHIP, 768), bf16),
        vmem((CHIP + HALF_PACK, 768), bf16),
        vmem((CHIP, 768), bf16),
        vmem((CHIP, 768), bf16),
        vmem((2, CHIP + HALF_PACK, 768), bf16),
        vmem((2, CHIP, 256), bf16),
        vmem((2, HALF_PACK, 384), bf16),
        vmem((6, CHIP, PACK), bf16),
        vmem((CHIP, PACK), bf16),
        vmem((2, CHIP, 768), bf16),
        vmem((2, CHIP, 768), bf16),
        vmem((2, CHIP, 256), bf16),
        vmem((CHIP + HALF_PACK, HD), f32),
        vmem((CHIP + HALF_PACK, HD), f32),
        vmem((OWN, 768), f32),
        vmem((OWN, 768), f32),
        vmem((OWN, 768), f32),
        vmem((4, OWN, 768), bf16),
        vmem((4, OWN, 768), bf16),
        vmem((16, 8, 128), f32),
        vmem((8, 1536), f32),
        vmem((SMALL_ROWS, 768), f32),
        vmem((9, SMALL_ROWS, 768), f32),
        vmem((3, 4, BLK, 768), bf16),
        vmem((3, 4, BLK, 768), bf16),
        vmem((3, 4, HALF_BLK, 768), bf16),
        vmem((3, 4, HALF_BLK, 768), bf16),
        vmem((3, 4, BLK, 768), bf16),
    ]
    scratch += [dma((3, 4))] * 20
    scratch += [dma((4, 3))] * 4 + [dma((4,))] * 2 + [dma((6,))] * 2 + [dma((7,))] * 2
    whole = pl.BlockSpec(memory_space=vmem)
    return pl.pallas_call(
        layer_kernel,
        out_shape=(
            jax.ShapeDtypeStruct((OWN, 768), bf16),
            jax.ShapeDtypeStruct((OWN, 768), f32),
            jax.ShapeDtypeStruct((3, BLK, 768), f32),
            jax.ShapeDtypeStruct((SMALL_ROWS, 768), f32),
        ),
        in_specs=[whole] * len(operands),
        out_specs=(whole,) * 4,
        scratch_shapes=scratch,
        compiler_params=pltpu.CompilerParams(
            collective_id=0, has_side_effects=True, vmem_limit_bytes=63 * 2**20
        ),
    )(*operands)


def fits_kernel(mesh):
    return dict(mesh.shape) == {"wide": 8, "narrow": 4}


def fused_shards(
    tokens,
    type_ids,
    segment_ids,
    cotangent,
    type_table,
    type_first,
    type_second,
    norm_gains,
    gains_first,
    gains_second,
    biases,
    biases_first,
    biases_second,
    qkv_weight,
    qkv_first,
    qkv_second,
    out_weight,
    out_first,
    out_second,
    up_weight,
    up_first,
    up_second,
    up_bias,
    up_bias_first,
    up_bias_second,
    down_weight,
    down_first,
    down_second,
):
    f32, bf16 = jnp.float32, jnp.bfloat16
    wide, narrow = lax.axis_index("wide"), lax.axis_index("narrow")
    y, core = narrow // 2, narrow % 2
    attn = jnp.concatenate(
        [qkv_weight[1], qkv_weight[2], qkv_weight[0], out_weight.T], axis=1
    )
    own = jnp.stack([attn, up_weight.T, down_weight]).astype(bf16)
    unit_bias = jnp.broadcast_to(
        jnp.pad(up_bias.astype(bf16).astype(f32), (0, 128 - BLK))[None, :], (8, 128)
    )
    is_image = (type_ids == 1).astype(f32)[:, None]
    first, middle, last = segment_ids[0], segment_ids[1], segment_ids[2]
    early = y == 0
    near = jnp.where(early, middle[:HALF_PACK], middle[HALF_PACK:])
    far = jnp.where(early, middle[HALF_PACK:], middle[:HALF_PACK])
    whole = jnp.where(early, first, last)
    query_doc = jnp.concatenate([whole, near])[:, None]
    key_doc = jnp.stack([whole, jnp.concatenate([near, far])])
    by_head = biases.reshape(6, 2, 2, 192)
    by_head = lax.dynamic_index_in_dim(by_head, core, 2, keepdims=False)
    zeros = jnp.zeros((2, 192), f32)
    qkv_bias = jnp.concatenate([zeros, by_head[2], by_head[1], zeros[:, :64]], axis=1)[:, None, :]
    activations, input_grad, grads, small = run_layer(
        own, unit_bias, tokens, is_image, cotangent, query_doc, key_doc, type_table, norm_gains,
        biases, qkv_bias,
    )
    grad_attn, grad_up, grad_down = grads[0], grads[1].T, grads[2]
    grad_qkv = jnp.stack([grad_attn[:, 384:576], grad_attn[:, 0:192], grad_attn[:, 192:384]])
    grad_out = grad_attn[:, 576:768].T
    grad_up_bias = lax.dynamic_slice(small, (UP_BIAS_ROW + 2 * core + y, wide * BLK), (1, BLK))[0]
    step_sizes = step_rates()
    updates = [
        adam_update(type_table, type_first, type_second, small[8:10], step_sizes[0]),
        adam_update(norm_gains, gains_first, gains_second, small[0:2], step_sizes[1]),
        adam_update(biases, biases_first, biases_second, small[2:8], step_sizes[2]),
        adam_update(qkv_weight, qkv_first, qkv_second, grad_qkv, step_sizes[3]),
        adam_update(out_weight, out_first, out_second, grad_out, step_sizes[4]),
        adam_update(up_weight, up_first, up_second, grad_up, step_sizes[5]),
        adam_update(up_bias, up_bias_first, up_bias_second, grad_up_bias, step_sizes[6]),
        adam_update(down_weight, down_first, down_second, grad_down, step_sizes[7]),
    ]
    return (activations, input_grad) + tuple(value for update in updates for value in update)


def solution(mesh):
    placed = (
        P(("wide", "narrow"), None),
        P(("wide", "narrow")),
        P("wide", None),
        P(("wide", "narrow"), None),
        P(),
        P(),
        P(),
        P(),
        P(),
        P(),
        P(),
        P(),
        P(),
        P(None, "wide", "narrow"),
        P(None, "wide", "narrow"),
        P(None, "wide", "narrow"),
        P("narrow", "wide"),
        P("narrow", "wide"),
        P("narrow", "wide"),
        P(None, ("wide", "narrow")),
        P(None, ("wide", "narrow")),
        P(None, ("wide", "narrow")),
        P(("wide", "narrow")),
        P(("wide", "narrow")),
        P(("wide", "narrow")),
        P(("wide", "narrow"), None),
        P(("wide", "narrow"), None),
        P(("wide", "narrow"), None),
    )
    return jax.shard_map(
        fused_shards if fits_kernel(mesh) else shards,
        mesh=mesh,
        in_specs=placed,
        out_specs=(
            P(("wide", "narrow"), None),
            P(("wide", "narrow"), None),
            P(),
            P(),
            P(),
            P(),
            P(),
            P(),
            P(),
            P(),
            P(),
            P(None, "wide", "narrow"),
            P(None, "wide", "narrow"),
            P(None, "wide", "narrow"),
            P("narrow", "wide"),
            P("narrow", "wide"),
            P("narrow", "wide"),
            P(None, ("wide", "narrow")),
            P(None, ("wide", "narrow")),
            P(None, ("wide", "narrow")),
            P(("wide", "narrow")),
            P(("wide", "narrow")),
            P(("wide", "narrow")),
            P(("wide", "narrow"), None),
            P(("wide", "narrow"), None),
            P(("wide", "narrow"), None),
        ),
        check_vma=False,
    )
```

```python
import math

import jax
import jax.numpy as jnp
from jax import lax
from jax.experimental import pallas as pl
from jax.experimental.pallas import tpu as pltpu
from jax.sharding import PartitionSpec as P

D = 768
HD = 64
FF = 3072
STEP = 5


norm_eps = 1e-06
masked_score = -1e30


def in_blocks(value, dim, size):
    shape = value.shape
    tiles = value.reshape(*shape[:dim], size, shape[dim] // size, *shape[dim + 1 :])
    return jnp.moveaxis(tiles, dim, 0)


def sent_and_summed(value, axis, dim):
    tiles = in_blocks(value, dim, lax.axis_size(axis))
    arrived = lax.all_to_all(tiles, axis, split_axis=0, concat_axis=0, tiled=True)
    return arrived.astype(jnp.float32).sum(axis=0)


def norm_rows(values, gain, shift):
    center = jnp.mean(values, axis=-1, keepdims=True)
    spread = values - center
    variance = jnp.mean(spread * spread, axis=-1, keepdims=True)
    return spread * lax.rsqrt(variance + norm_eps) * gain + shift


def gelu_exact(values):
    return jax.nn.gelu(values, approximate=False)


def times_transposed(left_mat, right_mat):
    return lax.dot_general(
        left_mat, right_mat, (((1,), (1,)), ((), ())), preferred_element_type=jnp.float32
    )


def transposed_times(left_mat, right_mat):
    return lax.dot_general(
        left_mat, right_mat, (((0,), (0,)), ((), ())), preferred_element_type=jnp.float32
    )


def adam_update(weight_in, moment_one, moment_two, gradient, step_rate):
    moment_one = 0.5 * moment_one + 0.5 * gradient
    moment_two = 0.5 * moment_two + 0.5 * gradient * gradient
    correction = 1.0 - 0.5**STEP
    direction = moment_one / correction / (jnp.sqrt(moment_two / correction) + 1e-08)
    return (weight_in - step_rate * (direction + 0.01 * weight_in), moment_one, moment_two)


def step_rates():
    return (0.5, 0.4, 0.4, D ** (-0.5), 4.0 * D ** (-0.5), D ** (-0.5), 0.4, FF ** (-0.5))


def group_rows(values):
    return lax.all_gather(values, "narrow", axis=0, tiled=True)


def group_sums(term_fn, local_rows):
    return lax.psum_scatter(
        term_fn(jnp.int32(0), lax.axis_size("narrow") * local_rows).astype(jnp.bfloat16),
        "narrow",
        scatter_dimension=0,
        tiled=True,
    ).astype(jnp.float32)


def masked_scores(queries, key_rows, segment):
    raw_scores = jnp.einsum(
        "qhd,khd->hqk", queries, key_rows, preferred_element_type=jnp.float32
    ) * HD ** (-0.5)
    same_doc = segment[:, None] == segment[None, :]
    return jnp.where(same_doc[None, :, :], raw_scores, masked_score)


def pack_forward(pack_item):
    queries, key_rows, values, segment = pack_item
    scores = masked_scores(queries, key_rows, segment)
    highest = jnp.max(scores, axis=-1, keepdims=True)
    exponentials = jnp.exp(scores - highest)
    totals = jnp.sum(exponentials, axis=-1, keepdims=True)
    weights = exponentials / totals
    attended = jnp.einsum(
        "hqk,khd->qhd", weights.astype(jnp.bfloat16), values, preferred_element_type=jnp.float32
    )
    return (attended.astype(jnp.bfloat16), (highest + jnp.log(totals))[:, :, 0])


def pack_backward(pack_item):
    queries, key_rows, values, segment, log_totals, grad_attended = pack_item
    scores = masked_scores(queries, key_rows, segment)
    weights = jnp.exp(scores - log_totals[:, :, None])
    grad_values = jnp.einsum(
        "hqk,qhd->khd",
        weights.astype(jnp.bfloat16),
        grad_attended,
        preferred_element_type=jnp.float32,
    )
    grad_weights = jnp.einsum(
        "qhd,khd->hqk", grad_attended, values, preferred_element_type=jnp.float32
    )
    center = jnp.sum(weights * grad_weights, axis=-1, keepdims=True)
    grad_scores = (weights * (grad_weights - center)).astype(jnp.bfloat16)
    grad_queries = jnp.einsum(
        "hqk,khd->qhd", grad_scores, key_rows, preferred_element_type=jnp.float32
    ) * HD ** (-0.5)
    grad_keys = jnp.einsum(
        "hqk,qhd->khd", grad_scores, queries, preferred_element_type=jnp.float32
    ) * HD ** (-0.5)
    return (
        grad_queries.astype(jnp.bfloat16),
        grad_keys.astype(jnp.bfloat16),
        grad_values.astype(jnp.bfloat16),
    )


def shards(
    tokens,
    type_ids,
    segment_ids,
    cotangent,
    type_table,
    type_first,
    type_second,
    norm_gains,
    gains_first,
    gains_second,
    biases,
    biases_first,
    biases_second,
    qkv_weight,
    qkv_first,
    qkv_second,
    out_weight,
    out_first,
    out_second,
    up_weight,
    up_first,
    up_second,
    up_bias,
    up_bias_first,
    up_bias_second,
    down_weight,
    down_first,
    down_second,
):
    local_rows = tokens.shape[0]
    model_width = tokens.shape[1]
    head_cols = qkv_weight.shape[2]
    heads_here = head_cols // HD
    pack_count = segment_ids.shape[0]
    pack_rows = segment_ids.shape[1]
    group_count = pack_count * pack_rows
    narrow_index = lax.axis_index("narrow")
    qkv_low = qkv_weight.astype(jnp.bfloat16)
    out_low = out_weight.astype(jnp.bfloat16)
    up_low = up_weight.astype(jnp.bfloat16)
    up_bias_low = up_bias.astype(jnp.bfloat16)
    down_low = down_weight.astype(jnp.bfloat16)
    qkv_full, out_rows = (
        lax.all_gather(qkv_low, "wide", axis=1, tiled=True),
        lax.all_gather(out_low, "wide", axis=1, tiled=True),
    )
    up_cols, up_bias_cols, down_rows = (
        lax.all_gather(up_low, ("wide", "narrow"), axis=1, tiled=True),
        lax.all_gather(up_bias_low, ("wide", "narrow"), axis=0, tiled=True),
        lax.all_gather(down_low, ("wide", "narrow"), axis=0, tiled=True),
    )
    is_image = (type_ids == 1)[:, None]
    embedded = tokens.astype(jnp.float32) + jnp.where(
        is_image, type_table[1][None, :], type_table[0][None, :]
    )
    normed1_full, norm1_pull = jax.vjp(norm_rows, embedded, norm_gains[0], biases[0])
    normed1 = normed1_full.astype(jnp.bfloat16)
    group_normed = group_rows(normed1)
    head_offset = narrow_index * head_cols
    bias_query = lax.dynamic_slice_in_dim(biases[1], head_offset, head_cols)
    bias_value = lax.dynamic_slice_in_dim(biases[2], head_offset, head_cols)
    bias_stack = jnp.stack([bias_query, jnp.zeros_like(bias_query), bias_value])
    projected = jnp.einsum(
        "rd,sde->sre", group_normed, qkv_full, preferred_element_type=jnp.float32
    )
    qkv_rows = (projected + bias_stack[:, None, :]).astype(jnp.bfloat16)
    qkv_packs = qkv_rows.reshape(3, pack_count, pack_rows, heads_here, HD)
    attended, log_totals = lax.map(
        pack_forward, (qkv_packs[0], qkv_packs[1], qkv_packs[2], segment_ids)
    )
    attended = attended.reshape(group_count, head_cols)

    def out_term(first_row, row_span):
        return jnp.dot(attended, out_rows, preferred_element_type=jnp.float32)

    attn_proj = group_sums(out_term, local_rows)
    hidden1 = embedded + attn_proj + biases[3]
    normed2_full, norm2_pull = jax.vjp(norm_rows, hidden1, norm_gains[1], biases[4])
    normed2 = normed2_full.astype(jnp.bfloat16)
    mlp_input, mlp_back = (normed2, cotangent)
    pre_act = jnp.dot(mlp_input, up_cols, preferred_element_type=jnp.float32) + up_bias_cols.astype(
        jnp.float32
    )
    activated, gelu_pull = jax.vjp(gelu_exact, pre_act)
    act_low = activated.astype(jnp.bfloat16)
    mlp_out = jnp.dot(act_low, down_rows, preferred_element_type=jnp.float32)
    activations = (hidden1 + mlp_out + biases[5]).astype(jnp.bfloat16)
    grad_act = times_transposed(mlp_back, down_rows)
    (grad_pre,) = gelu_pull(grad_act)
    grad_pre_low = grad_pre.astype(jnp.bfloat16)
    grad_down = transposed_times(act_low, mlp_back)
    grad_up = transposed_times(mlp_input, grad_pre_low)
    grad_up_bias = jnp.sum(grad_pre_low.astype(jnp.float32), axis=0)
    grad_normed2 = times_transposed(grad_pre_low, up_cols)
    grad_hidden_part, grad_gain2, grad_shift2 = norm2_pull(grad_normed2)
    cotangent_full = cotangent.astype(jnp.float32)
    grad_hidden = cotangent_full + grad_hidden_part
    grad_hidden_low = grad_hidden.astype(jnp.bfloat16)
    group_back = group_rows(grad_hidden_low)
    grad_attended = times_transposed(group_back, out_rows).astype(jnp.bfloat16)
    grad_out_weight = transposed_times(attended, group_back)
    back_packs = grad_attended.reshape(pack_count, pack_rows, heads_here, HD)
    grad_queries, grad_keys, grad_values = lax.map(
        pack_backward,
        (qkv_packs[0], qkv_packs[1], qkv_packs[2], segment_ids, log_totals, back_packs),
    )
    grad_qkv_rows = jnp.stack([grad_queries, grad_keys, grad_values]).reshape(
        3, group_count, head_cols
    )
    grad_qkv_weight = jnp.einsum(
        "rd,sre->sde", group_normed, grad_qkv_rows, preferred_element_type=jnp.float32
    )
    head_sums = jnp.sum(grad_qkv_rows.astype(jnp.float32), axis=1)

    def in_term(first_row, row_span):
        return jnp.einsum(
            "sre,sde->rd", grad_qkv_rows, qkv_full, preferred_element_type=jnp.float32
        )

    grad_normed1 = group_sums(in_term, local_rows)
    grad_embed_part, grad_gain1, grad_shift1 = norm1_pull(grad_normed1)
    input_grad = grad_hidden + grad_embed_part
    zero_row = jnp.zeros((model_width,), jnp.float32)
    query_sums = lax.dynamic_update_slice_in_dim(zero_row, head_sums[0], head_offset, 0)
    value_sums = lax.dynamic_update_slice_in_dim(zero_row, head_sums[2], head_offset, 0)
    gain_part = jnp.stack([grad_gain1, grad_gain2])
    shift_part = jnp.stack(
        [
            grad_shift1,
            query_sums,
            value_sums,
            jnp.sum(grad_hidden, axis=0),
            grad_shift2,
            jnp.sum(cotangent_full, axis=0),
        ]
    )
    type_part = jnp.stack(
        [
            jnp.sum(jnp.where(is_image, 0.0, input_grad), axis=0),
            jnp.sum(jnp.where(is_image, input_grad, 0.0), axis=0),
        ]
    )
    grad_gains, grad_biases, grad_types = lax.psum(
        (gain_part, shift_part, type_part), ("wide", "narrow")
    )
    owned_qkv, owned_out = (
        sent_and_summed(grad_qkv_weight.astype(jnp.bfloat16), "wide", 1),
        sent_and_summed(grad_out_weight.astype(jnp.bfloat16), "wide", 1),
    )
    owned_up, owned_up_bias, owned_down = (
        lax.psum_scatter(grad_up, ("wide", "narrow"), scatter_dimension=1, tiled=True),
        lax.psum_scatter(grad_up_bias, ("wide", "narrow"), scatter_dimension=0, tiled=True),
        lax.psum_scatter(grad_down, ("wide", "narrow"), scatter_dimension=0, tiled=True),
    )
    step_sizes = step_rates()
    new_type = adam_update(type_table, type_first, type_second, grad_types, step_sizes[0])
    new_gains = adam_update(norm_gains, gains_first, gains_second, grad_gains, step_sizes[1])
    new_biases = adam_update(biases, biases_first, biases_second, grad_biases, step_sizes[2])
    new_qkv = adam_update(qkv_weight, qkv_first, qkv_second, owned_qkv, step_sizes[3])
    new_out = adam_update(out_weight, out_first, out_second, owned_out, step_sizes[4])
    new_up = adam_update(up_weight, up_first, up_second, owned_up, step_sizes[5])
    new_up_bias = adam_update(up_bias, up_bias_first, up_bias_second, owned_up_bias, step_sizes[6])
    new_down = adam_update(down_weight, down_first, down_second, owned_down, step_sizes[7])
    return (
        activations,
        input_grad,
        new_type[0],
        new_type[1],
        new_type[2],
        new_gains[0],
        new_gains[1],
        new_gains[2],
        new_biases[0],
        new_biases[1],
        new_biases[2],
        new_qkv[0],
        new_qkv[1],
        new_qkv[2],
        new_out[0],
        new_out[1],
        new_out[2],
        new_up[0],
        new_up[1],
        new_up[2],
        new_up_bias[0],
        new_up_bias[1],
        new_up_bias[2],
        new_down[0],
        new_down[1],
        new_down[2],
    )


def dot_nn(left_mat, right_mat):
    return lax.dot_general(
        left_mat, right_mat, (((1,), (0,)), ((), ())), preferred_element_type=jnp.float32
    )


def dot_nt(left_mat, right_mat):
    return lax.dot_general(
        left_mat, right_mat, (((1,), (1,)), ((), ())), preferred_element_type=jnp.float32
    )


def dot_tn(left_mat, right_mat):
    return lax.dot_general(
        left_mat, right_mat, (((0,), (0,)), ((), ())), preferred_element_type=jnp.float32
    )


def rows_at(block, size):
    return pl.ds(pl.multiple_of(block * size, size), size)


def row_stats(values):
    center = jnp.mean(values, axis=-1, keepdims=True)
    spread = values - center
    variance = jnp.mean(spread * spread, axis=-1, keepdims=True)
    scale = lax.rsqrt(variance + norm_eps)
    return spread * scale, scale


def column_sums(values):
    return jnp.sum(values, axis=0, keepdims=True)


ROW = 128
OWN = 384
CHIP = 768
HALF_PACK = 256
PACK = 512
BLK = 96
ATTN, UP, DOWN = 0, 1, 2
Z_FIRST = (96, 64, 64)
Z_LAST = 32
LAST_AT = 512
GATHER_BY_Y = (32, 32, 32)
SCATTER_BY_Y = (48, 16, 16)
GAIN_ROW, BIAS_ROW, TYPE_ROW, UP_BIAS_ROW, SMALL_ROWS = 0, 2, 8, 10, 16


def layer_kernel(
    qkv_weight, out_weight, up_rows, down_rows, up_bias, tokens, type_ids, cotangent, segment_ids, type_table,
    gains, biases,
    act_out, input_grad, qkv_grad, out_grad, up_out, down_out, small_out,
    full, part, g_all, n1_all, n2_all, dh_all, qkv, att, dkv_far, probs, mask, act, slope, datt,
    key_acc, value_acc, embedded, hidden1, own_sum, attn_out, swap_send, swap_recv, type_cols, qkv_bias,
    bias_slots, bias_row, small, small_recv, rx, ry, rdx, rdy, rz, rl,
    gz_s, gz_r, gx_s, gx_r, gy_s, gy_r, gfx_s, gfx_r, gfy_s, gfy_r,
    sz_s, sz_r, sx_s, sx_r, sy_s, sy_r, sdx_s, sdx_r, sdy_s, sdy_r,
    gl_s, gl_r, sl_s, sl_r, glz_s, glz_r, slz_s, slz_r,
    spread_s, spread_r, swap_s, swap_r, far_s, far_r, bias_s, bias_r, small_s, small_r,
):
    f32, bf16 = jnp.float32, jnp.bfloat16
    wide = lax.axis_index("wide")
    narrow = lax.axis_index("narrow")
    z, x = wide // 2, wide % 2
    y, core = narrow // 2, narrow % 2
    z_of = [z, z + 1 - 2 * (z % 2), (z + 2) % 4, 3 - z]
    sibling = (wide, y * 2 + (1 - core))
    x_side = (z * 2 + (1 - x), narrow)
    y_side = (wide, (1 - y) * 2 + core)
    z_side = [None] + [(z_of[j] * 2 + x, narrow) for j in (1, 2, 3)]

    def copy(src, dst, send, recv, to):
        return pltpu.make_async_remote_copy(
            src_ref=src, dst_ref=dst, send_sem=send, recv_sem=recv, device_id=to,
            device_id_type=pl.DeviceIdType.MESH,
        )

    pending = []
    pending_if = []
    totals = (attn_out, up_out, down_out)

    def start(*args):
        one = copy(*args)
        one.start()
        pending.append(one)
        return one

    barrier = pltpu.get_barrier_semaphore()
    for to in (sibling, x_side, y_side, z_side[1], z_side[2], z_side[3]):
        pl.semaphore_signal(barrier, inc=1, device_id=to, device_id_type=pl.DeviceIdType.MESH)
    pl.semaphore_wait(barrier, 6)

    inner = z * (3 - z) == 2
    outer = z * (3 - z) == 0

    def start_if(which, *args):
        one = copy(*args)

        @pl.when(which)
        def _():
            one.start()

        pending_if.append((which, one))

    def slot(ref, kind, yy, zz, xx, first=0, size=None):
        rows = Z_FIRST[kind]
        row = pl.multiple_of((zz * 2 + xx) * rows + first, 16)
        return ref.at[kind, yy, pl.ds(row, rows if size is None else size)]

    def last(ref, kind, yy, zz, xx, first=0, size=Z_LAST):
        row = pl.multiple_of(LAST_AT + (zz * 2 + xx) * Z_LAST + first, 16)
        return ref.at[kind, yy, pl.ds(row, size)]

    def last_pair(ref, kind, yy, zz):
        return last(ref, kind, yy, zz, 0, 0, 2 * Z_LAST)

    def gather_z(kind):
        mine = slot(full, kind, y, z, x)
        for j in (1, 2):
            start(mine, mine, gz_s.at[kind, j], gz_r.at[kind, j], z_side[j])
        start_if(inner, mine, mine, gz_s.at[kind, 3], gz_r.at[kind, 3], z_side[3])

    def gather_on(kind, j):
        block = slot(full, kind, y, z_of[j], x)
        if j:
            copy(block, block, gz_s.at[kind, j], gz_r.at[kind, j], z_side[j]).wait_recv()
        if j == 2:
            start_if(inner, block, block, gz_s.at[kind, 0], gz_r.at[kind, 3], z_side[1])
        start(block, block, gx_s.at[kind, j], gx_r.at[kind, j], x_side)
        start(block, block, gy_s.at[kind, j], gy_r.at[kind, j], y_side)
        if kind != ATTN and j == 0:
            block = last(full, kind, y, z, x)
            start(block, block, gl_s.at[kind, 0], gl_r.at[kind, 0], x_side)
            start(block, block, gl_s.at[kind, 1], gl_r.at[kind, 1], y_side)

    def gather_far(kind, j):
        zz = z_of[j]
        by_y, by_x = GATHER_BY_Y[kind], Z_FIRST[kind] - GATHER_BY_Y[kind]
        block = slot(full, kind, y, zz, 1 - x)
        copy(block, block, gx_s.at[kind, j], gx_r.at[kind, j], x_side).wait_recv()
        half = slot(full, kind, y, zz, 1 - x, 0, by_y)
        start(half, half, gfy_s.at[kind, j], gfy_r.at[kind, j], y_side)
        block = slot(full, kind, 1 - y, zz, x)
        copy(block, block, gy_s.at[kind, j], gy_r.at[kind, j], y_side).wait_recv()
        half = slot(full, kind, 1 - y, zz, x, by_y, by_x)
        start(half, half, gfx_s.at[kind, j], gfx_r.at[kind, j], x_side)
        if kind != ATTN and j == 0:
            block = last(full, kind, y, z, 1 - x)
            copy(block, block, gl_s.at[kind, 0], gl_r.at[kind, 0], x_side).wait_recv()
            half = last(full, kind, y, z, 1 - x, 0, 16)
            start(half, half, gl_s.at[kind, 2], gl_r.at[kind, 2], y_side)
            block = last(full, kind, 1 - y, z, x)
            copy(block, block, gl_s.at[kind, 1], gl_r.at[kind, 1], y_side).wait_recv()
            half = last(full, kind, 1 - y, z, x, 16, 16)
            start(half, half, gl_s.at[kind, 3], gl_r.at[kind, 3], x_side)

    def gather_last(kind):
        half = last(full, kind, 1 - y, z, 1 - x, 0, 16)
        copy(half, half, gl_s.at[kind, 2], gl_r.at[kind, 2], y_side).wait_recv()
        half = last(full, kind, 1 - y, z, 1 - x, 16, 16)
        copy(half, half, gl_s.at[kind, 3], gl_r.at[kind, 3], x_side).wait_recv()
        for yy in (0, 1):
            pair = last_pair(full, kind, yy, z)
            for j in (1, 2):
                start(pair, pair, glz_s.at[kind, 2 * j + yy], glz_r.at[kind, 2 * j + yy], z_side[j])
            start_if(inner, pair, pair, glz_s.at[kind, 6 + yy], glz_r.at[kind, 6 + yy], z_side[3])

    def last_arrived(kind, j):
        for yy in (0, 1):
            pair = last_pair(full, kind, yy, z_of[j])
            copy(pair, pair, glz_s.at[kind, 2 * j + yy], glz_r.at[kind, 2 * j + yy], z_side[j]).wait_recv()

    def gather_relay(kind):
        last_arrived(kind, 2)
        for yy in (0, 1):
            pair = last_pair(full, kind, yy, z_of[2])
            start_if(inner, pair, pair, glz_s.at[kind, yy], glz_r.at[kind, 6 + yy], z_side[1])

    def gather_last_done(kind):
        last_arrived(kind, 1)
        last_arrived(kind, 3)

    def gather_done(kind):
        by_y, by_x = GATHER_BY_Y[kind], Z_FIRST[kind] - GATHER_BY_Y[kind]
        for j in range(4):
            half = slot(full, kind, 1 - y, z_of[j], 1 - x, 0, by_y)
            copy(half, half, gfy_s.at[kind, j], gfy_r.at[kind, j], y_side).wait_recv()
            half = slot(full, kind, 1 - y, z_of[j], 1 - x, by_y, by_x)
            copy(half, half, gfx_s.at[kind, j], gfx_r.at[kind, j], x_side).wait_recv()

    def add_in(ref, arrived):
        ref[...] = (ref[...].astype(f32) + arrived[...].astype(f32)).astype(bf16)

    def scatter_last(kind):
        for yy in (0, 1):
            def target(j):
                return last_pair(part, kind, yy, z_of[j])

            def landing(j):
                return rl.at[kind - 1, j, yy]

            def sems(sent, landed):
                return slz_s.at[kind, 2 * sent + yy], slz_r.at[kind, 2 * landed + yy]

            start(target(1), landing(1), *sems(1, 1), z_side[1])
            start_if(outer, target(2), landing(2), *sems(2, 2), z_side[2])
            start_if(inner, target(3), landing(3), *sems(3, 3), z_side[3])
            start_if(outer, target(3), landing(0), *sems(3, 0), z_side[1])

    def scatter_relay(kind):
        @pl.when(inner)
        def _():
            for yy in (0, 1):
                here = last_pair(part, kind, yy, z_of[2])
                came = rl.at[kind - 1, 0, yy]
                copy(here, came, slz_s.at[kind, yy], slz_r.at[kind, yy], z_side[1]).wait_recv()
                add_in(here, came)

        for yy in (0, 1):
            here = last_pair(part, kind, yy, z_of[2])
            start_if(
                inner, here, rl.at[kind - 1, 2, yy], slz_s.at[kind, 4 + yy], slz_r.at[kind, 4 + yy], z_side[2]
            )

    def scatter_last_add(kind):
        for yy in (0, 1):
            here = last_pair(part, kind, yy, z)
            for j in (1, 2):
                came = rl.at[kind - 1, j, yy]
                copy(here, came, slz_s.at[kind, 2 * j + yy], slz_r.at[kind, 2 * j + yy], z_side[j]).wait_recv()
            total = here[...].astype(f32) + rl[kind - 1, 1, yy].astype(f32) + rl[kind - 1, 2, yy].astype(f32)
            here[...] = total.astype(bf16)

        @pl.when(inner)
        def _():
            for yy in (0, 1):
                here = last_pair(part, kind, yy, z)
                came = rl.at[kind - 1, 3, yy]
                copy(here, came, slz_s.at[kind, 6 + yy], slz_r.at[kind, 6 + yy], z_side[3]).wait_recv()
                add_in(here, came)

    def scatter_far(kind, j):
        by_y, by_x = SCATTER_BY_Y[kind], Z_FIRST[kind] - SCATTER_BY_Y[kind]
        half = slot(part, kind, 1 - y, z_of[j], 1 - x, 0, by_y)
        start(half, rdy.at[kind, j, pl.ds(0, by_y)], sdy_s.at[kind, j], sdy_r.at[kind, j], y_side)
        half = slot(part, kind, 1 - y, z_of[j], 1 - x, by_y, by_x)
        start(half, rdx.at[kind, j, pl.ds(0, by_x)], sdx_s.at[kind, j], sdx_r.at[kind, j], x_side)
        if kind != ATTN and j == 0:
            half = last(part, kind, 1 - y, z, 1 - x, 0, 16)
            start(half, rdy.at[kind, 0, pl.ds(48, 16)], sl_s.at[kind, 0], sl_r.at[kind, 0], y_side)
            half = last(part, kind, 1 - y, z, 1 - x, 16, 16)
            start(half, rdx.at[kind, 0, pl.ds(48, 16)], sl_s.at[kind, 1], sl_r.at[kind, 1], x_side)

    def scatter_near(kind, j):
        zz = z_of[j]
        rows = Z_FIRST[kind]
        by_y, by_x = SCATTER_BY_Y[kind], rows - SCATTER_BY_Y[kind]
        half = slot(part, kind, y, zz, 1 - x, 0, by_y)
        came = rdy.at[kind, j, pl.ds(0, by_y)]
        copy(half, came, sdy_s.at[kind, j], sdy_r.at[kind, j], y_side).wait_recv()
        add_in(half, came)
        land = pl.ds(0, rows)
        start(slot(part, kind, y, zz, 1 - x), rx.at[kind, j, land], sx_s.at[kind, j], sx_r.at[kind, j], x_side)
        half = slot(part, kind, 1 - y, zz, x, by_y, by_x)
        came = rdx.at[kind, j, pl.ds(0, by_x)]
        copy(half, came, sdx_s.at[kind, j], sdx_r.at[kind, j], x_side).wait_recv()
        add_in(half, came)
        start(slot(part, kind, 1 - y, zz, x), ry.at[kind, j, land], sy_s.at[kind, j], sy_r.at[kind, j], y_side)
        if kind != ATTN and j == 0:
            land = pl.ds(rows, Z_LAST)
            half = last(part, kind, y, z, 1 - x, 0, 16)
            came = rdy.at[kind, 0, pl.ds(48, 16)]
            copy(half, came, sl_s.at[kind, 0], sl_r.at[kind, 0], y_side).wait_recv()
            add_in(half, came)
            start(last(part, kind, y, z, 1 - x), rx.at[kind, 0, land], sl_s.at[kind, 2], sl_r.at[kind, 2], x_side)
            half = last(part, kind, 1 - y, z, x, 16, 16)
            came = rdx.at[kind, 0, pl.ds(48, 16)]
            copy(half, came, sl_s.at[kind, 1], sl_r.at[kind, 1], x_side).wait_recv()
            add_in(half, came)
            start(last(part, kind, 1 - y, z, x), ry.at[kind, 0, land], sl_s.at[kind, 3], sl_r.at[kind, 3], y_side)

    def scatter_z(kind, j):
        land = pl.ds(0, Z_FIRST[kind])
        block = slot(part, kind, y, z_of[j], x)
        copy(block, rx.at[kind, j, land], sx_s.at[kind, j], sx_r.at[kind, j], x_side).wait_recv()
        copy(block, ry.at[kind, j, land], sy_s.at[kind, j], sy_r.at[kind, j], y_side).wait_recv()
        total = block[...].astype(f32) + rx[kind, j, land].astype(f32) + ry[kind, j, land].astype(f32)
        if j == 0:
            totals[kind][land] = total
            if kind != ATTN:
                land = pl.ds(Z_FIRST[kind], Z_LAST)
                block = last(part, kind, y, z, x)
                copy(block, rx.at[kind, 0, land], sl_s.at[kind, 2], sl_r.at[kind, 2], x_side).wait_recv()
                copy(block, ry.at[kind, 0, land], sl_s.at[kind, 3], sl_r.at[kind, 3], y_side).wait_recv()
                totals[kind][land] = (
                    block[...].astype(f32) + rx[kind, 0, land].astype(f32) + ry[kind, 0, land].astype(f32)
                )
            return
        block[...] = total.astype(bf16)
        came = rz.at[kind, j, land]
        if j == 1:
            start(block, came, sz_s.at[kind, j], sz_r.at[kind, j], z_side[j])
        elif j == 2:
            relayed = rz.at[kind, 0, land]

            @pl.when(inner)
            def _():
                copy(block, relayed, sz_s.at[kind, 0], sz_r.at[kind, 0], z_side[1]).wait_recv()
                add_in(block, relayed)

            start(block, came, sz_s.at[kind, j], sz_r.at[kind, j], z_side[j])
        else:
            start_if(inner, block, came, sz_s.at[kind, 3], sz_r.at[kind, 3], z_side[3])
            start_if(outer, block, rz.at[kind, 0, land], sz_s.at[kind, 3], sz_r.at[kind, 0], z_side[1])

    def scatter_done(kind):
        land = pl.ds(0, Z_FIRST[kind])
        for j in (1, 2):
            came = rz.at[kind, j, land]
            copy(came, came, sz_s.at[kind, j], sz_r.at[kind, j], z_side[j]).wait_recv()
        totals[kind][land] += rz[kind, 1, land].astype(f32) + rz[kind, 2, land].astype(f32)

        @pl.when(inner)
        def _():
            came = rz.at[kind, 3, land]
            copy(came, came, sz_s.at[kind, 3], sz_r.at[kind, 3], z_side[3]).wait_recv()
            totals[kind][land] += came[...].astype(f32)

    def place(which, block):
        return rows_at((3 * which + block + 4 * y) % 6, ROW)

    def hand_over(ref, use, block):
        here = ref.at[place(core, block)]
        return copy(here, here, spread_s.at[use, block], spread_r.at[use, block], sibling)

    def spread_done(ref, use):
        for block in range(3):
            there = ref.at[place(1 - core, block)]
            copy(there, there, spread_s.at[use, block], spread_r.at[use, block], sibling).wait_recv()
            pending.append(hand_over(ref, use, block))

    def swap_sums(use, term):
        def for_sibling(block, carry):
            rows = rows_at(block, ROW)
            swap_send[rows] = term(place(1 - core, block)).astype(bf16)
            copy(
                swap_send.at[rows], swap_recv.at[use, rows], swap_s.at[use, block],
                swap_r.at[use, block], sibling,
            ).start()
            return carry

        def for_self(block, carry):
            own_sum[rows_at(block, ROW)] = term(place(core, block))
            return carry

        lax.fori_loop(0, 3, for_sibling, 0)
        lax.fori_loop(0, 3, for_self, 0)

    def swap_done(use):
        for block in range(3):
            rows = pl.ds(block * ROW, ROW)
            one = copy(
                swap_send.at[rows], swap_recv.at[use, rows], swap_s.at[use, block],
                swap_r.at[use, block], sibling,
            )
            one.wait_recv()
            one.wait_send()

    def swapped(use, rows):
        return own_sum[rows] + swap_recv[use, rows].astype(f32)

    def own_attn():
        slot(full, ATTN, y, z, x)[...] = jnp.concatenate(
            [qkv_weight[1], qkv_weight[2], qkv_weight[0], out_weight[...].T], axis=1
        ).astype(bf16)

    def own_rest():
        for kind, rows in ((UP, up_rows), (DOWN, down_rows)):
            slot(full, kind, y, z, x)[...] = rows[0:64].astype(bf16)
            last(full, kind, y, z, x)[...] = rows[64:96].astype(bf16)

    def as_column(row):
        return jnp.broadcast_to(row, (ROW, ROW)).T

    def column_types():
        types = type_ids[...].astype(f32)
        for block in range(3):
            rows = pl.ds(block * ROW, ROW)
            type_cols[rows] = as_column(types[:, block * ROW : block * ROW + ROW])

    def give_cotangent():
        def body(block, carry):
            g_all[place(core, block)] = cotangent[rows_at(block, ROW)]
            hand_over(g_all, 0, block).start()
            return carry

        lax.fori_loop(0, 3, body, 0)

    def first_norm():
        def body(block, carry):
            rows = rows_at(block, ROW)
            values = tokens[rows].astype(f32) + jnp.where(
                type_cols[rows, 0:1] > 0, type_table[1:2, :], type_table[0:1, :]
            )
            embedded[rows] = values
            xhat, _ = row_stats(values)
            n1_all[place(core, block)] = (xhat * gains[0:1, :] + biases[0:1, :]).astype(bf16)
            hand_over(n1_all, 1, block).start()
            return carry

        lax.fori_loop(0, 3, body, 0)

    half_rows = pl.ds(PACK, HALF_PACK)
    far_rows = pl.ds(CHIP, HALF_PACK)
    over_y = copy(n1_all.at[half_rows], n1_all.at[far_rows], far_s.at[0], far_r.at[0], y_side)
    relay = copy(n1_all.at[far_rows], n1_all.at[far_rows], far_s.at[1], far_r.at[1], sibling)
    holds_half = (core + y) == 1

    def half_over():
        @pl.when(holds_half)
        def _():
            over_y.start()

    def half_relay():
        @pl.when(jnp.logical_not(holds_half))
        def _():
            over_y.wait_recv()
            relay.start()

    def half_arrived():
        @pl.when(holds_half)
        def _():
            relay.wait_recv()

    bias_first = (y * 2 + x) * 4

    def bias_hop(first, size, index, to):
        ref = bias_slots.at[pl.ds(first, size)]
        return start(ref, ref, bias_s.at[index], bias_r.at[index], to)

    def bias_wait(first, size, index, to):
        ref = bias_slots.at[pl.ds(first, size)]
        copy(ref, ref, bias_s.at[index], bias_r.at[index], to).wait_recv()

    def bias_along_z():
        bias_slots[bias_first + z] = jnp.broadcast_to(
            jnp.concatenate(
                [up_bias[...].astype(bf16).astype(f32), jnp.zeros((1, 128 - BLK), f32)], axis=1
            ),
            (8, 128),
        )
        for j in (1, 2, 3):
            bias_hop(bias_first + z, 1, j, z_side[j])

    def bias_along_x():
        for j in (1, 2, 3):
            bias_wait(bias_first + z_of[j], 1, j, z_side[j])
        bias_hop(bias_first, 4, 4, x_side)

    def bias_along_y():
        bias_wait((y * 2 + 1 - x) * 4, 4, 4, x_side)
        bias_hop(y * 8, 8, 5, y_side)

    def bias_as_rows():
        bias_wait((1 - y) * 8, 8, 5, y_side)
        for yy in (0, 1):
            for xx in (0, 1):
                for zz in range(4):
                    which, block = zz * 2 + xx, (yy * 2 + xx) * 4 + zz
                    bias_row[yy, :, which * 64 : which * 64 + 64] = bias_slots[block, :, 0:64]
                    first = LAST_AT + which * Z_LAST
                    bias_row[yy, :, first : first + Z_LAST] = bias_slots[block, :, 64:96]

    def masks():
        documents = segment_ids[...].astype(f32)
        early = y == 0
        whole_doc = jnp.where(early, documents[0:1], documents[2:3])
        near_doc = jnp.where(early, documents[1:2, 0:256], documents[1:2, 256:512])
        far_doc = jnp.where(early, documents[1:2, 256:512], documents[1:2, 0:256])
        query_rows = (whole_doc[:, 0:256], whole_doc[:, 256:512], near_doc)
        key_rows_of = (whole_doc, jnp.concatenate([near_doc, far_doc], axis=1))
        for side, tiles in ((0, (0, 1)), (1, (2,))):
            for chunk in range(4):
                keys = slice(chunk * ROW, chunk * ROW + ROW)
                column = as_column(key_rows_of[side][:, keys])[:, 0:1]
                for tile in tiles:
                    mask[tile, keys] = jnp.where(
                        column == query_rows[tile], 0.0, masked_score
                    ).astype(bf16)

    def zeros_and_biases():
        small[...] = jnp.zeros_like(small)
        for yy in (0, 1):
            att[yy, :, 0:HD] = jnp.zeros((CHIP, HD), bf16)
            qkv[yy, :, 576:768] = jnp.zeros((CHIP + HALF_PACK, 192), bf16)
            first = yy * 384
            chosen = [
                jnp.where(
                    core == 0,
                    biases[i : i + 1, first : first + 192],
                    biases[i : i + 1, first + 192 : first + 384],
                )
                for i in (2, 1)
            ]
            zeros = jnp.zeros((1, 192), f32)
            qkv_bias[yy] = jnp.concatenate([zeros] + chosen + [zeros[:, 0:64]], axis=1)

    lane = lax.broadcasted_iota(jnp.int32, (1, 640), 1)
    shrink = jnp.where(lane >= 384, HD ** (-0.5), 1.0).astype(f32)

    def project(yy):
        def body(tile, carry):
            rows = rows_at(tile, 256)
            found = dot_nn(n1_all[rows], full[ATTN, yy, :, 0:640]) + qkv_bias[yy]
            qkv[yy, rows, 0:576] = (found * shrink)[:, 0:576].astype(bf16)
            return carry

        lax.fori_loop(0, 4, body, 0)

    def head_rows(yy, head, rows, keys):
        queries = qkv[yy, rows, 384 + HD * head : 448 + HD * head]
        key_rows = qkv[yy, keys, HD * head : HD * head + HD]
        values = qkv[yy, keys, 192 + HD * head : 256 + HD * head]
        return queries, key_rows, values

    def attend(yy, head):
        def body(tile, carry):
            rows = rows_at(tile, 256)
            queries, key_rows, values = head_rows(yy, head, rows, rows_at(tile // 2, PACK))
            scores = dot_nt(key_rows, queries) + mask[tile].astype(f32)
            exponentials = jnp.exp(scores - jnp.max(scores, axis=0, keepdims=True))
            totals = jnp.sum(exponentials, axis=0, keepdims=True)
            weights = (exponentials * (1.0 / totals)).astype(bf16)
            probs[yy * 3 + head, tile] = weights
            att[yy, rows, HD + HD * head : 2 * HD + HD * head] = dot_tn(values, weights).T.astype(bf16)
            return carry

        lax.fori_loop(0, 3, body, 0)

    def out_term(rows):
        return dot_nt(att[0, rows], full[ATTN, 0, :, 512:768]) + dot_nt(
            att[1, rows], full[ATTN, 1, :, 512:768]
        )

    def second_norm():
        def body(block, carry):
            rows = rows_at(block, ROW)
            values = embedded[rows] + swapped(0, rows) + biases[3:4, :]
            hidden1[rows] = values
            xhat, _ = row_stats(values)
            n2_all[place(core, block)] = (xhat * gains[1:2, :] + biases[4:5, :]).astype(bf16)
            hand_over(n2_all, 2, block).start()
            return carry

        lax.fori_loop(0, 3, body, 0)

    def up_chunk(yy, chunk):
        lanes = slice(chunk * 256, chunk * 256 + 256)
        shift = bias_row[yy, 0:1, lanes]

        def body(tile, carry):
            rows = rows_at(tile, 256)
            before = dot_nt(n2_all[rows], full[UP, yy, lanes]) + shift
            normal = 0.5 + 0.5 * lax.erf(before * (0.5**0.5))
            act[yy, rows, lanes] = (before * normal).astype(bf16)
            bell = jnp.exp(-0.5 * before * before) * ((2.0 * math.pi) ** -0.5)
            slope[yy, rows, lanes] = (normal + before * bell).astype(bf16)
            return carry

        lax.fori_loop(0, 3, body, 0)

    def down_grad(yy):
        for chunk in range(3):
            lanes = slice(chunk * 256, chunk * 256 + 256)
            part[DOWN, yy, lanes] = dot_tn(act[yy, :, lanes], g_all[...]).astype(bf16)

    def du_chunk(yy, chunk):
        lanes = slice(chunk * 256, chunk * 256 + 256)

        def body(tile, carry):
            rows = rows_at(tile, 256)
            grad = dot_nt(g_all[rows], full[DOWN, yy, lanes]) * slope[yy, rows, lanes].astype(f32)
            grad = grad.astype(bf16)
            slope[yy, rows, lanes] = grad
            return carry + column_sums(grad.astype(f32))

        total = lax.fori_loop(0, 3, body, jnp.zeros((1, 256), f32))
        for cc in (0, 1):
            for side in (0, 1):
                row = UP_BIAS_ROW + 2 * cc + side
                small[row : row + 1, lanes] = jnp.where(
                    jnp.logical_and(core == cc, yy == side), total, small[row : row + 1, lanes]
                )

    def mlp_term(rows):
        return dot_nn(act[0, rows], full[DOWN, 0]) + dot_nn(act[1, rows], full[DOWN, 1])

    def du_term(rows):
        return dot_nn(slope[0, rows], full[UP, 0]) + dot_nn(slope[1, rows], full[UP, 1])

    def up_grad(yy):
        for chunk in range(3):
            lanes = slice(chunk * 256, chunk * 256 + 256)
            part[UP, yy, lanes] = dot_tn(slope[yy, :, lanes], n2_all[...]).astype(bf16)

    def second_norm_back():
        def body(block, carry):
            rows = rows_at(block, ROW)
            grad = swapped(2, rows)
            xhat, scale = row_stats(hidden1[rows])
            scaled = grad * gains[1:2, :]
            back = (
                scaled
                - jnp.mean(scaled, axis=-1, keepdims=True)
                - xhat * jnp.mean(scaled * xhat, axis=-1, keepdims=True)
            ) * scale
            given = cotangent[rows].astype(f32)
            total = given + back
            input_grad[rows] = total
            dh_all[place(core, block)] = total.astype(bf16)
            hand_over(dh_all, 3, block).start()
            small[1:2, :] += column_sums(grad * xhat)
            small[6:7, :] += column_sums(grad)
            small[5:6, :] += column_sums(total)
            small[7:8, :] += column_sums(given)
            return carry

        lax.fori_loop(0, 3, body, 0)

    def project_back(yy):
        def body(tile, carry):
            rows = rows_at(tile, 256)
            datt[yy, rows] = dot_nn(dh_all[rows], full[ATTN, yy, :, 512:768]).astype(bf16)
            return carry

        lax.fori_loop(0, 3, body, 0)

    def attend_back(yy, head):
        key_acc[...] = jnp.zeros_like(key_acc)
        value_acc[...] = jnp.zeros_like(value_acc)

        def body(tile, carry):
            rows = rows_at(tile, 256)
            keys = rows_at(tile // 2, PACK)
            queries, key_rows, values = head_rows(yy, head, rows, keys)
            grad = datt[yy, rows, HD + HD * head : 2 * HD + HD * head]
            weights = probs[yy * 3 + head, tile]
            weights_full = weights.astype(f32)
            back = dot_nt(values, grad) * weights_full
            center = jnp.sum(back, axis=0, keepdims=True)
            grad_scores = (back - weights_full * center).astype(bf16)
            grad_queries = dot_tn(key_rows, grad_scores) * HD ** (-0.5)
            value_acc[keys] += dot_nn(weights, grad)
            key_acc[keys] += dot_nn(grad_scores, queries)
            qkv[yy, rows, 384 + HD * head : 448 + HD * head] = grad_queries.T.astype(bf16)
            return carry

        lax.fori_loop(0, 3, body, 0)
        qkv[yy, :, HD * head : HD * head + HD] = key_acc[...].astype(bf16)
        qkv[yy, :, 192 + HD * head : 256 + HD * head] = value_acc[...].astype(bf16)

    def send_far(yy):
        start(qkv.at[yy, far_rows, 0:384], dkv_far.at[yy], far_s.at[2 + yy], far_r.at[2 + yy], y_side)

    def add_far(yy):
        copy(
            qkv.at[yy, far_rows, 0:384], dkv_far.at[yy], far_s.at[2 + yy], far_r.at[2 + yy], y_side
        ).wait_recv()
        qkv[yy, half_rows, 0:384] = (
            qkv[yy, half_rows, 0:384].astype(f32) + dkv_far[yy].astype(f32)
        ).astype(bf16)

    def finish_act():
        def body(block, carry):
            rows = rows_at(block, ROW)
            act_out[rows] = (hidden1[rows] + swapped(1, rows) + biases[5:6, :]).astype(bf16)
            return carry

        lax.fori_loop(0, 3, body, 0)

    def attn_grad(yy):
        for chunk in range(3):
            lanes = slice(chunk * 256, chunk * 256 + 256)
            n1_part = n1_all[0:CHIP, lanes]
            part[ATTN, yy, lanes, 0:512] = dot_tn(n1_part, qkv[yy, 0:CHIP, 0:512]).astype(bf16)
            part[ATTN, yy, lanes, 512:768] = (
                dot_tn(n1_part, qkv[yy, 0:CHIP, 512:768]) + dot_tn(dh_all[:, lanes], att[yy])
            ).astype(bf16)

    def in_term(rows):
        return dot_nt(qkv[0, rows], full[ATTN, 0]) + dot_nt(qkv[1, rows], full[ATTN, 1])

    def head_bias_sums():
        for yy in (0, 1):
            sums = column_sums(qkv[yy, 0:CHIP, 192:576].astype(f32))
            for cc in (0, 1):
                first = yy * 384 + cc * 192
                small[4:5, first : first + 192] = jnp.where(core == cc, sums[:, 0:192], 0.0)
                small[3:4, first : first + 192] = jnp.where(core == cc, sums[:, 192:384], 0.0)

    def first_norm_back():
        def body(block, carry):
            rows = rows_at(block, ROW)
            grad = swapped(3, rows)
            xhat, scale = row_stats(embedded[rows])
            scaled = grad * gains[0:1, :]
            back = (
                scaled
                - jnp.mean(scaled, axis=-1, keepdims=True)
                - xhat * jnp.mean(scaled * xhat, axis=-1, keepdims=True)
            ) * scale
            total = input_grad[rows] + back
            input_grad[rows] = total
            small[0:1, :] += column_sums(grad * xhat)
            small[2:3, :] += column_sums(grad)
            image = type_cols[rows, 0:1] > 0
            small[8:9, :] += column_sums(jnp.where(image, 0.0, total))
            small[9:10, :] += column_sums(jnp.where(image, total, 0.0))
            return carry

        lax.fori_loop(0, 3, body, 0)

    def small_core():
        start(small, small_recv.at[4], small_s.at[4], small_r.at[4], sibling)

    def small_x():
        copy(small, small_recv.at[4], small_s.at[4], small_r.at[4], sibling).wait_recv()
        small_recv[5] = small[...] + small_recv[4]
        start(small_recv.at[5], small_recv.at[6], small_s.at[5], small_r.at[5], x_side)

    def small_y():
        copy(small_recv.at[5], small_recv.at[6], small_s.at[5], small_r.at[5], x_side).wait_recv()
        small_recv[7] = small_recv[5] + small_recv[6]
        start(small_recv.at[7], small_recv.at[8], small_s.at[6], small_r.at[6], y_side)

    def small_z():
        copy(small_recv.at[7], small_recv.at[8], small_s.at[6], small_r.at[6], y_side).wait_recv()
        small_recv[z] = small_recv[7] + small_recv[8]
        for j in (1, 2, 3):
            start(small_recv.at[z], small_recv.at[z], small_s.at[j], small_r.at[j], z_side[j])

    def small_done():
        for j in (1, 2, 3):
            there = small_recv.at[z_of[j]]
            copy(there, there, small_s.at[j], small_r.at[j], z_side[j]).wait_recv()
        small_out[...] = (small_recv[0] + small_recv[1]) + (small_recv[2] + small_recv[3])

    def attn_out_rows():
        qkv_grad[0] = attn_out[:, 384:576]
        qkv_grad[1] = attn_out[:, 0:192]
        qkv_grad[2] = attn_out[:, 192:384]
        out_grad[...] = attn_out[:, 576:768].T

    own_attn()
    gather_on(ATTN, 0)
    gather_z(ATTN)
    own_rest()
    column_types()
    gather_on(UP, 0)
    gather_on(ATTN, 1)
    gather_far(UP, 0)
    bias_along_z()
    gather_on(ATTN, 2)
    first_norm()
    gather_z(UP)
    half_over()
    gather_last(UP)
    spread_done(n1_all, 1)
    gather_on(ATTN, 3)
    bias_along_x()
    masks()
    gather_far(ATTN, 1)
    gather_far(ATTN, 0)
    gather_far(ATTN, 2)
    half_relay()
    gather_far(ATTN, 3)
    zeros_and_biases()
    gather_on(DOWN, 0)
    half_arrived()
    give_cotangent()
    gather_on(UP, 1)
    project(y)
    gather_on(UP, 2)
    gather_z(DOWN)
    gather_done(ATTN)
    project(1 - y)
    gather_far(DOWN, 0)
    bias_along_y()
    attend(y, 0)
    gather_relay(UP)
    attend(y, 1)
    attend(y, 2)
    gather_on(DOWN, 2)
    gather_last(DOWN)
    gather_on(DOWN, 1)
    attend(1 - y, 0)
    attend(1 - y, 1)
    gather_last_done(UP)
    gather_on(UP, 3)
    gather_far(UP, 2)
    attend(1 - y, 2)
    gather_on(DOWN, 3)
    swap_sums(0, out_term)
    gather_far(UP, 1)
    gather_far(UP, 3)
    spread_done(g_all, 0)
    swap_done(0)
    second_norm()
    bias_as_rows()
    gather_done(UP)
    gather_far(DOWN, 2)
    spread_done(n2_all, 2)
    up_chunk(y, 0)
    gather_far(DOWN, 1)
    up_chunk(y, 1)
    gather_far(DOWN, 3)
    gather_relay(DOWN)
    up_chunk(y, 2)
    up_chunk(1 - y, 0)
    up_chunk(1 - y, 1)
    up_chunk(1 - y, 2)
    gather_last_done(DOWN)
    down_grad(1 - y)
    down_grad(y)
    scatter_last(DOWN)
    du_chunk(y, 0)
    du_chunk(y, 1)
    scatter_far(DOWN, 3)
    du_chunk(y, 2)
    gather_done(DOWN)
    du_chunk(1 - y, 0)
    du_chunk(1 - y, 1)
    scatter_far(DOWN, 2)
    du_chunk(1 - y, 2)
    swap_sums(2, du_term)
    up_grad(y)
    up_grad(1 - y)
    scatter_far(UP, 3)
    swap_done(2)
    second_norm_back()
    scatter_far(UP, 2)
    scatter_far(UP, 1)
    scatter_last(UP)
    scatter_near(DOWN, 2)
    scatter_near(DOWN, 3)
    spread_done(dh_all, 3)
    scatter_far(DOWN, 1)
    project_back(0)
    scatter_near(UP, 3)
    project_back(1)
    scatter_near(UP, 2)
    scatter_relay(DOWN)
    attend_back(0, 0)
    scatter_near(UP, 1)
    attend_back(0, 1)
    attend_back(0, 2)
    attend_back(1, 0)
    send_far(0)
    attend_back(1, 1)
    attend_back(1, 2)
    send_far(1)
    swap_sums(1, mlp_term)
    scatter_near(DOWN, 1)
    scatter_z(DOWN, 3)
    add_far(0)
    swap_done(1)
    scatter_z(UP, 3)
    add_far(1)
    attn_grad(1 - y)
    scatter_far(ATTN, 0)
    scatter_far(ATTN, 1)
    scatter_far(ATTN, 2)
    attn_grad(y)
    finish_act()
    scatter_far(ATTN, 3)
    swap_sums(3, in_term)
    scatter_z(DOWN, 2)
    swap_done(3)
    scatter_relay(UP)
    scatter_near(ATTN, 1)
    scatter_near(ATTN, 3)
    scatter_last_add(DOWN)
    scatter_z(UP, 2)
    scatter_z(DOWN, 1)
    scatter_z(ATTN, 1)
    scatter_near(ATTN, 0)
    head_bias_sums()
    first_norm_back()
    small_core()
    scatter_far(DOWN, 0)
    scatter_z(UP, 1)
    scatter_z(ATTN, 3)
    small_x()
    scatter_near(ATTN, 2)
    scatter_last_add(UP)
    scatter_z(ATTN, 0)
    small_y()
    scatter_far(UP, 0)
    scatter_near(DOWN, 0)
    small_z()
    scatter_z(ATTN, 2)
    small_done()
    scatter_near(UP, 0)
    scatter_z(DOWN, 0)
    scatter_done(ATTN)
    attn_out_rows()
    scatter_z(UP, 0)
    scatter_done(DOWN)
    scatter_done(UP)
    for one in pending:
        one.wait_send()
    for which, one in pending_if:
        @pl.when(which)
        def _(one=one):
            one.wait_send()

    @pl.when(holds_half)
    def _():
        over_y.wait_send()

    @pl.when(jnp.logical_not(holds_half))
    def _():
        relay.wait_send()


def run_layer(*operands):
    f32, bf16 = jnp.float32, jnp.bfloat16
    vmem, dma = pltpu.VMEM, pltpu.SemaphoreType.DMA
    scratch = [
        vmem((3, 2, 768, 768), bf16),
        vmem((3, 2, 768, 768), bf16),
        vmem((CHIP, 768), bf16),
        vmem((CHIP + HALF_PACK, 768), bf16),
        vmem((CHIP, 768), bf16),
        vmem((CHIP, 768), bf16),
        vmem((2, CHIP + HALF_PACK, 768), bf16),
        vmem((2, CHIP, 256), bf16),
        vmem((2, HALF_PACK, 384), bf16),
        vmem((6, 3, PACK, 256), bf16),
        vmem((3, PACK, 256), bf16),
        vmem((2, CHIP, 768), bf16),
        vmem((2, CHIP, 768), bf16),
        vmem((2, CHIP, 256), bf16),
        vmem((CHIP + HALF_PACK, HD), f32),
        vmem((CHIP + HALF_PACK, HD), f32),
        vmem((OWN, 768), f32),
        vmem((OWN, 768), f32),
        vmem((OWN, 768), f32),
        vmem((BLK, 768), f32),
        vmem((OWN, 768), bf16),
        vmem((4, OWN, 768), bf16),
        vmem((OWN, 128), f32),
        vmem((2, 1, 640), f32),
        vmem((16, 8, 128), f32),
        vmem((2, 8, 768), f32),
        vmem((SMALL_ROWS, 768), f32),
        vmem((9, SMALL_ROWS, 768), f32),
        vmem((3, 4, BLK, 768), bf16),
        vmem((3, 4, BLK, 768), bf16),
        vmem((3, 4, 64, 768), bf16),
        vmem((3, 4, 64, 768), bf16),
        vmem((3, 4, BLK, 768), bf16),
        vmem((2, 4, 2, 2 * Z_LAST, 768), bf16),
    ]
    scratch += [dma((3, 4))] * 24 + [dma((3, 8))] * 4
    scratch += [dma((4, 3))] * 4 + [dma((4,))] * 2 + [dma((6,))] * 2 + [dma((7,))] * 2
    whole = pl.BlockSpec(memory_space=vmem)
    return pl.pallas_call(
        layer_kernel,
        out_shape=(
            jax.ShapeDtypeStruct((OWN, 768), bf16),
            jax.ShapeDtypeStruct((OWN, 768), f32),
            jax.ShapeDtypeStruct((3, BLK, 192), f32),
            jax.ShapeDtypeStruct((192, BLK), f32),
            jax.ShapeDtypeStruct((BLK, 768), f32),
            jax.ShapeDtypeStruct((BLK, 768), f32),
            jax.ShapeDtypeStruct((SMALL_ROWS, 768), f32),
        ),
        in_specs=[whole] * len(operands),
        out_specs=(whole,) * 7,
        scratch_shapes=scratch,
        compiler_params=pltpu.CompilerParams(
            collective_id=0, has_side_effects=True, vmem_limit_bytes=63 * 2**20
        ),
    )(*operands)


def fits_kernel(mesh):
    return dict(mesh.shape) == {"wide": 8, "narrow": 4}


def fused_shards(
    tokens,
    type_ids,
    segment_ids,
    cotangent,
    type_table,
    type_first,
    type_second,
    norm_gains,
    gains_first,
    gains_second,
    biases,
    biases_first,
    biases_second,
    qkv_weight,
    qkv_first,
    qkv_second,
    out_weight,
    out_first,
    out_second,
    up_weight,
    up_first,
    up_second,
    up_bias,
    up_bias_first,
    up_bias_second,
    down_weight,
    down_first,
    down_second,
):
    wide, narrow = lax.axis_index("wide"), lax.axis_index("narrow")
    y, core = narrow // 2, narrow % 2
    activations, input_grad, grad_qkv, grad_out, grad_up, grad_down, small = run_layer(
        qkv_weight, out_weight, up_weight.T, down_weight, up_bias[None, :], tokens, type_ids[None, :],
        cotangent, segment_ids, type_table, norm_gains, biases,
    )
    grad_up = grad_up.T
    bias_part = lax.dynamic_slice_in_dim(small, UP_BIAS_ROW + 2 * core + y, 1)[0]
    grad_up_bias = jnp.concatenate(
        [
            lax.dynamic_slice_in_dim(bias_part, wide * 64, 64),
            lax.dynamic_slice_in_dim(bias_part, LAST_AT + wide * Z_LAST, Z_LAST),
        ]
    )
    step_sizes = step_rates()
    updates = [
        adam_update(type_table, type_first, type_second, small[8:10], step_sizes[0]),
        adam_update(norm_gains, gains_first, gains_second, small[0:2], step_sizes[1]),
        adam_update(biases, biases_first, biases_second, small[2:8], step_sizes[2]),
        adam_update(qkv_weight, qkv_first, qkv_second, grad_qkv, step_sizes[3]),
        adam_update(out_weight, out_first, out_second, grad_out, step_sizes[4]),
        adam_update(up_weight, up_first, up_second, grad_up, step_sizes[5]),
        adam_update(up_bias, up_bias_first, up_bias_second, grad_up_bias, step_sizes[6]),
        adam_update(down_weight, down_first, down_second, grad_down, step_sizes[7]),
    ]
    return (activations, input_grad) + tuple(value for update in updates for value in update)


def solution(mesh):
    placed = (
        P(("wide", "narrow"), None),
        P(("wide", "narrow")),
        P("wide", None),
        P(("wide", "narrow"), None),
        P(),
        P(),
        P(),
        P(),
        P(),
        P(),
        P(),
        P(),
        P(),
        P(None, "wide", "narrow"),
        P(None, "wide", "narrow"),
        P(None, "wide", "narrow"),
        P("narrow", "wide"),
        P("narrow", "wide"),
        P("narrow", "wide"),
        P(None, ("wide", "narrow")),
        P(None, ("wide", "narrow")),
        P(None, ("wide", "narrow")),
        P(("wide", "narrow")),
        P(("wide", "narrow")),
        P(("wide", "narrow")),
        P(("wide", "narrow"), None),
        P(("wide", "narrow"), None),
        P(("wide", "narrow"), None),
    )
    return jax.shard_map(
        fused_shards if fits_kernel(mesh) else shards,
        mesh=mesh,
        in_specs=placed,
        out_specs=(
            P(("wide", "narrow"), None),
            P(("wide", "narrow"), None),
            P(),
            P(),
            P(),
            P(),
            P(),
            P(),
            P(),
            P(),
            P(),
            P(None, "wide", "narrow"),
            P(None, "wide", "narrow"),
            P(None, "wide", "narrow"),
            P("narrow", "wide"),
            P("narrow", "wide"),
            P("narrow", "wide"),
            P(None, ("wide", "narrow")),
            P(None, ("wide", "narrow")),
            P(None, ("wide", "narrow")),
            P(("wide", "narrow")),
            P(("wide", "narrow")),
            P(("wide", "narrow")),
            P(("wide", "narrow"), None),
            P(("wide", "narrow"), None),
            P(("wide", "narrow"), None),
        ),
        check_vma=False,
    )
```

```python
import math

import jax
import jax.numpy as jnp
from jax import lax
from jax.experimental import pallas as pl
from jax.experimental.pallas import tpu as pltpu
from jax.sharding import PartitionSpec as P

D = 768
HD = 64
FF = 3072
STEP = 5


norm_eps = 1e-06
masked_score = -1e30


def in_blocks(value, dim, size):
    shape = value.shape
    tiles = value.reshape(*shape[:dim], size, shape[dim] // size, *shape[dim + 1 :])
    return jnp.moveaxis(tiles, dim, 0)


def sent_and_summed(value, axis, dim):
    tiles = in_blocks(value, dim, lax.axis_size(axis))
    arrived = lax.all_to_all(tiles, axis, split_axis=0, concat_axis=0, tiled=True)
    return arrived.astype(jnp.float32).sum(axis=0)


def norm_rows(values, gain, shift):
    center = jnp.mean(values, axis=-1, keepdims=True)
    spread = values - center
    variance = jnp.mean(spread * spread, axis=-1, keepdims=True)
    return spread * lax.rsqrt(variance + norm_eps) * gain + shift


def gelu_exact(values):
    return jax.nn.gelu(values, approximate=False)


def times_transposed(left_mat, right_mat):
    return lax.dot_general(
        left_mat, right_mat, (((1,), (1,)), ((), ())), preferred_element_type=jnp.float32
    )


def transposed_times(left_mat, right_mat):
    return lax.dot_general(
        left_mat, right_mat, (((0,), (0,)), ((), ())), preferred_element_type=jnp.float32
    )


def adam_update(weight_in, moment_one, moment_two, gradient, step_rate):
    moment_one = 0.5 * moment_one + 0.5 * gradient
    moment_two = 0.5 * moment_two + 0.5 * gradient * gradient
    correction = 1.0 - 0.5**STEP
    direction = moment_one / correction / (jnp.sqrt(moment_two / correction) + 1e-08)
    return (weight_in - step_rate * (direction + 0.01 * weight_in), moment_one, moment_two)


def step_rates():
    return (0.5, 0.4, 0.4, D ** (-0.5), 4.0 * D ** (-0.5), D ** (-0.5), 0.4, FF ** (-0.5))


def group_rows(values):
    return lax.all_gather(values, "narrow", axis=0, tiled=True)


def group_sums(term_fn, local_rows):
    return lax.psum_scatter(
        term_fn(jnp.int32(0), lax.axis_size("narrow") * local_rows).astype(jnp.bfloat16),
        "narrow",
        scatter_dimension=0,
        tiled=True,
    ).astype(jnp.float32)


def masked_scores(queries, key_rows, segment):
    raw_scores = jnp.einsum(
        "qhd,khd->hqk", queries, key_rows, preferred_element_type=jnp.float32
    ) * HD ** (-0.5)
    same_doc = segment[:, None] == segment[None, :]
    return jnp.where(same_doc[None, :, :], raw_scores, masked_score)


def pack_forward(pack_item):
    queries, key_rows, values, segment = pack_item
    scores = masked_scores(queries, key_rows, segment)
    highest = jnp.max(scores, axis=-1, keepdims=True)
    exponentials = jnp.exp(scores - highest)
    totals = jnp.sum(exponentials, axis=-1, keepdims=True)
    weights = exponentials / totals
    attended = jnp.einsum(
        "hqk,khd->qhd", weights.astype(jnp.bfloat16), values, preferred_element_type=jnp.float32
    )
    return (attended.astype(jnp.bfloat16), (highest + jnp.log(totals))[:, :, 0])


def pack_backward(pack_item):
    queries, key_rows, values, segment, log_totals, grad_attended = pack_item
    scores = masked_scores(queries, key_rows, segment)
    weights = jnp.exp(scores - log_totals[:, :, None])
    grad_values = jnp.einsum(
        "hqk,qhd->khd",
        weights.astype(jnp.bfloat16),
        grad_attended,
        preferred_element_type=jnp.float32,
    )
    grad_weights = jnp.einsum(
        "qhd,khd->hqk", grad_attended, values, preferred_element_type=jnp.float32
    )
    center = jnp.sum(weights * grad_weights, axis=-1, keepdims=True)
    grad_scores = (weights * (grad_weights - center)).astype(jnp.bfloat16)
    grad_queries = jnp.einsum(
        "hqk,khd->qhd", grad_scores, key_rows, preferred_element_type=jnp.float32
    ) * HD ** (-0.5)
    grad_keys = jnp.einsum(
        "hqk,qhd->khd", grad_scores, queries, preferred_element_type=jnp.float32
    ) * HD ** (-0.5)
    return (
        grad_queries.astype(jnp.bfloat16),
        grad_keys.astype(jnp.bfloat16),
        grad_values.astype(jnp.bfloat16),
    )


def shards(
    tokens,
    type_ids,
    segment_ids,
    cotangent,
    type_table,
    type_first,
    type_second,
    norm_gains,
    gains_first,
    gains_second,
    biases,
    biases_first,
    biases_second,
    qkv_weight,
    qkv_first,
    qkv_second,
    out_weight,
    out_first,
    out_second,
    up_weight,
    up_first,
    up_second,
    up_bias,
    up_bias_first,
    up_bias_second,
    down_weight,
    down_first,
    down_second,
):
    local_rows = tokens.shape[0]
    model_width = tokens.shape[1]
    head_cols = qkv_weight.shape[2]
    heads_here = head_cols // HD
    pack_count = segment_ids.shape[0]
    pack_rows = segment_ids.shape[1]
    group_count = pack_count * pack_rows
    narrow_index = lax.axis_index("narrow")
    qkv_low = qkv_weight.astype(jnp.bfloat16)
    out_low = out_weight.astype(jnp.bfloat16)
    up_low = up_weight.astype(jnp.bfloat16)
    up_bias_low = up_bias.astype(jnp.bfloat16)
    down_low = down_weight.astype(jnp.bfloat16)
    qkv_full, out_rows = (
        lax.all_gather(qkv_low, "wide", axis=1, tiled=True),
        lax.all_gather(out_low, "wide", axis=1, tiled=True),
    )
    up_cols, up_bias_cols, down_rows = (
        lax.all_gather(up_low, ("wide", "narrow"), axis=1, tiled=True),
        lax.all_gather(up_bias_low, ("wide", "narrow"), axis=0, tiled=True),
        lax.all_gather(down_low, ("wide", "narrow"), axis=0, tiled=True),
    )
    is_image = (type_ids == 1)[:, None]
    embedded = tokens.astype(jnp.float32) + jnp.where(
        is_image, type_table[1][None, :], type_table[0][None, :]
    )
    normed1_full, norm1_pull = jax.vjp(norm_rows, embedded, norm_gains[0], biases[0])
    normed1 = normed1_full.astype(jnp.bfloat16)
    group_normed = group_rows(normed1)
    head_offset = narrow_index * head_cols
    bias_query = lax.dynamic_slice_in_dim(biases[1], head_offset, head_cols)
    bias_value = lax.dynamic_slice_in_dim(biases[2], head_offset, head_cols)
    bias_stack = jnp.stack([bias_query, jnp.zeros_like(bias_query), bias_value])
    projected = jnp.einsum(
        "rd,sde->sre", group_normed, qkv_full, preferred_element_type=jnp.float32
    )
    qkv_rows = (projected + bias_stack[:, None, :]).astype(jnp.bfloat16)
    qkv_packs = qkv_rows.reshape(3, pack_count, pack_rows, heads_here, HD)
    attended, log_totals = lax.map(
        pack_forward, (qkv_packs[0], qkv_packs[1], qkv_packs[2], segment_ids)
    )
    attended = attended.reshape(group_count, head_cols)

    def out_term(first_row, row_span):
        return jnp.dot(attended, out_rows, preferred_element_type=jnp.float32)

    attn_proj = group_sums(out_term, local_rows)
    hidden1 = embedded + attn_proj + biases[3]
    normed2_full, norm2_pull = jax.vjp(norm_rows, hidden1, norm_gains[1], biases[4])
    normed2 = normed2_full.astype(jnp.bfloat16)
    mlp_input, mlp_back = (normed2, cotangent)
    pre_act = jnp.dot(mlp_input, up_cols, preferred_element_type=jnp.float32) + up_bias_cols.astype(
        jnp.float32
    )
    activated, gelu_pull = jax.vjp(gelu_exact, pre_act)
    act_low = activated.astype(jnp.bfloat16)
    mlp_out = jnp.dot(act_low, down_rows, preferred_element_type=jnp.float32)
    activations = (hidden1 + mlp_out + biases[5]).astype(jnp.bfloat16)
    grad_act = times_transposed(mlp_back, down_rows)
    (grad_pre,) = gelu_pull(grad_act)
    grad_pre_low = grad_pre.astype(jnp.bfloat16)
    grad_down = transposed_times(act_low, mlp_back)
    grad_up = transposed_times(mlp_input, grad_pre_low)
    grad_up_bias = jnp.sum(grad_pre_low.astype(jnp.float32), axis=0)
    grad_normed2 = times_transposed(grad_pre_low, up_cols)
    grad_hidden_part, grad_gain2, grad_shift2 = norm2_pull(grad_normed2)
    cotangent_full = cotangent.astype(jnp.float32)
    grad_hidden = cotangent_full + grad_hidden_part
    grad_hidden_low = grad_hidden.astype(jnp.bfloat16)
    group_back = group_rows(grad_hidden_low)
    grad_attended = times_transposed(group_back, out_rows).astype(jnp.bfloat16)
    grad_out_weight = transposed_times(attended, group_back)
    back_packs = grad_attended.reshape(pack_count, pack_rows, heads_here, HD)
    grad_queries, grad_keys, grad_values = lax.map(
        pack_backward,
        (qkv_packs[0], qkv_packs[1], qkv_packs[2], segment_ids, log_totals, back_packs),
    )
    grad_qkv_rows = jnp.stack([grad_queries, grad_keys, grad_values]).reshape(
        3, group_count, head_cols
    )
    grad_qkv_weight = jnp.einsum(
        "rd,sre->sde", group_normed, grad_qkv_rows, preferred_element_type=jnp.float32
    )
    head_sums = jnp.sum(grad_qkv_rows.astype(jnp.float32), axis=1)

    def in_term(first_row, row_span):
        return jnp.einsum(
            "sre,sde->rd", grad_qkv_rows, qkv_full, preferred_element_type=jnp.float32
        )

    grad_normed1 = group_sums(in_term, local_rows)
    grad_embed_part, grad_gain1, grad_shift1 = norm1_pull(grad_normed1)
    input_grad = grad_hidden + grad_embed_part
    zero_row = jnp.zeros((model_width,), jnp.float32)
    query_sums = lax.dynamic_update_slice_in_dim(zero_row, head_sums[0], head_offset, 0)
    value_sums = lax.dynamic_update_slice_in_dim(zero_row, head_sums[2], head_offset, 0)
    gain_part = jnp.stack([grad_gain1, grad_gain2])
    shift_part = jnp.stack(
        [
            grad_shift1,
            query_sums,
            value_sums,
            jnp.sum(grad_hidden, axis=0),
            grad_shift2,
            jnp.sum(cotangent_full, axis=0),
        ]
    )
    type_part = jnp.stack(
        [
            jnp.sum(jnp.where(is_image, 0.0, input_grad), axis=0),
            jnp.sum(jnp.where(is_image, input_grad, 0.0), axis=0),
        ]
    )
    grad_gains, grad_biases, grad_types = lax.psum(
        (gain_part, shift_part, type_part), ("wide", "narrow")
    )
    owned_qkv, owned_out = (
        sent_and_summed(grad_qkv_weight.astype(jnp.bfloat16), "wide", 1),
        sent_and_summed(grad_out_weight.astype(jnp.bfloat16), "wide", 1),
    )
    owned_up, owned_up_bias, owned_down = (
        lax.psum_scatter(grad_up, ("wide", "narrow"), scatter_dimension=1, tiled=True),
        lax.psum_scatter(grad_up_bias, ("wide", "narrow"), scatter_dimension=0, tiled=True),
        lax.psum_scatter(grad_down, ("wide", "narrow"), scatter_dimension=0, tiled=True),
    )
    step_sizes = step_rates()
    new_type = adam_update(type_table, type_first, type_second, grad_types, step_sizes[0])
    new_gains = adam_update(norm_gains, gains_first, gains_second, grad_gains, step_sizes[1])
    new_biases = adam_update(biases, biases_first, biases_second, grad_biases, step_sizes[2])
    new_qkv = adam_update(qkv_weight, qkv_first, qkv_second, owned_qkv, step_sizes[3])
    new_out = adam_update(out_weight, out_first, out_second, owned_out, step_sizes[4])
    new_up = adam_update(up_weight, up_first, up_second, owned_up, step_sizes[5])
    new_up_bias = adam_update(up_bias, up_bias_first, up_bias_second, owned_up_bias, step_sizes[6])
    new_down = adam_update(down_weight, down_first, down_second, owned_down, step_sizes[7])
    return (
        activations,
        input_grad,
        new_type[0],
        new_type[1],
        new_type[2],
        new_gains[0],
        new_gains[1],
        new_gains[2],
        new_biases[0],
        new_biases[1],
        new_biases[2],
        new_qkv[0],
        new_qkv[1],
        new_qkv[2],
        new_out[0],
        new_out[1],
        new_out[2],
        new_up[0],
        new_up[1],
        new_up[2],
        new_up_bias[0],
        new_up_bias[1],
        new_up_bias[2],
        new_down[0],
        new_down[1],
        new_down[2],
    )


def dot_nn(left_mat, right_mat):
    return lax.dot_general(
        left_mat, right_mat, (((1,), (0,)), ((), ())), preferred_element_type=jnp.float32
    )


def dot_nt(left_mat, right_mat):
    return lax.dot_general(
        left_mat, right_mat, (((1,), (1,)), ((), ())), preferred_element_type=jnp.float32
    )


def dot_tn(left_mat, right_mat):
    return lax.dot_general(
        left_mat, right_mat, (((0,), (0,)), ((), ())), preferred_element_type=jnp.float32
    )


def rows_at(block, size):
    return pl.ds(pl.multiple_of(block * size, size), size)


def row_stats(values):
    center = jnp.mean(values, axis=-1, keepdims=True)
    spread = values - center
    variance = jnp.mean(spread * spread, axis=-1, keepdims=True)
    scale = lax.rsqrt(variance + norm_eps)
    return spread * scale, scale


def column_sums(values):
    return jnp.sum(values, axis=0, keepdims=True)


ROW = 128
OWN = 384
CHIP = 768
HALF_PACK = 256
PACK = 512
BLK = 96
ATTN, UP, DOWN = 0, 1, 2
Z_FIRST = (96, 80, 80)
Z_LAST = 16
LAST_AT = 640
GATHER_BY_Y = (32, 48, 32)
SCATTER_BY_Y = (48, 32, 16)
GAIN_ROW, BIAS_ROW, TYPE_ROW, UP_BIAS_ROW, SMALL_ROWS = 0, 2, 8, 10, 16


def layer_kernel(
    qkv_weight, out_weight, up_rows, down_rows, up_bias, tokens, type_ids, cotangent, segment_ids, type_table,
    gains, biases, type_first, type_second, gains_first, gains_second, biases_first, biases_second,
    act_out, input_grad, qkv_grad, out_grad, up_out, down_out, small_out,
    full, part, g_all, n1_all, n2_all, dh_all, qkv, att, dkv_far, probs, mask, act, slope, datt,
    key_acc, value_acc, embedded, hidden1, own_sum, attn_out, swap_send, swap_recv, type_cols, qkv_bias,
    bias_slots, bias_row, small, small_recv, rx, ry, rdx, rdy, rz, rl,
    gz_s, gz_r, gx_s, gx_r, gy_s, gy_r, gfx_s, gfx_r, gfy_s, gfy_r,
    sz_s, sz_r, sx_s, sx_r, sy_s, sy_r, sdx_s, sdx_r, sdy_s, sdy_r,
    gl_s, gl_r, sl_s, sl_r, glz_s, glz_r, slz_s, slz_r,
    spread_s, spread_r, swap_s, swap_r, far_s, far_r, bias_s, bias_r, small_s, small_r,
):
    f32, bf16 = jnp.float32, jnp.bfloat16
    wide = lax.axis_index("wide")
    narrow = lax.axis_index("narrow")
    z, x = wide // 2, wide % 2
    y, core = narrow // 2, narrow % 2
    z_of = [z, z + 1 - 2 * (z % 2), (z + 2) % 4, 3 - z]
    sibling = (wide, y * 2 + (1 - core))
    x_side = (z * 2 + (1 - x), narrow)
    y_side = (wide, (1 - y) * 2 + core)
    z_side = [None] + [(z_of[j] * 2 + x, narrow) for j in (1, 2, 3)]

    def copy(src, dst, send, recv, to):
        return pltpu.make_async_remote_copy(
            src_ref=src, dst_ref=dst, send_sem=send, recv_sem=recv, device_id=to,
            device_id_type=pl.DeviceIdType.MESH,
        )

    pending = []
    pending_if = []
    totals = (attn_out, up_out, down_out)

    def start(*args):
        one = copy(*args)
        one.start()
        pending.append(one)
        return one

    barrier = pltpu.get_barrier_semaphore()
    for to in (sibling, x_side, y_side, z_side[1], z_side[2], z_side[3]):
        pl.semaphore_signal(barrier, inc=1, device_id=to, device_id_type=pl.DeviceIdType.MESH)
    pl.semaphore_wait(barrier, 6)

    inner = z * (3 - z) == 2
    outer = z * (3 - z) == 0

    def start_if(which, *args):
        one = copy(*args)

        @pl.when(which)
        def _():
            one.start()

        pending_if.append((which, one))

    def slot(ref, kind, yy, zz, xx, first=0, size=None):
        rows = Z_FIRST[kind]
        row = pl.multiple_of((zz * 2 + xx) * rows + first, 16)
        return ref.at[kind, yy, pl.ds(row, rows if size is None else size)]

    def last(ref, kind, yy, zz, xx, first=0, size=Z_LAST):
        row = pl.multiple_of(LAST_AT + (zz * 2 + xx) * Z_LAST + first, 16)
        return ref.at[kind, yy, pl.ds(row, size)]

    def last_pair(ref, kind, yy, zz):
        return last(ref, kind, yy, zz, 0, 0, 2 * Z_LAST)

    def gather_z(kind):
        mine = slot(full, kind, y, z, x)
        for j in (1, 2):
            start(mine, mine, gz_s.at[kind, j], gz_r.at[kind, j], z_side[j])
        start_if(inner, mine, mine, gz_s.at[kind, 3], gz_r.at[kind, 3], z_side[3])

    def gather_on(kind, j):
        block = slot(full, kind, y, z_of[j], x)
        if j:
            copy(block, block, gz_s.at[kind, j], gz_r.at[kind, j], z_side[j]).wait_recv()
        if j == 2:
            start_if(inner, block, block, gz_s.at[kind, 0], gz_r.at[kind, 3], z_side[1])
        start(block, block, gx_s.at[kind, j], gx_r.at[kind, j], x_side)
        start(block, block, gy_s.at[kind, j], gy_r.at[kind, j], y_side)
        if kind != ATTN and j == 0:
            block = last(full, kind, y, z, x)
            start(block, block, gl_s.at[kind, 0], gl_r.at[kind, 0], x_side)
            start(block, block, gl_s.at[kind, 1], gl_r.at[kind, 1], y_side)

    def gather_far(kind, j):
        zz = z_of[j]
        by_y, by_x = GATHER_BY_Y[kind], Z_FIRST[kind] - GATHER_BY_Y[kind]
        block = slot(full, kind, y, zz, 1 - x)
        copy(block, block, gx_s.at[kind, j], gx_r.at[kind, j], x_side).wait_recv()
        half = slot(full, kind, y, zz, 1 - x, 0, by_y)
        start(half, half, gfy_s.at[kind, j], gfy_r.at[kind, j], y_side)
        block = slot(full, kind, 1 - y, zz, x)
        copy(block, block, gy_s.at[kind, j], gy_r.at[kind, j], y_side).wait_recv()
        half = slot(full, kind, 1 - y, zz, x, by_y, by_x)
        start(half, half, gfx_s.at[kind, j], gfx_r.at[kind, j], x_side)
        if kind != ATTN and j == 0:
            block = last(full, kind, y, z, 1 - x)
            copy(block, block, gl_s.at[kind, 0], gl_r.at[kind, 0], x_side).wait_recv()
            block = last(full, kind, 1 - y, z, x)
            copy(block, block, gl_s.at[kind, 1], gl_r.at[kind, 1], y_side).wait_recv()
            start(block, block, gl_s.at[kind, 2], gl_r.at[kind, 2], x_side)

    def gather_last(kind):
        block = last(full, kind, 1 - y, z, 1 - x)
        copy(block, block, gl_s.at[kind, 2], gl_r.at[kind, 2], x_side).wait_recv()
        for yy in (0, 1):
            pair = last_pair(full, kind, yy, z)
            for j in (1, 2):
                start(pair, pair, glz_s.at[kind, 2 * j + yy], glz_r.at[kind, 2 * j + yy], z_side[j])
            start_if(inner, pair, pair, glz_s.at[kind, 6 + yy], glz_r.at[kind, 6 + yy], z_side[3])

    def last_arrived(kind, j):
        for yy in (0, 1):
            pair = last_pair(full, kind, yy, z_of[j])
            copy(pair, pair, glz_s.at[kind, 2 * j + yy], glz_r.at[kind, 2 * j + yy], z_side[j]).wait_recv()

    def gather_relay(kind):
        last_arrived(kind, 2)
        for yy in (0, 1):
            pair = last_pair(full, kind, yy, z_of[2])
            start_if(inner, pair, pair, glz_s.at[kind, yy], glz_r.at[kind, 6 + yy], z_side[1])

    def gather_last_done(kind):
        last_arrived(kind, 1)
        last_arrived(kind, 3)

    def gather_done(kind):
        by_y, by_x = GATHER_BY_Y[kind], Z_FIRST[kind] - GATHER_BY_Y[kind]
        for j in range(4):
            half = slot(full, kind, 1 - y, z_of[j], 1 - x, 0, by_y)
            copy(half, half, gfy_s.at[kind, j], gfy_r.at[kind, j], y_side).wait_recv()
            half = slot(full, kind, 1 - y, z_of[j], 1 - x, by_y, by_x)
            copy(half, half, gfx_s.at[kind, j], gfx_r.at[kind, j], x_side).wait_recv()

    def add_in(ref, arrived):
        ref[...] = (ref[...].astype(f32) + arrived[...].astype(f32)).astype(bf16)

    def scatter_last(kind):
        for yy in (0, 1):
            def target(j):
                return last_pair(part, kind, yy, z_of[j])

            def landing(j):
                return rl.at[kind - 1, j, yy]

            def sems(sent, landed):
                return slz_s.at[kind, 2 * sent + yy], slz_r.at[kind, 2 * landed + yy]

            start(target(1), landing(1), *sems(1, 1), z_side[1])
            start_if(outer, target(2), landing(2), *sems(2, 2), z_side[2])
            start_if(inner, target(3), landing(3), *sems(3, 3), z_side[3])
            start_if(outer, target(3), landing(0), *sems(3, 0), z_side[1])

    def scatter_relay(kind):
        @pl.when(inner)
        def _():
            for yy in (0, 1):
                here = last_pair(part, kind, yy, z_of[2])
                came = rl.at[kind - 1, 0, yy]
                copy(here, came, slz_s.at[kind, yy], slz_r.at[kind, yy], z_side[1]).wait_recv()
                add_in(here, came)

        for yy in (0, 1):
            here = last_pair(part, kind, yy, z_of[2])
            start_if(
                inner, here, rl.at[kind - 1, 2, yy], slz_s.at[kind, 4 + yy], slz_r.at[kind, 4 + yy], z_side[2]
            )

    def scatter_last_add(kind):
        for yy in (0, 1):
            here = last_pair(part, kind, yy, z)
            for j in (1, 2):
                came = rl.at[kind - 1, j, yy]
                copy(here, came, slz_s.at[kind, 2 * j + yy], slz_r.at[kind, 2 * j + yy], z_side[j]).wait_recv()
            total = here[...].astype(f32) + rl[kind - 1, 1, yy].astype(f32) + rl[kind - 1, 2, yy].astype(f32)
            here[...] = total.astype(bf16)

        @pl.when(inner)
        def _():
            for yy in (0, 1):
                here = last_pair(part, kind, yy, z)
                came = rl.at[kind - 1, 3, yy]
                copy(here, came, slz_s.at[kind, 6 + yy], slz_r.at[kind, 6 + yy], z_side[3]).wait_recv()
                add_in(here, came)

    def scatter_far(kind, j):
        by_y, by_x = SCATTER_BY_Y[kind], Z_FIRST[kind] - SCATTER_BY_Y[kind]
        half = slot(part, kind, 1 - y, z_of[j], 1 - x, 0, by_y)
        start(half, rdy.at[kind, j, pl.ds(0, by_y)], sdy_s.at[kind, j], sdy_r.at[kind, j], y_side)
        half = slot(part, kind, 1 - y, z_of[j], 1 - x, by_y, by_x)
        start(half, rdx.at[kind, j, pl.ds(0, by_x)], sdx_s.at[kind, j], sdx_r.at[kind, j], x_side)
        if kind != ATTN and j == 0:
            block = last(part, kind, 1 - y, z, 1 - x)
            start(block, rdx.at[kind, 0, pl.ds(64, Z_LAST)], sl_s.at[kind, 1], sl_r.at[kind, 1], x_side)

    def scatter_near(kind, j):
        zz = z_of[j]
        rows = Z_FIRST[kind]
        by_y, by_x = SCATTER_BY_Y[kind], rows - SCATTER_BY_Y[kind]
        half = slot(part, kind, y, zz, 1 - x, 0, by_y)
        came = rdy.at[kind, j, pl.ds(0, by_y)]
        copy(half, came, sdy_s.at[kind, j], sdy_r.at[kind, j], y_side).wait_recv()
        add_in(half, came)
        land = pl.ds(0, rows)
        start(slot(part, kind, y, zz, 1 - x), rx.at[kind, j, land], sx_s.at[kind, j], sx_r.at[kind, j], x_side)
        half = slot(part, kind, 1 - y, zz, x, by_y, by_x)
        came = rdx.at[kind, j, pl.ds(0, by_x)]
        copy(half, came, sdx_s.at[kind, j], sdx_r.at[kind, j], x_side).wait_recv()
        add_in(half, came)
        start(slot(part, kind, 1 - y, zz, x), ry.at[kind, j, land], sy_s.at[kind, j], sy_r.at[kind, j], y_side)
        if kind != ATTN and j == 0:
            land = pl.ds(rows, Z_LAST)
            start(last(part, kind, y, z, 1 - x), rx.at[kind, 0, land], sl_s.at[kind, 2], sl_r.at[kind, 2], x_side)
            block = last(part, kind, 1 - y, z, x)
            came = rdx.at[kind, 0, pl.ds(64, Z_LAST)]
            copy(block, came, sl_s.at[kind, 1], sl_r.at[kind, 1], x_side).wait_recv()
            add_in(block, came)
            start(last(part, kind, 1 - y, z, x), ry.at[kind, 0, land], sl_s.at[kind, 3], sl_r.at[kind, 3], y_side)

    def scatter_z(kind, j):
        land = pl.ds(0, Z_FIRST[kind])
        block = slot(part, kind, y, z_of[j], x)
        copy(block, rx.at[kind, j, land], sx_s.at[kind, j], sx_r.at[kind, j], x_side).wait_recv()
        copy(block, ry.at[kind, j, land], sy_s.at[kind, j], sy_r.at[kind, j], y_side).wait_recv()
        total = block[...].astype(f32) + rx[kind, j, land].astype(f32) + ry[kind, j, land].astype(f32)
        if j == 0:
            totals[kind][land] = total
            if kind != ATTN:
                land = pl.ds(Z_FIRST[kind], Z_LAST)
                block = last(part, kind, y, z, x)
                copy(block, rx.at[kind, 0, land], sl_s.at[kind, 2], sl_r.at[kind, 2], x_side).wait_recv()
                copy(block, ry.at[kind, 0, land], sl_s.at[kind, 3], sl_r.at[kind, 3], y_side).wait_recv()
                totals[kind][land] = (
                    block[...].astype(f32) + rx[kind, 0, land].astype(f32) + ry[kind, 0, land].astype(f32)
                )
            return
        block[...] = total.astype(bf16)
        came = rz.at[kind, j, land]
        if j == 1:
            start(block, came, sz_s.at[kind, j], sz_r.at[kind, j], z_side[j])
        elif j == 2:
            relayed = rz.at[kind, 0, land]

            @pl.when(inner)
            def _():
                copy(block, relayed, sz_s.at[kind, 0], sz_r.at[kind, 0], z_side[1]).wait_recv()
                add_in(block, relayed)

            start(block, came, sz_s.at[kind, j], sz_r.at[kind, j], z_side[j])
        else:
            start_if(inner, block, came, sz_s.at[kind, 3], sz_r.at[kind, 3], z_side[3])
            start_if(outer, block, rz.at[kind, 0, land], sz_s.at[kind, 3], sz_r.at[kind, 0], z_side[1])

    def scatter_done(kind):
        land = pl.ds(0, Z_FIRST[kind])
        for j in (1, 2):
            came = rz.at[kind, j, land]
            copy(came, came, sz_s.at[kind, j], sz_r.at[kind, j], z_side[j]).wait_recv()
        totals[kind][land] += rz[kind, 1, land].astype(f32) + rz[kind, 2, land].astype(f32)

        @pl.when(inner)
        def _():
            came = rz.at[kind, 3, land]
            copy(came, came, sz_s.at[kind, 3], sz_r.at[kind, 3], z_side[3]).wait_recv()
            totals[kind][land] += came[...].astype(f32)

    def place(which, block):
        return rows_at((3 * which + block + 4 * y) % 6, ROW)

    def hand_over(ref, use, block):
        here = ref.at[place(core, block)]
        return copy(here, here, spread_s.at[use, block], spread_r.at[use, block], sibling)

    def spread_done(ref, use):
        for block in range(3):
            there = ref.at[place(1 - core, block)]
            copy(there, there, spread_s.at[use, block], spread_r.at[use, block], sibling).wait_recv()
            pending.append(hand_over(ref, use, block))

    def swap_sums(use, term):
        def for_sibling(block, carry):
            rows = rows_at(block, ROW)
            swap_send[rows] = term(place(1 - core, block)).astype(bf16)
            copy(
                swap_send.at[rows], swap_recv.at[use, rows], swap_s.at[use, block],
                swap_r.at[use, block], sibling,
            ).start()
            return carry

        def for_self(block, carry):
            own_sum[rows_at(block, ROW)] = term(place(core, block))
            return carry

        lax.fori_loop(0, 3, for_sibling, 0)
        lax.fori_loop(0, 3, for_self, 0)

    def swap_done(use):
        for block in range(3):
            rows = pl.ds(block * ROW, ROW)
            one = copy(
                swap_send.at[rows], swap_recv.at[use, rows], swap_s.at[use, block],
                swap_r.at[use, block], sibling,
            )
            one.wait_recv()
            one.wait_send()

    def swapped(use, rows):
        return own_sum[rows] + swap_recv[use, rows].astype(f32)

    def own_attn():
        slot(full, ATTN, y, z, x)[...] = jnp.concatenate(
            [qkv_weight[1], qkv_weight[2], qkv_weight[0], out_weight[...].T], axis=1
        ).astype(bf16)

    def own_rest():
        for kind, rows in ((UP, up_rows), (DOWN, down_rows)):
            early = Z_FIRST[kind]
            slot(full, kind, y, z, x)[...] = rows[0:early].astype(bf16)
            last(full, kind, y, z, x)[...] = rows[early:BLK].astype(bf16)

    def as_column(row):
        return jnp.broadcast_to(row, (ROW, ROW)).T

    def column_types():
        types = type_ids[...].astype(f32)
        for block in range(3):
            rows = pl.ds(block * ROW, ROW)
            type_cols[rows] = as_column(types[:, block * ROW : block * ROW + ROW])

    def give_cotangent():
        def body(block, carry):
            g_all[place(core, block)] = cotangent[rows_at(block, ROW)]
            hand_over(g_all, 0, block).start()
            return carry

        lax.fori_loop(0, 3, body, 0)

    def first_norm():
        def body(block, carry):
            rows = rows_at(block, ROW)
            values = tokens[rows].astype(f32) + jnp.where(
                type_cols[rows, 0:1] > 0, type_table[1:2, :], type_table[0:1, :]
            )
            embedded[rows] = values
            xhat, _ = row_stats(values)
            n1_all[place(core, block)] = (xhat * gains[0:1, :] + biases[0:1, :]).astype(bf16)
            hand_over(n1_all, 1, block).start()
            return carry

        lax.fori_loop(0, 3, body, 0)

    half_rows = pl.ds(PACK, HALF_PACK)
    far_rows = pl.ds(CHIP, HALF_PACK)
    over_y = copy(n1_all.at[half_rows], n1_all.at[far_rows], far_s.at[0], far_r.at[0], y_side)
    relay = copy(n1_all.at[far_rows], n1_all.at[far_rows], far_s.at[1], far_r.at[1], sibling)
    holds_half = (core + y) == 1

    def half_over():
        @pl.when(holds_half)
        def _():
            over_y.start()

    def half_relay():
        @pl.when(jnp.logical_not(holds_half))
        def _():
            over_y.wait_recv()
            relay.start()

    def half_arrived():
        @pl.when(holds_half)
        def _():
            relay.wait_recv()

    bias_first = (y * 2 + x) * 4

    def bias_hop(first, size, index, to):
        ref = bias_slots.at[pl.ds(first, size)]
        return start(ref, ref, bias_s.at[index], bias_r.at[index], to)

    def bias_wait(first, size, index, to):
        ref = bias_slots.at[pl.ds(first, size)]
        copy(ref, ref, bias_s.at[index], bias_r.at[index], to).wait_recv()

    def bias_along_z():
        bias_slots[bias_first + z] = jnp.broadcast_to(
            jnp.concatenate(
                [up_bias[...].astype(bf16).astype(f32), jnp.zeros((1, 128 - BLK), f32)], axis=1
            ),
            (8, 128),
        )
        for j in (1, 2, 3):
            bias_hop(bias_first + z, 1, j, z_side[j])

    def bias_along_x():
        for j in (1, 2, 3):
            bias_wait(bias_first + z_of[j], 1, j, z_side[j])
        bias_hop(bias_first, 4, 4, x_side)

    def bias_along_y():
        bias_wait((y * 2 + 1 - x) * 4, 4, 4, x_side)
        bias_hop(y * 8, 8, 5, y_side)

    def bias_as_rows():
        bias_wait((1 - y) * 8, 8, 5, y_side)
        for yy in (0, 1):
            for xx in (0, 1):
                for zz in range(4):
                    which, block = zz * 2 + xx, (yy * 2 + xx) * 4 + zz
                    early = Z_FIRST[UP]
                    first = which * early
                    bias_row[yy, :, first : first + early] = bias_slots[block, :, 0:early]
                    first = LAST_AT + which * Z_LAST
                    bias_row[yy, :, first : first + Z_LAST] = bias_slots[block, :, early:BLK]

    def masks():
        documents = segment_ids[...].astype(f32)
        early = y == 0
        whole_doc = jnp.where(early, documents[0:1], documents[2:3])
        near_doc = jnp.where(early, documents[1:2, 0:256], documents[1:2, 256:512])
        far_doc = jnp.where(early, documents[1:2, 256:512], documents[1:2, 0:256])
        query_rows = (whole_doc[:, 0:256], whole_doc[:, 256:512], near_doc)
        key_rows_of = (whole_doc, jnp.concatenate([near_doc, far_doc], axis=1))
        for side, tiles in ((0, (0, 1)), (1, (2,))):
            for chunk in range(4):
                keys = slice(chunk * ROW, chunk * ROW + ROW)
                column = as_column(key_rows_of[side][:, keys])[:, 0:1]
                for tile in tiles:
                    mask[tile, keys] = jnp.where(
                        column == query_rows[tile], 0.0, masked_score
                    ).astype(bf16)

    def zeros_and_biases():
        small[...] = jnp.zeros_like(small)
        for yy in (0, 1):
            att[yy, :, 0:HD] = jnp.zeros((CHIP, HD), bf16)
            qkv[yy, :, 576:768] = jnp.zeros((CHIP + HALF_PACK, 192), bf16)
            first = yy * 384
            chosen = [
                jnp.where(
                    core == 0,
                    biases[i : i + 1, first : first + 192],
                    biases[i : i + 1, first + 192 : first + 384],
                )
                for i in (2, 1)
            ]
            zeros = jnp.zeros((1, 192), f32)
            qkv_bias[yy] = jnp.concatenate([zeros] + chosen + [zeros[:, 0:64]], axis=1)

    lane = lax.broadcasted_iota(jnp.int32, (1, 640), 1)
    shrink = jnp.where(lane >= 384, HD ** (-0.5), 1.0).astype(f32)

    def project(yy):
        def body(tile, carry):
            rows = rows_at(tile, 256)
            found = dot_nn(n1_all[rows], full[ATTN, yy, :, 0:640]) + qkv_bias[yy]
            qkv[yy, rows, 0:576] = (found * shrink)[:, 0:576].astype(bf16)
            return carry

        lax.fori_loop(0, 4, body, 0, unroll=True)

    def head_rows(yy, head, rows, keys):
        queries = qkv[yy, rows, 384 + HD * head : 448 + HD * head]
        key_rows = qkv[yy, keys, HD * head : HD * head + HD]
        values = qkv[yy, keys, 192 + HD * head : 256 + HD * head]
        return queries, key_rows, values

    def attend(yy, head):
        def body(tile, carry):
            rows = rows_at(tile, 256)
            queries, key_rows, values = head_rows(yy, head, rows, rows_at(tile // 2, PACK))
            scores = dot_nt(key_rows, queries) + mask[tile].astype(f32)
            exponentials = jnp.exp(scores - jnp.max(scores, axis=0, keepdims=True))
            totals = jnp.sum(exponentials, axis=0, keepdims=True)
            weights = (exponentials * (1.0 / totals)).astype(bf16)
            probs[yy * 3 + head, tile] = weights
            att[yy, rows, HD + HD * head : 2 * HD + HD * head] = dot_tn(values, weights).T.astype(bf16)
            return carry

        lax.fori_loop(0, 3, body, 0, unroll=True)

    def out_term(rows):
        return dot_nt(att[0, rows], full[ATTN, 0, :, 512:768]) + dot_nt(
            att[1, rows], full[ATTN, 1, :, 512:768]
        )

    def second_norm():
        def body(block, carry):
            rows = rows_at(block, ROW)
            values = embedded[rows] + swapped(0, rows) + biases[3:4, :]
            hidden1[rows] = values
            xhat, _ = row_stats(values)
            n2_all[place(core, block)] = (xhat * gains[1:2, :] + biases[4:5, :]).astype(bf16)
            hand_over(n2_all, 2, block).start()
            return carry

        lax.fori_loop(0, 3, body, 0)

    def up_chunk(yy, chunk):
        lanes = slice(chunk * 256, chunk * 256 + 256)
        shift = bias_row[yy, 0:1, lanes]

        def body(tile, carry):
            rows = rows_at(tile, 256)
            before = dot_nt(n2_all[rows], full[UP, yy, lanes]) + shift
            normal = 0.5 + 0.5 * lax.erf(before * (0.5**0.5))
            act[yy, rows, lanes] = (before * normal).astype(bf16)
            bell = jnp.exp(-0.5 * before * before) * ((2.0 * math.pi) ** -0.5)
            slope[yy, rows, lanes] = (normal + before * bell).astype(bf16)
            return carry

        lax.fori_loop(0, 3, body, 0, unroll=True)

    def down_grad(yy):
        for chunk in range(3):
            lanes = slice(chunk * 256, chunk * 256 + 256)
            part[DOWN, yy, lanes] = dot_tn(act[yy, :, lanes], g_all[...]).astype(bf16)

    def du_chunk(yy, chunk):
        lanes = slice(chunk * 256, chunk * 256 + 256)

        def body(tile, carry):
            rows = rows_at(tile, 256)
            grad = dot_nt(g_all[rows], full[DOWN, yy, lanes]) * slope[yy, rows, lanes].astype(f32)
            grad = grad.astype(bf16)
            slope[yy, rows, lanes] = grad
            return carry + column_sums(grad.astype(f32))

        total = lax.fori_loop(0, 3, body, jnp.zeros((1, 256), f32), unroll=True)
        for cc in (0, 1):
            for side in (0, 1):
                row = UP_BIAS_ROW + 2 * cc + side
                small[row : row + 1, lanes] = jnp.where(
                    jnp.logical_and(core == cc, yy == side), total, small[row : row + 1, lanes]
                )

    def mlp_term(rows):
        return dot_nn(act[0, rows], full[DOWN, 0]) + dot_nn(act[1, rows], full[DOWN, 1])

    def du_term(rows):
        return dot_nn(slope[0, rows], full[UP, 0]) + dot_nn(slope[1, rows], full[UP, 1])

    def up_grad(yy):
        for chunk in range(3):
            lanes = slice(chunk * 256, chunk * 256 + 256)
            part[UP, yy, lanes] = dot_tn(slope[yy, :, lanes], n2_all[...]).astype(bf16)

    def second_norm_back():
        def body(block, carry):
            rows = rows_at(block, ROW)
            grad = swapped(2, rows)
            xhat, scale = row_stats(hidden1[rows])
            scaled = grad * gains[1:2, :]
            back = (
                scaled
                - jnp.mean(scaled, axis=-1, keepdims=True)
                - xhat * jnp.mean(scaled * xhat, axis=-1, keepdims=True)
            ) * scale
            given = cotangent[rows].astype(f32)
            total = given + back
            input_grad[rows] = total
            dh_all[place(core, block)] = total.astype(bf16)
            hand_over(dh_all, 3, block).start()
            small[1:2, :] += column_sums(grad * xhat)
            small[6:7, :] += column_sums(grad)
            small[5:6, :] += column_sums(total)
            small[7:8, :] += column_sums(given)
            return carry

        lax.fori_loop(0, 3, body, 0)

    def project_back(yy):
        def body(tile, carry):
            rows = rows_at(tile, 256)
            datt[yy, rows] = dot_nn(dh_all[rows], full[ATTN, yy, :, 512:768]).astype(bf16)
            return carry

        lax.fori_loop(0, 3, body, 0, unroll=True)

    def attend_back(yy, head):
        key_acc[...] = jnp.zeros_like(key_acc)
        value_acc[...] = jnp.zeros_like(value_acc)

        def body(tile, carry):
            rows = rows_at(tile, 256)
            keys = rows_at(tile // 2, PACK)
            queries, key_rows, values = head_rows(yy, head, rows, keys)
            grad = datt[yy, rows, HD + HD * head : 2 * HD + HD * head]
            weights = probs[yy * 3 + head, tile]
            weights_full = weights.astype(f32)
            back = dot_nt(values, grad) * weights_full
            center = jnp.sum(back, axis=0, keepdims=True)
            grad_scores = (back - weights_full * center).astype(bf16)
            grad_queries = dot_tn(key_rows, grad_scores) * HD ** (-0.5)
            value_acc[keys] += dot_nn(weights, grad)
            key_acc[keys] += dot_nn(grad_scores, queries)
            qkv[yy, rows, 384 + HD * head : 448 + HD * head] = grad_queries.T.astype(bf16)
            return carry

        lax.fori_loop(0, 3, body, 0, unroll=True)
        qkv[yy, :, HD * head : HD * head + HD] = key_acc[...].astype(bf16)
        qkv[yy, :, 192 + HD * head : 256 + HD * head] = value_acc[...].astype(bf16)

    def send_far(yy):
        start(qkv.at[yy, far_rows, 0:384], dkv_far.at[yy], far_s.at[2 + yy], far_r.at[2 + yy], y_side)

    def add_far(yy):
        copy(
            qkv.at[yy, far_rows, 0:384], dkv_far.at[yy], far_s.at[2 + yy], far_r.at[2 + yy], y_side
        ).wait_recv()
        qkv[yy, half_rows, 0:384] = (
            qkv[yy, half_rows, 0:384].astype(f32) + dkv_far[yy].astype(f32)
        ).astype(bf16)

    def finish_act():
        def body(block, carry):
            rows = rows_at(block, ROW)
            act_out[rows] = (hidden1[rows] + swapped(1, rows) + biases[5:6, :]).astype(bf16)
            return carry

        lax.fori_loop(0, 3, body, 0)

    def attn_grad(yy):
        for chunk in range(3):
            lanes = slice(chunk * 256, chunk * 256 + 256)
            n1_part = n1_all[0:CHIP, lanes]
            part[ATTN, yy, lanes, 0:512] = dot_tn(n1_part, qkv[yy, 0:CHIP, 0:512]).astype(bf16)
            part[ATTN, yy, lanes, 512:768] = (
                dot_tn(n1_part, qkv[yy, 0:CHIP, 512:768]) + dot_tn(dh_all[:, lanes], att[yy])
            ).astype(bf16)

    def in_term(rows):
        return dot_nt(qkv[0, rows], full[ATTN, 0]) + dot_nt(qkv[1, rows], full[ATTN, 1])

    def head_bias_sums():
        for yy in (0, 1):
            sums = column_sums(qkv[yy, 0:CHIP, 192:576].astype(f32))
            for cc in (0, 1):
                first = yy * 384 + cc * 192
                small[4:5, first : first + 192] = jnp.where(core == cc, sums[:, 0:192], 0.0)
                small[3:4, first : first + 192] = jnp.where(core == cc, sums[:, 192:384], 0.0)

    def first_norm_back():
        def body(block, carry):
            rows = rows_at(block, ROW)
            grad = swapped(3, rows)
            xhat, scale = row_stats(embedded[rows])
            scaled = grad * gains[0:1, :]
            back = (
                scaled
                - jnp.mean(scaled, axis=-1, keepdims=True)
                - xhat * jnp.mean(scaled * xhat, axis=-1, keepdims=True)
            ) * scale
            total = input_grad[rows] + back
            input_grad[rows] = total
            small[0:1, :] += column_sums(grad * xhat)
            small[2:3, :] += column_sums(grad)
            image = type_cols[rows, 0:1] > 0
            small[8:9, :] += column_sums(jnp.where(image, 0.0, total))
            small[9:10, :] += column_sums(jnp.where(image, total, 0.0))
            return carry

        lax.fori_loop(0, 3, body, 0)

    def small_core():
        start(small, small_recv.at[4], small_s.at[4], small_r.at[4], sibling)

    def small_x():
        copy(small, small_recv.at[4], small_s.at[4], small_r.at[4], sibling).wait_recv()
        small_recv[5] = small[...] + small_recv[4]
        start(small_recv.at[5], small_recv.at[6], small_s.at[5], small_r.at[5], x_side)

    def small_y():
        copy(small_recv.at[5], small_recv.at[6], small_s.at[5], small_r.at[5], x_side).wait_recv()
        small_recv[7] = small_recv[5] + small_recv[6]
        start(small_recv.at[7], small_recv.at[8], small_s.at[6], small_r.at[6], y_side)

    def small_z():
        copy(small_recv.at[7], small_recv.at[8], small_s.at[6], small_r.at[6], y_side).wait_recv()
        small_recv[z] = small_recv[7] + small_recv[8]
        for j in (1, 2, 3):
            start(small_recv.at[z], small_recv.at[z], small_s.at[j], small_r.at[j], z_side[j])

    def small_done():
        for j in (1, 2, 3):
            there = small_recv.at[z_of[j]]
            copy(there, there, small_s.at[j], small_r.at[j], z_side[j]).wait_recv()
        found = (small_recv[0] + small_recv[1]) + (small_recv[2] + small_recv[3])
        small_out[3] = found
        rates = step_rates()
        for first, kept, rate in (
            (GAIN_ROW, (gains, gains_first, gains_second), rates[1]),
            (BIAS_ROW, (biases, biases_first, biases_second), rates[2]),
            (TYPE_ROW, (type_table, type_first, type_second), rates[0]),
        ):
            rows = slice(first, first + kept[0].shape[0])
            updated = adam_update(*(ref[...] for ref in kept), found[rows], rate)
            for index, value in enumerate(updated):
                small_out[index, rows] = value

    def attn_out_rows():
        qkv_grad[0] = attn_out[:, 384:576]
        qkv_grad[1] = attn_out[:, 0:192]
        qkv_grad[2] = attn_out[:, 192:384]
        out_grad[...] = attn_out[:, 576:768].T

    own_attn()
    gather_on(ATTN, 0)
    bias_along_z()
    gather_z(ATTN)
    own_rest()
    gather_on(DOWN, 0)
    column_types()
    first_norm()
    half_over()
    gather_on(UP, 0)
    bias_along_x()
    give_cotangent()
    gather_far(ATTN, 0)
    zeros_and_biases()
    gather_on(ATTN, 2)
    half_relay()
    gather_z(UP)
    gather_on(ATTN, 1)
    gather_z(DOWN)
    masks()
    gather_on(ATTN, 3)
    gather_far(ATTN, 2)
    half_arrived()
    spread_done(n1_all, 1)
    gather_far(UP, 0)
    gather_far(ATTN, 1)
    spread_done(g_all, 0)
    gather_far(ATTN, 3)
    project(y)
    gather_on(UP, 2)
    gather_on(UP, 1)
    gather_far(DOWN, 0)
    gather_done(ATTN)
    project(1 - y)
    attend(y, 0)
    gather_on(UP, 3)
    gather_on(DOWN, 2)
    gather_last(UP)
    bias_along_y()
    attend(y, 1)
    attend(y, 2)
    gather_on(DOWN, 3)
    gather_far(UP, 2)
    attend(1 - y, 0)
    gather_last(DOWN)
    gather_far(UP, 1)
    attend(1 - y, 1)
    attend(1 - y, 2)
    swap_sums(0, out_term)
    gather_relay(UP)
    bias_as_rows()
    swap_done(0)
    second_norm()
    gather_far(DOWN, 2)
    gather_far(UP, 3)
    gather_on(DOWN, 1)
    gather_far(DOWN, 3)
    spread_done(n2_all, 2)
    gather_last_done(UP)
    gather_relay(DOWN)
    up_chunk(y, 0)
    up_chunk(y, 1)
    up_chunk(y, 2)
    gather_done(UP)
    up_chunk(1 - y, 0)
    up_chunk(1 - y, 1)
    up_chunk(1 - y, 2)
    gather_far(DOWN, 1)
    down_grad(1 - y)
    scatter_far(DOWN, 2)
    down_grad(y)
    gather_last_done(DOWN)
    du_chunk(y, 0)
    scatter_far(DOWN, 3)
    du_chunk(y, 1)
    gather_done(DOWN)
    du_chunk(y, 2)
    scatter_far(DOWN, 1)
    scatter_last(DOWN)
    du_chunk(1 - y, 0)
    du_chunk(1 - y, 1)
    du_chunk(1 - y, 2)
    scatter_near(DOWN, 3)
    swap_sums(2, du_term)
    up_grad(1 - y)
    swap_done(2)
    scatter_far(UP, 3)
    scatter_far(UP, 2)
    second_norm_back()
    up_grad(y)
    scatter_near(DOWN, 2)
    spread_done(dh_all, 3)
    project_back(0)
    scatter_near(UP, 3)
    project_back(1)
    attend_back(0, 0)
    scatter_far(UP, 1)
    scatter_near(DOWN, 1)
    attend_back(0, 1)
    scatter_relay(DOWN)
    attend_back(0, 2)
    send_far(0)
    scatter_last(UP)
    attend_back(1, 0)
    attend_back(1, 1)
    attend_back(1, 2)
    send_far(1)
    scatter_near(UP, 2)
    scatter_z(DOWN, 3)
    swap_sums(1, mlp_term)
    scatter_near(UP, 1)
    add_far(1)
    scatter_last_add(DOWN)
    scatter_relay(UP)
    add_far(0)
    scatter_far(DOWN, 0)
    attn_grad(1 - y)
    head_bias_sums()
    scatter_z(DOWN, 2)
    swap_done(1)
    scatter_far(ATTN, 1)
    scatter_z(UP, 1)
    scatter_far(ATTN, 3)
    scatter_far(ATTN, 0)
    scatter_z(UP, 3)
    attn_grad(y)
    finish_act()
    scatter_z(DOWN, 1)
    scatter_near(ATTN, 1)
    scatter_far(ATTN, 2)
    swap_sums(3, in_term)
    scatter_last_add(UP)
    scatter_z(UP, 2)
    swap_done(3)
    scatter_near(ATTN, 3)
    first_norm_back()
    scatter_z(ATTN, 1)
    scatter_far(UP, 0)
    scatter_near(ATTN, 2)
    scatter_z(ATTN, 3)
    small_core()
    small_x()
    scatter_near(ATTN, 0)
    scatter_z(ATTN, 2)
    small_y()
    scatter_near(UP, 0)
    scatter_z(ATTN, 0)
    small_z()
    scatter_near(DOWN, 0)
    scatter_done(ATTN)
    scatter_z(UP, 0)
    scatter_done(UP)
    small_done()
    scatter_z(DOWN, 0)
    scatter_done(DOWN)
    attn_out_rows()
    for one in pending:
        one.wait_send()
    for which, one in pending_if:
        @pl.when(which)
        def _(one=one):
            one.wait_send()

    @pl.when(holds_half)
    def _():
        over_y.wait_send()

    @pl.when(jnp.logical_not(holds_half))
    def _():
        relay.wait_send()


def run_layer(*operands):
    f32, bf16 = jnp.float32, jnp.bfloat16
    vmem, dma = pltpu.VMEM, pltpu.SemaphoreType.DMA
    scratch = [
        vmem((3, 2, 768, 768), bf16),
        vmem((3, 2, 768, 768), bf16),
        vmem((CHIP, 768), bf16),
        vmem((CHIP + HALF_PACK, 768), bf16),
        vmem((CHIP, 768), bf16),
        vmem((CHIP, 768), bf16),
        vmem((2, CHIP + HALF_PACK, 768), bf16),
        vmem((2, CHIP, 256), bf16),
        vmem((2, HALF_PACK, 384), bf16),
        vmem((6, 3, PACK, 256), bf16),
        vmem((3, PACK, 256), bf16),
        vmem((2, CHIP, 768), bf16),
        vmem((2, CHIP, 768), bf16),
        vmem((2, CHIP, 256), bf16),
        vmem((CHIP + HALF_PACK, HD), f32),
        vmem((CHIP + HALF_PACK, HD), f32),
        vmem((OWN, 768), f32),
        vmem((OWN, 768), f32),
        vmem((OWN, 768), f32),
        vmem((BLK, 768), f32),
        vmem((OWN, 768), bf16),
        vmem((4, OWN, 768), bf16),
        vmem((OWN, 128), f32),
        vmem((2, 1, 640), f32),
        vmem((16, 8, 128), f32),
        vmem((2, 8, 768), f32),
        vmem((SMALL_ROWS, 768), f32),
        vmem((9, SMALL_ROWS, 768), f32),
        vmem((3, 4, BLK, 768), bf16),
        vmem((3, 4, BLK, 768), bf16),
        vmem((3, 4, 80, 768), bf16),
        vmem((3, 4, 48, 768), bf16),
        vmem((3, 4, BLK, 768), bf16),
        vmem((2, 4, 2, 2 * Z_LAST, 768), bf16),
    ]
    scratch += [dma((3, 4))] * 24 + [dma((3, 8))] * 4
    scratch += [dma((4, 3))] * 4 + [dma((4,))] * 2 + [dma((6,))] * 2 + [dma((7,))] * 2
    whole = pl.BlockSpec(memory_space=vmem)
    return pl.pallas_call(
        layer_kernel,
        out_shape=(
            jax.ShapeDtypeStruct((OWN, 768), bf16),
            jax.ShapeDtypeStruct((OWN, 768), f32),
            jax.ShapeDtypeStruct((3, BLK, 192), f32),
            jax.ShapeDtypeStruct((192, BLK), f32),
            jax.ShapeDtypeStruct((BLK, 768), f32),
            jax.ShapeDtypeStruct((BLK, 768), f32),
            jax.ShapeDtypeStruct((4, SMALL_ROWS, 768), f32),
        ),
        in_specs=[whole] * len(operands),
        out_specs=(whole,) * 7,
        scratch_shapes=scratch,
        compiler_params=pltpu.CompilerParams(
            collective_id=0, has_side_effects=True, vmem_limit_bytes=63 * 2**20
        ),
    )(*operands)


def fits_kernel(mesh):
    return dict(mesh.shape) == {"wide": 8, "narrow": 4}


def fused_shards(
    tokens,
    type_ids,
    segment_ids,
    cotangent,
    type_table,
    type_first,
    type_second,
    norm_gains,
    gains_first,
    gains_second,
    biases,
    biases_first,
    biases_second,
    qkv_weight,
    qkv_first,
    qkv_second,
    out_weight,
    out_first,
    out_second,
    up_weight,
    up_first,
    up_second,
    up_bias,
    up_bias_first,
    up_bias_second,
    down_weight,
    down_first,
    down_second,
):
    wide, narrow = lax.axis_index("wide"), lax.axis_index("narrow")
    y, core = narrow // 2, narrow % 2
    activations, input_grad, grad_qkv, grad_out, grad_up, grad_down, small = run_layer(
        qkv_weight, out_weight, up_weight.T, down_weight, up_bias[None, :], tokens, type_ids[None, :],
        cotangent, segment_ids, type_table, norm_gains, biases, type_first, type_second, gains_first,
        gains_second, biases_first, biases_second,
    )
    grad_up = grad_up.T
    bias_part = lax.dynamic_slice_in_dim(small[3], UP_BIAS_ROW + 2 * core + y, 1)[0]
    grad_up_bias = jnp.concatenate(
        [
            lax.dynamic_slice_in_dim(bias_part, wide * Z_FIRST[UP], Z_FIRST[UP]),
            lax.dynamic_slice_in_dim(bias_part, LAST_AT + wide * Z_LAST, Z_LAST),
        ]
    )
    step_sizes = step_rates()
    updates = [
        small[0:3, TYPE_ROW : TYPE_ROW + 2],
        small[0:3, GAIN_ROW : GAIN_ROW + 2],
        small[0:3, BIAS_ROW : BIAS_ROW + 6],
        adam_update(qkv_weight, qkv_first, qkv_second, grad_qkv, step_sizes[3]),
        adam_update(out_weight, out_first, out_second, grad_out, step_sizes[4]),
        adam_update(up_weight, up_first, up_second, grad_up, step_sizes[5]),
        adam_update(up_bias, up_bias_first, up_bias_second, grad_up_bias, step_sizes[6]),
        adam_update(down_weight, down_first, down_second, grad_down, step_sizes[7]),
    ]
    updates = [value for update in updates for value in (update[0], update[1], update[2])]
    return (activations, input_grad, *updates)


def solution(mesh):
    placed = (
        P(("wide", "narrow"), None),
        P(("wide", "narrow")),
        P("wide", None),
        P(("wide", "narrow"), None),
        P(),
        P(),
        P(),
        P(),
        P(),
        P(),
        P(),
        P(),
        P(),
        P(None, "wide", "narrow"),
        P(None, "wide", "narrow"),
        P(None, "wide", "narrow"),
        P("narrow", "wide"),
        P("narrow", "wide"),
        P("narrow", "wide"),
        P(None, ("wide", "narrow")),
        P(None, ("wide", "narrow")),
        P(None, ("wide", "narrow")),
        P(("wide", "narrow")),
        P(("wide", "narrow")),
        P(("wide", "narrow")),
        P(("wide", "narrow"), None),
        P(("wide", "narrow"), None),
        P(("wide", "narrow"), None),
    )
    return jax.shard_map(
        fused_shards if fits_kernel(mesh) else shards,
        mesh=mesh,
        in_specs=placed,
        out_specs=(
            P(("wide", "narrow"), None),
            P(("wide", "narrow"), None),
            P(),
            P(),
            P(),
            P(),
            P(),
            P(),
            P(),
            P(),
            P(),
            P(None, "wide", "narrow"),
            P(None, "wide", "narrow"),
            P(None, "wide", "narrow"),
            P("narrow", "wide"),
            P("narrow", "wide"),
            P("narrow", "wide"),
            P(None, ("wide", "narrow")),
            P(None, ("wide", "narrow")),
            P(None, ("wide", "narrow")),
            P(("wide", "narrow")),
            P(("wide", "narrow")),
            P(("wide", "narrow")),
            P(("wide", "narrow"), None),
            P(("wide", "narrow"), None),
            P(("wide", "narrow"), None),
        ),
        check_vma=False,
    )
```

```python
import math

import jax
import jax.numpy as jnp
from jax import lax
from jax.experimental import pallas as pl
from jax.experimental.pallas import tpu as pltpu
from jax.sharding import PartitionSpec as P

D = 768
HD = 64
FF = 3072
STEP = 5


norm_eps = 1e-06
masked_score = -1e30


def in_blocks(value, dim, size):
    shape = value.shape
    tiles = value.reshape(*shape[:dim], size, shape[dim] // size, *shape[dim + 1 :])
    return jnp.moveaxis(tiles, dim, 0)


def sent_and_summed(value, axis, dim):
    tiles = in_blocks(value, dim, lax.axis_size(axis))
    arrived = lax.all_to_all(tiles, axis, split_axis=0, concat_axis=0, tiled=True)
    return arrived.astype(jnp.float32).sum(axis=0)


def norm_rows(values, gain, shift):
    center = jnp.mean(values, axis=-1, keepdims=True)
    spread = values - center
    variance = jnp.mean(spread * spread, axis=-1, keepdims=True)
    return spread * lax.rsqrt(variance + norm_eps) * gain + shift


def gelu_exact(values):
    return jax.nn.gelu(values, approximate=False)


def times_transposed(left_mat, right_mat):
    return lax.dot_general(
        left_mat, right_mat, (((1,), (1,)), ((), ())), preferred_element_type=jnp.float32
    )


def transposed_times(left_mat, right_mat):
    return lax.dot_general(
        left_mat, right_mat, (((0,), (0,)), ((), ())), preferred_element_type=jnp.float32
    )


def adam_update(weight_in, moment_one, moment_two, gradient, step_rate):
    moment_one = 0.5 * moment_one + 0.5 * gradient
    moment_two = 0.5 * moment_two + 0.5 * gradient * gradient
    correction = 1.0 - 0.5**STEP
    direction = moment_one / correction / (jnp.sqrt(moment_two / correction) + 1e-08)
    return (weight_in - step_rate * (direction + 0.01 * weight_in), moment_one, moment_two)


def step_rates():
    return (0.5, 0.4, 0.4, D ** (-0.5), 4.0 * D ** (-0.5), D ** (-0.5), 0.4, FF ** (-0.5))


def group_rows(values):
    return lax.all_gather(values, "narrow", axis=0, tiled=True)


def group_sums(term_fn, local_rows):
    return lax.psum_scatter(
        term_fn(jnp.int32(0), lax.axis_size("narrow") * local_rows).astype(jnp.bfloat16),
        "narrow",
        scatter_dimension=0,
        tiled=True,
    ).astype(jnp.float32)


def masked_scores(queries, key_rows, segment):
    raw_scores = jnp.einsum(
        "qhd,khd->hqk", queries, key_rows, preferred_element_type=jnp.float32
    ) * HD ** (-0.5)
    same_doc = segment[:, None] == segment[None, :]
    return jnp.where(same_doc[None, :, :], raw_scores, masked_score)


def pack_forward(pack_item):
    queries, key_rows, values, segment = pack_item
    scores = masked_scores(queries, key_rows, segment)
    highest = jnp.max(scores, axis=-1, keepdims=True)
    exponentials = jnp.exp(scores - highest)
    totals = jnp.sum(exponentials, axis=-1, keepdims=True)
    weights = exponentials / totals
    attended = jnp.einsum(
        "hqk,khd->qhd", weights.astype(jnp.bfloat16), values, preferred_element_type=jnp.float32
    )
    return (attended.astype(jnp.bfloat16), (highest + jnp.log(totals))[:, :, 0])


def pack_backward(pack_item):
    queries, key_rows, values, segment, log_totals, grad_attended = pack_item
    scores = masked_scores(queries, key_rows, segment)
    weights = jnp.exp(scores - log_totals[:, :, None])
    grad_values = jnp.einsum(
        "hqk,qhd->khd",
        weights.astype(jnp.bfloat16),
        grad_attended,
        preferred_element_type=jnp.float32,
    )
    grad_weights = jnp.einsum(
        "qhd,khd->hqk", grad_attended, values, preferred_element_type=jnp.float32
    )
    center = jnp.sum(weights * grad_weights, axis=-1, keepdims=True)
    grad_scores = (weights * (grad_weights - center)).astype(jnp.bfloat16)
    grad_queries = jnp.einsum(
        "hqk,khd->qhd", grad_scores, key_rows, preferred_element_type=jnp.float32
    ) * HD ** (-0.5)
    grad_keys = jnp.einsum(
        "hqk,qhd->khd", grad_scores, queries, preferred_element_type=jnp.float32
    ) * HD ** (-0.5)
    return (
        grad_queries.astype(jnp.bfloat16),
        grad_keys.astype(jnp.bfloat16),
        grad_values.astype(jnp.bfloat16),
    )


def shards(
    tokens,
    type_ids,
    segment_ids,
    cotangent,
    type_table,
    type_first,
    type_second,
    norm_gains,
    gains_first,
    gains_second,
    biases,
    biases_first,
    biases_second,
    qkv_weight,
    qkv_first,
    qkv_second,
    out_weight,
    out_first,
    out_second,
    up_weight,
    up_first,
    up_second,
    up_bias,
    up_bias_first,
    up_bias_second,
    down_weight,
    down_first,
    down_second,
):
    local_rows = tokens.shape[0]
    model_width = tokens.shape[1]
    head_cols = qkv_weight.shape[2]
    heads_here = head_cols // HD
    pack_count = segment_ids.shape[0]
    pack_rows = segment_ids.shape[1]
    group_count = pack_count * pack_rows
    narrow_index = lax.axis_index("narrow")
    qkv_low = qkv_weight.astype(jnp.bfloat16)
    out_low = out_weight.astype(jnp.bfloat16)
    up_low = up_weight.astype(jnp.bfloat16)
    up_bias_low = up_bias.astype(jnp.bfloat16)
    down_low = down_weight.astype(jnp.bfloat16)
    qkv_full, out_rows = (
        lax.all_gather(qkv_low, "wide", axis=1, tiled=True),
        lax.all_gather(out_low, "wide", axis=1, tiled=True),
    )
    up_cols, up_bias_cols, down_rows = (
        lax.all_gather(up_low, ("wide", "narrow"), axis=1, tiled=True),
        lax.all_gather(up_bias_low, ("wide", "narrow"), axis=0, tiled=True),
        lax.all_gather(down_low, ("wide", "narrow"), axis=0, tiled=True),
    )
    is_image = (type_ids == 1)[:, None]
    embedded = tokens.astype(jnp.float32) + jnp.where(
        is_image, type_table[1][None, :], type_table[0][None, :]
    )
    normed1_full, norm1_pull = jax.vjp(norm_rows, embedded, norm_gains[0], biases[0])
    normed1 = normed1_full.astype(jnp.bfloat16)
    group_normed = group_rows(normed1)
    head_offset = narrow_index * head_cols
    bias_query = lax.dynamic_slice_in_dim(biases[1], head_offset, head_cols)
    bias_value = lax.dynamic_slice_in_dim(biases[2], head_offset, head_cols)
    bias_stack = jnp.stack([bias_query, jnp.zeros_like(bias_query), bias_value])
    projected = jnp.einsum(
        "rd,sde->sre", group_normed, qkv_full, preferred_element_type=jnp.float32
    )
    qkv_rows = (projected + bias_stack[:, None, :]).astype(jnp.bfloat16)
    qkv_packs = qkv_rows.reshape(3, pack_count, pack_rows, heads_here, HD)
    attended, log_totals = lax.map(
        pack_forward, (qkv_packs[0], qkv_packs[1], qkv_packs[2], segment_ids)
    )
    attended = attended.reshape(group_count, head_cols)

    def out_term(first_row, row_span):
        return jnp.dot(attended, out_rows, preferred_element_type=jnp.float32)

    attn_proj = group_sums(out_term, local_rows)
    hidden1 = embedded + attn_proj + biases[3]
    normed2_full, norm2_pull = jax.vjp(norm_rows, hidden1, norm_gains[1], biases[4])
    normed2 = normed2_full.astype(jnp.bfloat16)
    mlp_input, mlp_back = (normed2, cotangent)
    pre_act = jnp.dot(mlp_input, up_cols, preferred_element_type=jnp.float32) + up_bias_cols.astype(
        jnp.float32
    )
    activated, gelu_pull = jax.vjp(gelu_exact, pre_act)
    act_low = activated.astype(jnp.bfloat16)
    mlp_out = jnp.dot(act_low, down_rows, preferred_element_type=jnp.float32)
    activations = (hidden1 + mlp_out + biases[5]).astype(jnp.bfloat16)
    grad_act = times_transposed(mlp_back, down_rows)
    (grad_pre,) = gelu_pull(grad_act)
    grad_pre_low = grad_pre.astype(jnp.bfloat16)
    grad_down = transposed_times(act_low, mlp_back)
    grad_up = transposed_times(mlp_input, grad_pre_low)
    grad_up_bias = jnp.sum(grad_pre_low.astype(jnp.float32), axis=0)
    grad_normed2 = times_transposed(grad_pre_low, up_cols)
    grad_hidden_part, grad_gain2, grad_shift2 = norm2_pull(grad_normed2)
    cotangent_full = cotangent.astype(jnp.float32)
    grad_hidden = cotangent_full + grad_hidden_part
    grad_hidden_low = grad_hidden.astype(jnp.bfloat16)
    group_back = group_rows(grad_hidden_low)
    grad_attended = times_transposed(group_back, out_rows).astype(jnp.bfloat16)
    grad_out_weight = transposed_times(attended, group_back)
    back_packs = grad_attended.reshape(pack_count, pack_rows, heads_here, HD)
    grad_queries, grad_keys, grad_values = lax.map(
        pack_backward,
        (qkv_packs[0], qkv_packs[1], qkv_packs[2], segment_ids, log_totals, back_packs),
    )
    grad_qkv_rows = jnp.stack([grad_queries, grad_keys, grad_values]).reshape(
        3, group_count, head_cols
    )
    grad_qkv_weight = jnp.einsum(
        "rd,sre->sde", group_normed, grad_qkv_rows, preferred_element_type=jnp.float32
    )
    head_sums = jnp.sum(grad_qkv_rows.astype(jnp.float32), axis=1)

    def in_term(first_row, row_span):
        return jnp.einsum(
            "sre,sde->rd", grad_qkv_rows, qkv_full, preferred_element_type=jnp.float32
        )

    grad_normed1 = group_sums(in_term, local_rows)
    grad_embed_part, grad_gain1, grad_shift1 = norm1_pull(grad_normed1)
    input_grad = grad_hidden + grad_embed_part
    zero_row = jnp.zeros((model_width,), jnp.float32)
    query_sums = lax.dynamic_update_slice_in_dim(zero_row, head_sums[0], head_offset, 0)
    value_sums = lax.dynamic_update_slice_in_dim(zero_row, head_sums[2], head_offset, 0)
    gain_part = jnp.stack([grad_gain1, grad_gain2])
    shift_part = jnp.stack(
        [
            grad_shift1,
            query_sums,
            value_sums,
            jnp.sum(grad_hidden, axis=0),
            grad_shift2,
            jnp.sum(cotangent_full, axis=0),
        ]
    )
    type_part = jnp.stack(
        [
            jnp.sum(jnp.where(is_image, 0.0, input_grad), axis=0),
            jnp.sum(jnp.where(is_image, input_grad, 0.0), axis=0),
        ]
    )
    grad_gains, grad_biases, grad_types = lax.psum(
        (gain_part, shift_part, type_part), ("wide", "narrow")
    )
    owned_qkv, owned_out = (
        sent_and_summed(grad_qkv_weight.astype(jnp.bfloat16), "wide", 1),
        sent_and_summed(grad_out_weight.astype(jnp.bfloat16), "wide", 1),
    )
    owned_up, owned_up_bias, owned_down = (
        lax.psum_scatter(grad_up, ("wide", "narrow"), scatter_dimension=1, tiled=True),
        lax.psum_scatter(grad_up_bias, ("wide", "narrow"), scatter_dimension=0, tiled=True),
        lax.psum_scatter(grad_down, ("wide", "narrow"), scatter_dimension=0, tiled=True),
    )
    step_sizes = step_rates()
    new_type = adam_update(type_table, type_first, type_second, grad_types, step_sizes[0])
    new_gains = adam_update(norm_gains, gains_first, gains_second, grad_gains, step_sizes[1])
    new_biases = adam_update(biases, biases_first, biases_second, grad_biases, step_sizes[2])
    new_qkv = adam_update(qkv_weight, qkv_first, qkv_second, owned_qkv, step_sizes[3])
    new_out = adam_update(out_weight, out_first, out_second, owned_out, step_sizes[4])
    new_up = adam_update(up_weight, up_first, up_second, owned_up, step_sizes[5])
    new_up_bias = adam_update(up_bias, up_bias_first, up_bias_second, owned_up_bias, step_sizes[6])
    new_down = adam_update(down_weight, down_first, down_second, owned_down, step_sizes[7])
    return (
        activations,
        input_grad,
        new_type[0],
        new_type[1],
        new_type[2],
        new_gains[0],
        new_gains[1],
        new_gains[2],
        new_biases[0],
        new_biases[1],
        new_biases[2],
        new_qkv[0],
        new_qkv[1],
        new_qkv[2],
        new_out[0],
        new_out[1],
        new_out[2],
        new_up[0],
        new_up[1],
        new_up[2],
        new_up_bias[0],
        new_up_bias[1],
        new_up_bias[2],
        new_down[0],
        new_down[1],
        new_down[2],
    )


def dot_nn(left_mat, right_mat):
    return lax.dot_general(
        left_mat, right_mat, (((1,), (0,)), ((), ())), preferred_element_type=jnp.float32
    )


def dot_nt(left_mat, right_mat):
    return lax.dot_general(
        left_mat, right_mat, (((1,), (1,)), ((), ())), preferred_element_type=jnp.float32
    )


def dot_tn(left_mat, right_mat):
    return lax.dot_general(
        left_mat, right_mat, (((0,), (0,)), ((), ())), preferred_element_type=jnp.float32
    )


def rows_at(block, size):
    return pl.ds(pl.multiple_of(block * size, size), size)


def row_stats(values):
    center = jnp.mean(values, axis=-1, keepdims=True)
    spread = values - center
    variance = jnp.mean(spread * spread, axis=-1, keepdims=True)
    scale = lax.rsqrt(variance + norm_eps)
    return spread * scale, scale


def column_sums(values):
    return jnp.sum(values, axis=0, keepdims=True)


ROW = 128
OWN = 384
CHIP = 768
HALF_PACK = 256
PACK = 512
BLK = 96
ATTN, UP, DOWN = 0, 1, 2
Z_FIRST = (96, 80, 80)
Z_LAST = 16
LAST_AT = 640
GATHER_BY_Y = (32, 48, 32)
SCATTER_BY_Y = (48, 32, 16)
GAIN_ROW, BIAS_ROW, TYPE_ROW, UP_BIAS_ROW, SMALL_ROWS = 0, 2, 8, 10, 16


def layer_kernel(
    qkv_weight, out_weight, up_rows, down_rows, up_bias, tokens, type_ids, cotangent, segment_ids, type_table,
    gains, biases, type_first, type_second, gains_first, gains_second, biases_first, biases_second,
    act_out, input_grad, qkv_grad, out_grad, up_out, down_out, small_out,
    full, part, g_all, n1_all, n2_all, dh_all, qkv, att, dkv_far, probs, mask, act, slope, datt,
    key_acc, value_acc, embedded, hidden1, own_sum, attn_out, swap_send, swap_recv, type_cols, qkv_bias,
    bias_slots, bias_row, small, small_recv, rx, ry, rdx, rdy, rz, rl,
    gz_s, gz_r, gx_s, gx_r, gy_s, gy_r, gfx_s, gfx_r, gfy_s, gfy_r,
    sz_s, sz_r, sx_s, sx_r, sy_s, sy_r, sdx_s, sdx_r, sdy_s, sdy_r,
    gl_s, gl_r, sl_s, sl_r, glz_s, glz_r, slz_s, slz_r,
    spread_s, spread_r, swap_s, swap_r, far_s, far_r, bias_s, bias_r, small_s, small_r,
):
    f32, bf16 = jnp.float32, jnp.bfloat16
    wide = lax.axis_index("wide")
    narrow = lax.axis_index("narrow")
    z, x = wide // 2, wide % 2
    y, core = narrow // 2, narrow % 2
    z_of = [z, z + 1 - 2 * (z % 2), (z + 2) % 4, 3 - z]
    sibling = (wide, y * 2 + (1 - core))
    x_side = (z * 2 + (1 - x), narrow)
    y_side = (wide, (1 - y) * 2 + core)
    z_side = [None] + [(z_of[j] * 2 + x, narrow) for j in (1, 2, 3)]

    def copy(src, dst, send, recv, to):
        return pltpu.make_async_remote_copy(
            src_ref=src, dst_ref=dst, send_sem=send, recv_sem=recv, device_id=to,
            device_id_type=pl.DeviceIdType.MESH,
        )

    pending = []
    pending_if = []
    totals = (attn_out, up_out, down_out)

    def start(*args):
        one = copy(*args)
        one.start()
        pending.append(one)
        return one

    barrier = pltpu.get_barrier_semaphore()
    for to in (sibling, x_side, y_side, z_side[1], z_side[2], z_side[3]):
        pl.semaphore_signal(barrier, inc=1, device_id=to, device_id_type=pl.DeviceIdType.MESH)
    pl.semaphore_wait(barrier, 6)

    inner = z * (3 - z) == 2
    outer = z * (3 - z) == 0

    def start_if(which, *args):
        one = copy(*args)

        @pl.when(which)
        def _():
            one.start()

        pending_if.append((which, one))

    def slot(ref, kind, yy, zz, xx, first=0, size=None):
        rows = Z_FIRST[kind]
        row = pl.multiple_of((zz * 2 + xx) * rows + first, 16)
        return ref.at[kind, yy, pl.ds(row, rows if size is None else size)]

    def last(ref, kind, yy, zz, xx, first=0, size=Z_LAST):
        row = pl.multiple_of(LAST_AT + (zz * 2 + xx) * Z_LAST + first, 16)
        return ref.at[kind, yy, pl.ds(row, size)]

    def last_pair(ref, kind, yy, zz):
        return last(ref, kind, yy, zz, 0, 0, 2 * Z_LAST)

    def gather_z(kind):
        mine = slot(full, kind, y, z, x)
        for j in (1, 2):
            start(mine, mine, gz_s.at[kind, j], gz_r.at[kind, j], z_side[j])
        start_if(inner, mine, mine, gz_s.at[kind, 3], gz_r.at[kind, 3], z_side[3])

    def gather_on(kind, j):
        block = slot(full, kind, y, z_of[j], x)
        if j:
            copy(block, block, gz_s.at[kind, j], gz_r.at[kind, j], z_side[j]).wait_recv()
        if j == 2:
            start_if(inner, block, block, gz_s.at[kind, 0], gz_r.at[kind, 3], z_side[1])
        start(block, block, gx_s.at[kind, j], gx_r.at[kind, j], x_side)
        start(block, block, gy_s.at[kind, j], gy_r.at[kind, j], y_side)
        if kind != ATTN and j == 0:
            block = last(full, kind, y, z, x)
            start(block, block, gl_s.at[kind, 0], gl_r.at[kind, 0], x_side)
            start(block, block, gl_s.at[kind, 1], gl_r.at[kind, 1], y_side)

    def gather_far(kind, j):
        zz = z_of[j]
        by_y, by_x = GATHER_BY_Y[kind], Z_FIRST[kind] - GATHER_BY_Y[kind]
        block = slot(full, kind, y, zz, 1 - x)
        copy(block, block, gx_s.at[kind, j], gx_r.at[kind, j], x_side).wait_recv()
        half = slot(full, kind, y, zz, 1 - x, 0, by_y)
        start(half, half, gfy_s.at[kind, j], gfy_r.at[kind, j], y_side)
        block = slot(full, kind, 1 - y, zz, x)
        copy(block, block, gy_s.at[kind, j], gy_r.at[kind, j], y_side).wait_recv()
        half = slot(full, kind, 1 - y, zz, x, by_y, by_x)
        start(half, half, gfx_s.at[kind, j], gfx_r.at[kind, j], x_side)
        if kind != ATTN and j == 0:
            block = last(full, kind, y, z, 1 - x)
            copy(block, block, gl_s.at[kind, 0], gl_r.at[kind, 0], x_side).wait_recv()
            block = last(full, kind, 1 - y, z, x)
            copy(block, block, gl_s.at[kind, 1], gl_r.at[kind, 1], y_side).wait_recv()
            start(block, block, gl_s.at[kind, 2], gl_r.at[kind, 2], x_side)

    def gather_last(kind):
        block = last(full, kind, 1 - y, z, 1 - x)
        copy(block, block, gl_s.at[kind, 2], gl_r.at[kind, 2], x_side).wait_recv()
        for yy in (0, 1):
            pair = last_pair(full, kind, yy, z)
            for j in (1, 2):
                start(pair, pair, glz_s.at[kind, 2 * j + yy], glz_r.at[kind, 2 * j + yy], z_side[j])
            start_if(inner, pair, pair, glz_s.at[kind, 6 + yy], glz_r.at[kind, 6 + yy], z_side[3])

    def last_arrived(kind, j):
        for yy in (0, 1):
            pair = last_pair(full, kind, yy, z_of[j])
            copy(pair, pair, glz_s.at[kind, 2 * j + yy], glz_r.at[kind, 2 * j + yy], z_side[j]).wait_recv()

    def gather_relay(kind):
        last_arrived(kind, 2)
        for yy in (0, 1):
            pair = last_pair(full, kind, yy, z_of[2])
            start_if(inner, pair, pair, glz_s.at[kind, yy], glz_r.at[kind, 6 + yy], z_side[1])

    def gather_last_done(kind):
        last_arrived(kind, 1)
        last_arrived(kind, 3)

    def gather_done(kind):
        by_y, by_x = GATHER_BY_Y[kind], Z_FIRST[kind] - GATHER_BY_Y[kind]
        for j in range(4):
            half = slot(full, kind, 1 - y, z_of[j], 1 - x, 0, by_y)
            copy(half, half, gfy_s.at[kind, j], gfy_r.at[kind, j], y_side).wait_recv()
            half = slot(full, kind, 1 - y, z_of[j], 1 - x, by_y, by_x)
            copy(half, half, gfx_s.at[kind, j], gfx_r.at[kind, j], x_side).wait_recv()

    def add_in(ref, arrived):
        ref[...] = (ref[...].astype(f32) + arrived[...].astype(f32)).astype(bf16)

    def scatter_last(kind):
        for yy in (0, 1):
            def target(j):
                return last_pair(part, kind, yy, z_of[j])

            def landing(j):
                return rl.at[kind - 1, j, yy]

            def sems(sent, landed):
                return slz_s.at[kind, 2 * sent + yy], slz_r.at[kind, 2 * landed + yy]

            start(target(1), landing(1), *sems(1, 1), z_side[1])
            start_if(outer, target(2), landing(2), *sems(2, 2), z_side[2])
            start_if(inner, target(3), landing(3), *sems(3, 3), z_side[3])
            start_if(outer, target(3), landing(0), *sems(3, 0), z_side[1])

    def scatter_relay(kind):
        @pl.when(inner)
        def _():
            for yy in (0, 1):
                here = last_pair(part, kind, yy, z_of[2])
                came = rl.at[kind - 1, 0, yy]
                copy(here, came, slz_s.at[kind, yy], slz_r.at[kind, yy], z_side[1]).wait_recv()
                add_in(here, came)

        for yy in (0, 1):
            here = last_pair(part, kind, yy, z_of[2])
            start_if(
                inner, here, rl.at[kind - 1, 2, yy], slz_s.at[kind, 4 + yy], slz_r.at[kind, 4 + yy], z_side[2]
            )

    def scatter_last_add(kind):
        for yy in (0, 1):
            here = last_pair(part, kind, yy, z)
            for j in (1, 2):
                came = rl.at[kind - 1, j, yy]
                copy(here, came, slz_s.at[kind, 2 * j + yy], slz_r.at[kind, 2 * j + yy], z_side[j]).wait_recv()
            total = here[...].astype(f32) + rl[kind - 1, 1, yy].astype(f32) + rl[kind - 1, 2, yy].astype(f32)
            here[...] = total.astype(bf16)

        @pl.when(inner)
        def _():
            for yy in (0, 1):
                here = last_pair(part, kind, yy, z)
                came = rl.at[kind - 1, 3, yy]
                copy(here, came, slz_s.at[kind, 6 + yy], slz_r.at[kind, 6 + yy], z_side[3]).wait_recv()
                add_in(here, came)

    def scatter_far(kind, j):
        by_y, by_x = SCATTER_BY_Y[kind], Z_FIRST[kind] - SCATTER_BY_Y[kind]
        half = slot(part, kind, 1 - y, z_of[j], 1 - x, 0, by_y)
        start(half, rdy.at[kind, j, pl.ds(0, by_y)], sdy_s.at[kind, j], sdy_r.at[kind, j], y_side)
        half = slot(part, kind, 1 - y, z_of[j], 1 - x, by_y, by_x)
        start(half, rdx.at[kind, j, pl.ds(0, by_x)], sdx_s.at[kind, j], sdx_r.at[kind, j], x_side)
        if kind != ATTN and j == 0:
            block = last(part, kind, 1 - y, z, 1 - x)
            start(block, rdx.at[kind, 0, pl.ds(64, Z_LAST)], sl_s.at[kind, 1], sl_r.at[kind, 1], x_side)

    def scatter_near(kind, j):
        zz = z_of[j]
        rows = Z_FIRST[kind]
        by_y, by_x = SCATTER_BY_Y[kind], rows - SCATTER_BY_Y[kind]
        half = slot(part, kind, y, zz, 1 - x, 0, by_y)
        came = rdy.at[kind, j, pl.ds(0, by_y)]
        copy(half, came, sdy_s.at[kind, j], sdy_r.at[kind, j], y_side).wait_recv()
        add_in(half, came)
        land = pl.ds(0, rows)
        start(slot(part, kind, y, zz, 1 - x), rx.at[kind, j, land], sx_s.at[kind, j], sx_r.at[kind, j], x_side)
        half = slot(part, kind, 1 - y, zz, x, by_y, by_x)
        came = rdx.at[kind, j, pl.ds(0, by_x)]
        copy(half, came, sdx_s.at[kind, j], sdx_r.at[kind, j], x_side).wait_recv()
        add_in(half, came)
        start(slot(part, kind, 1 - y, zz, x), ry.at[kind, j, land], sy_s.at[kind, j], sy_r.at[kind, j], y_side)
        if kind != ATTN and j == 0:
            land = pl.ds(rows, Z_LAST)
            start(last(part, kind, y, z, 1 - x), rx.at[kind, 0, land], sl_s.at[kind, 2], sl_r.at[kind, 2], x_side)
            block = last(part, kind, 1 - y, z, x)
            came = rdx.at[kind, 0, pl.ds(64, Z_LAST)]
            copy(block, came, sl_s.at[kind, 1], sl_r.at[kind, 1], x_side).wait_recv()
            add_in(block, came)
            start(last(part, kind, 1 - y, z, x), ry.at[kind, 0, land], sl_s.at[kind, 3], sl_r.at[kind, 3], y_side)

    def scatter_z(kind, j):
        land = pl.ds(0, Z_FIRST[kind])
        block = slot(part, kind, y, z_of[j], x)
        copy(block, rx.at[kind, j, land], sx_s.at[kind, j], sx_r.at[kind, j], x_side).wait_recv()
        copy(block, ry.at[kind, j, land], sy_s.at[kind, j], sy_r.at[kind, j], y_side).wait_recv()
        total = block[...].astype(f32) + rx[kind, j, land].astype(f32) + ry[kind, j, land].astype(f32)
        if j == 0:
            totals[kind][land] = total
            if kind != ATTN:
                land = pl.ds(Z_FIRST[kind], Z_LAST)
                block = last(part, kind, y, z, x)
                copy(block, rx.at[kind, 0, land], sl_s.at[kind, 2], sl_r.at[kind, 2], x_side).wait_recv()
                copy(block, ry.at[kind, 0, land], sl_s.at[kind, 3], sl_r.at[kind, 3], y_side).wait_recv()
                totals[kind][land] = (
                    block[...].astype(f32) + rx[kind, 0, land].astype(f32) + ry[kind, 0, land].astype(f32)
                )
            return
        block[...] = total.astype(bf16)
        came = rz.at[kind, j, land]
        if j == 1:
            start(block, came, sz_s.at[kind, j], sz_r.at[kind, j], z_side[j])
        elif j == 2:
            relayed = rz.at[kind, 0, land]

            @pl.when(inner)
            def _():
                copy(block, relayed, sz_s.at[kind, 0], sz_r.at[kind, 0], z_side[1]).wait_recv()
                add_in(block, relayed)

            start(block, came, sz_s.at[kind, j], sz_r.at[kind, j], z_side[j])
        else:
            start_if(inner, block, came, sz_s.at[kind, 3], sz_r.at[kind, 3], z_side[3])
            start_if(outer, block, rz.at[kind, 0, land], sz_s.at[kind, 3], sz_r.at[kind, 0], z_side[1])

    def scatter_done(kind):
        land = pl.ds(0, Z_FIRST[kind])
        for j in (1, 2):
            came = rz.at[kind, j, land]
            copy(came, came, sz_s.at[kind, j], sz_r.at[kind, j], z_side[j]).wait_recv()
        totals[kind][land] += rz[kind, 1, land].astype(f32) + rz[kind, 2, land].astype(f32)

        @pl.when(inner)
        def _():
            came = rz.at[kind, 3, land]
            copy(came, came, sz_s.at[kind, 3], sz_r.at[kind, 3], z_side[3]).wait_recv()
            totals[kind][land] += came[...].astype(f32)

    def place(which, block):
        return rows_at((3 * which + block + 4 * y) % 6, ROW)

    def hand_over(ref, use, block):
        here = ref.at[place(core, block)]
        return copy(here, here, spread_s.at[use, block], spread_r.at[use, block], sibling)

    def spread_done(ref, use):
        for block in range(3):
            there = ref.at[place(1 - core, block)]
            copy(there, there, spread_s.at[use, block], spread_r.at[use, block], sibling).wait_recv()
            pending.append(hand_over(ref, use, block))

    def swap_sums(use, term):
        def for_sibling(block, carry):
            rows = rows_at(block, ROW)
            swap_send[rows] = term(place(1 - core, block)).astype(bf16)
            copy(
                swap_send.at[rows], swap_recv.at[use, rows], swap_s.at[use, block],
                swap_r.at[use, block], sibling,
            ).start()
            return carry

        def for_self(block, carry):
            own_sum[rows_at(block, ROW)] = term(place(core, block))
            return carry

        lax.fori_loop(0, 3, for_sibling, 0)
        lax.fori_loop(0, 3, for_self, 0)

    def swap_done(use):
        for block in range(3):
            rows = pl.ds(block * ROW, ROW)
            one = copy(
                swap_send.at[rows], swap_recv.at[use, rows], swap_s.at[use, block],
                swap_r.at[use, block], sibling,
            )
            one.wait_recv()
            one.wait_send()

    def swapped(use, rows):
        return own_sum[rows] + swap_recv[use, rows].astype(f32)

    def own_attn():
        slot(full, ATTN, y, z, x)[...] = jnp.concatenate(
            [qkv_weight[1], qkv_weight[2], qkv_weight[0], out_weight[...].T], axis=1
        ).astype(bf16)

    def own_rest():
        for kind, rows in ((UP, up_rows), (DOWN, down_rows)):
            early = Z_FIRST[kind]
            slot(full, kind, y, z, x)[...] = rows[0:early].astype(bf16)
            last(full, kind, y, z, x)[...] = rows[early:BLK].astype(bf16)

    def as_column(row):
        return jnp.broadcast_to(row, (ROW, ROW)).T

    def column_types():
        types = type_ids[...].astype(f32)
        for block in range(3):
            rows = pl.ds(block * ROW, ROW)
            type_cols[rows] = as_column(types[:, block * ROW : block * ROW + ROW])

    def give_cotangent():
        def body(block, carry):
            g_all[place(core, block)] = cotangent[rows_at(block, ROW)]
            hand_over(g_all, 0, block).start()
            return carry

        lax.fori_loop(0, 3, body, 0)

    def first_norm():
        def body(block, carry):
            rows = rows_at(block, ROW)
            values = tokens[rows].astype(f32) + jnp.where(
                type_cols[rows, 0:1] > 0, type_table[1:2, :], type_table[0:1, :]
            )
            embedded[rows] = values
            xhat, _ = row_stats(values)
            n1_all[place(core, block)] = (xhat * gains[0:1, :] + biases[0:1, :]).astype(bf16)
            hand_over(n1_all, 1, block).start()
            return carry

        lax.fori_loop(0, 3, body, 0)

    half_rows = pl.ds(PACK, HALF_PACK)
    far_rows = pl.ds(CHIP, HALF_PACK)
    over_y = copy(n1_all.at[half_rows], n1_all.at[far_rows], far_s.at[0], far_r.at[0], y_side)
    relay = copy(n1_all.at[far_rows], n1_all.at[far_rows], far_s.at[1], far_r.at[1], sibling)
    holds_half = (core + y) == 1

    def half_over():
        @pl.when(holds_half)
        def _():
            over_y.start()

    def half_relay():
        @pl.when(jnp.logical_not(holds_half))
        def _():
            over_y.wait_recv()
            relay.start()

    def half_arrived():
        @pl.when(holds_half)
        def _():
            relay.wait_recv()

    bias_first = (y * 2 + x) * 4

    def bias_hop(first, size, index, to):
        ref = bias_slots.at[pl.ds(first, size)]
        return start(ref, ref, bias_s.at[index], bias_r.at[index], to)

    def bias_wait(first, size, index, to):
        ref = bias_slots.at[pl.ds(first, size)]
        copy(ref, ref, bias_s.at[index], bias_r.at[index], to).wait_recv()

    def bias_along_z():
        bias_slots[bias_first + z] = jnp.broadcast_to(
            jnp.concatenate(
                [up_bias[...].astype(bf16).astype(f32), jnp.zeros((1, 128 - BLK), f32)], axis=1
            ),
            (8, 128),
        )
        for j in (1, 2, 3):
            bias_hop(bias_first + z, 1, j, z_side[j])

    def bias_along_x():
        for j in (1, 2, 3):
            bias_wait(bias_first + z_of[j], 1, j, z_side[j])
        bias_hop(bias_first, 4, 4, x_side)

    def bias_along_y():
        bias_wait((y * 2 + 1 - x) * 4, 4, 4, x_side)
        bias_hop(y * 8, 8, 5, y_side)

    def bias_as_rows():
        bias_wait((1 - y) * 8, 8, 5, y_side)
        for yy in (0, 1):
            for xx in (0, 1):
                for zz in range(4):
                    which, block = zz * 2 + xx, (yy * 2 + xx) * 4 + zz
                    early = Z_FIRST[UP]
                    first = which * early
                    bias_row[yy, :, first : first + early] = bias_slots[block, :, 0:early]
                    first = LAST_AT + which * Z_LAST
                    bias_row[yy, :, first : first + Z_LAST] = bias_slots[block, :, early:BLK]

    def masks():
        documents = segment_ids[...].astype(f32)
        early = y == 0
        whole_doc = jnp.where(early, documents[0:1], documents[2:3])
        near_doc = jnp.where(early, documents[1:2, 0:256], documents[1:2, 256:512])
        far_doc = jnp.where(early, documents[1:2, 256:512], documents[1:2, 0:256])
        query_rows = (whole_doc[:, 0:256], whole_doc[:, 256:512], near_doc)
        key_rows_of = (whole_doc, jnp.concatenate([near_doc, far_doc], axis=1))
        for side, tiles in ((0, (0, 1)), (1, (2,))):
            for chunk in range(4):
                keys = slice(chunk * ROW, chunk * ROW + ROW)
                column = as_column(key_rows_of[side][:, keys])[:, 0:1]
                for tile in tiles:
                    mask[tile, keys] = jnp.where(
                        column == query_rows[tile], 0.0, masked_score
                    ).astype(bf16)

    def zeros_and_biases():
        small[...] = jnp.zeros_like(small)
        for yy in (0, 1):
            att[yy, :, 0:HD] = jnp.zeros((CHIP, HD), bf16)
            qkv[yy, :, 576:768] = jnp.zeros((CHIP + HALF_PACK, 192), bf16)
            first = yy * 384
            chosen = [
                jnp.where(
                    core == 0,
                    biases[i : i + 1, first : first + 192],
                    biases[i : i + 1, first + 192 : first + 384],
                )
                for i in (2, 1)
            ]
            zeros = jnp.zeros((1, 192), f32)
            qkv_bias[yy] = jnp.concatenate([zeros] + chosen + [zeros[:, 0:64]], axis=1)

    lane = lax.broadcasted_iota(jnp.int32, (1, 640), 1)
    shrink = jnp.where(lane >= 384, HD ** (-0.5), 1.0).astype(f32)

    def project(yy):
        def body(tile, carry):
            rows = rows_at(tile, 256)
            found = dot_nn(n1_all[rows], full[ATTN, yy, :, 0:640]) + qkv_bias[yy]
            qkv[yy, rows, 0:576] = (found * shrink)[:, 0:576].astype(bf16)
            return carry

        lax.fori_loop(0, 4, body, 0, unroll=True)

    def head_rows(yy, head, rows, keys):
        queries = qkv[yy, rows, 384 + HD * head : 448 + HD * head]
        key_rows = qkv[yy, keys, HD * head : HD * head + HD]
        values = qkv[yy, keys, 192 + HD * head : 256 + HD * head]
        return queries, key_rows, values

    def attend(yy, head):
        def body(tile, carry):
            rows = rows_at(tile, 256)
            queries, key_rows, values = head_rows(yy, head, rows, rows_at(tile // 2, PACK))
            scores = dot_nt(key_rows, queries) + mask[tile].astype(f32)
            exponentials = jnp.exp(scores - jnp.max(scores, axis=0, keepdims=True))
            totals = jnp.sum(exponentials, axis=0, keepdims=True)
            weights = (exponentials * (1.0 / totals)).astype(bf16)
            probs[yy * 3 + head, tile] = weights
            att[yy, rows, HD + HD * head : 2 * HD + HD * head] = dot_tn(values, weights).T.astype(bf16)
            return carry

        lax.fori_loop(0, 3, body, 0, unroll=True)

    def out_term(rows):
        return dot_nt(att[0, rows], full[ATTN, 0, :, 512:768]) + dot_nt(
            att[1, rows], full[ATTN, 1, :, 512:768]
        )

    def second_norm():
        def body(block, carry):
            rows = rows_at(block, ROW)
            values = embedded[rows] + swapped(0, rows) + biases[3:4, :]
            hidden1[rows] = values
            xhat, _ = row_stats(values)
            n2_all[place(core, block)] = (xhat * gains[1:2, :] + biases[4:5, :]).astype(bf16)
            hand_over(n2_all, 2, block).start()
            return carry

        lax.fori_loop(0, 3, body, 0)

    def up_chunk(yy, chunk):
        lanes = slice(chunk * 256, chunk * 256 + 256)
        shift = bias_row[yy, 0:1, lanes]

        def body(tile, carry):
            rows = rows_at(tile, 256)
            before = dot_nt(n2_all[rows], full[UP, yy, lanes]) + shift
            normal = 0.5 + 0.5 * lax.erf(before * (0.5**0.5))
            act[yy, rows, lanes] = (before * normal).astype(bf16)
            bell = jnp.exp(-0.5 * before * before) * ((2.0 * math.pi) ** -0.5)
            slope[yy, rows, lanes] = (normal + before * bell).astype(bf16)
            return carry

        lax.fori_loop(0, 3, body, 0, unroll=True)

    def down_grad(yy):
        for chunk in range(3):
            lanes = slice(chunk * 256, chunk * 256 + 256)
            part[DOWN, yy, lanes] = dot_tn(act[yy, :, lanes], g_all[...]).astype(bf16)

    def du_chunk(yy, chunk):
        lanes = slice(chunk * 256, chunk * 256 + 256)

        def body(tile, carry):
            rows = rows_at(tile, 256)
            grad = dot_nt(g_all[rows], full[DOWN, yy, lanes]) * slope[yy, rows, lanes].astype(f32)
            grad = grad.astype(bf16)
            slope[yy, rows, lanes] = grad
            return carry + column_sums(grad.astype(f32))

        total = lax.fori_loop(0, 3, body, jnp.zeros((1, 256), f32), unroll=True)
        for cc in (0, 1):
            for side in (0, 1):
                row = UP_BIAS_ROW + 2 * cc + side
                small[row : row + 1, lanes] = jnp.where(
                    jnp.logical_and(core == cc, yy == side), total, small[row : row + 1, lanes]
                )

    def mlp_term(rows):
        return dot_nn(act[0, rows], full[DOWN, 0]) + dot_nn(act[1, rows], full[DOWN, 1])

    def du_term(rows):
        return dot_nn(slope[0, rows], full[UP, 0]) + dot_nn(slope[1, rows], full[UP, 1])

    def up_grad(yy):
        for chunk in range(3):
            lanes = slice(chunk * 256, chunk * 256 + 256)
            part[UP, yy, lanes] = dot_tn(slope[yy, :, lanes], n2_all[...]).astype(bf16)

    def second_norm_back():
        def body(block, carry):
            rows = rows_at(block, ROW)
            grad = swapped(2, rows)
            xhat, scale = row_stats(hidden1[rows])
            scaled = grad * gains[1:2, :]
            back = (
                scaled
                - jnp.mean(scaled, axis=-1, keepdims=True)
                - xhat * jnp.mean(scaled * xhat, axis=-1, keepdims=True)
            ) * scale
            given = cotangent[rows].astype(f32)
            total = given + back
            input_grad[rows] = total
            dh_all[place(core, block)] = total.astype(bf16)
            hand_over(dh_all, 3, block).start()
            small[1:2, :] += column_sums(grad * xhat)
            small[6:7, :] += column_sums(grad)
            small[5:6, :] += column_sums(total)
            small[7:8, :] += column_sums(given)
            return carry

        lax.fori_loop(0, 3, body, 0)

    def project_back(yy):
        def body(tile, carry):
            rows = rows_at(tile, 256)
            datt[yy, rows] = dot_nn(dh_all[rows], full[ATTN, yy, :, 512:768]).astype(bf16)
            return carry

        lax.fori_loop(0, 3, body, 0, unroll=True)

    def attend_back(yy, head):
        key_acc[...] = jnp.zeros_like(key_acc)
        value_acc[...] = jnp.zeros_like(value_acc)

        def body(tile, carry):
            rows = rows_at(tile, 256)
            keys = rows_at(tile // 2, PACK)
            queries, key_rows, values = head_rows(yy, head, rows, keys)
            grad = datt[yy, rows, HD + HD * head : 2 * HD + HD * head]
            weights = probs[yy * 3 + head, tile]
            weights_full = weights.astype(f32)
            back = dot_nt(values, grad) * weights_full
            center = jnp.sum(back, axis=0, keepdims=True)
            grad_scores = (back - weights_full * center).astype(bf16)
            grad_queries = dot_tn(key_rows, grad_scores) * HD ** (-0.5)
            value_acc[keys] += dot_nn(weights, grad)
            key_acc[keys] += dot_nn(grad_scores, queries)
            qkv[yy, rows, 384 + HD * head : 448 + HD * head] = grad_queries.T.astype(bf16)
            return carry

        lax.fori_loop(0, 3, body, 0, unroll=True)
        qkv[yy, :, HD * head : HD * head + HD] = key_acc[...].astype(bf16)
        qkv[yy, :, 192 + HD * head : 256 + HD * head] = value_acc[...].astype(bf16)

    def send_far(yy):
        start(qkv.at[yy, far_rows, 0:384], dkv_far.at[yy], far_s.at[2 + yy], far_r.at[2 + yy], y_side)

    def add_far(yy):
        copy(
            qkv.at[yy, far_rows, 0:384], dkv_far.at[yy], far_s.at[2 + yy], far_r.at[2 + yy], y_side
        ).wait_recv()
        qkv[yy, half_rows, 0:384] = (
            qkv[yy, half_rows, 0:384].astype(f32) + dkv_far[yy].astype(f32)
        ).astype(bf16)

    def finish_act():
        def body(block, carry):
            rows = rows_at(block, ROW)
            act_out[rows] = (hidden1[rows] + swapped(1, rows) + biases[5:6, :]).astype(bf16)
            return carry

        lax.fori_loop(0, 3, body, 0)

    def attn_grad(yy):
        for chunk in range(3):
            lanes = slice(chunk * 256, chunk * 256 + 256)
            n1_part = n1_all[0:CHIP, lanes]
            part[ATTN, yy, lanes, 0:512] = dot_tn(n1_part, qkv[yy, 0:CHIP, 0:512]).astype(bf16)
            part[ATTN, yy, lanes, 512:768] = (
                dot_tn(n1_part, qkv[yy, 0:CHIP, 512:768]) + dot_tn(dh_all[:, lanes], att[yy])
            ).astype(bf16)

    def in_term(rows):
        return dot_nt(qkv[0, rows], full[ATTN, 0]) + dot_nt(qkv[1, rows], full[ATTN, 1])

    def head_bias_sums():
        for yy in (0, 1):
            sums = column_sums(qkv[yy, 0:CHIP, 192:576].astype(f32))
            for cc in (0, 1):
                first = yy * 384 + cc * 192
                small[4:5, first : first + 192] = jnp.where(core == cc, sums[:, 0:192], 0.0)
                small[3:4, first : first + 192] = jnp.where(core == cc, sums[:, 192:384], 0.0)

    def first_norm_back():
        def body(block, carry):
            rows = rows_at(block, ROW)
            grad = swapped(3, rows)
            xhat, scale = row_stats(embedded[rows])
            scaled = grad * gains[0:1, :]
            back = (
                scaled
                - jnp.mean(scaled, axis=-1, keepdims=True)
                - xhat * jnp.mean(scaled * xhat, axis=-1, keepdims=True)
            ) * scale
            total = input_grad[rows] + back
            input_grad[rows] = total
            small[0:1, :] += column_sums(grad * xhat)
            small[2:3, :] += column_sums(grad)
            image = type_cols[rows, 0:1] > 0
            small[8:9, :] += column_sums(jnp.where(image, 0.0, total))
            small[9:10, :] += column_sums(jnp.where(image, total, 0.0))
            return carry

        lax.fori_loop(0, 3, body, 0)

    def small_core():
        start(small, small_recv.at[4], small_s.at[4], small_r.at[4], sibling)

    def small_x():
        copy(small, small_recv.at[4], small_s.at[4], small_r.at[4], sibling).wait_recv()
        small_recv[5] = small[...] + small_recv[4]
        start(small_recv.at[5], small_recv.at[6], small_s.at[5], small_r.at[5], x_side)

    def small_y():
        copy(small_recv.at[5], small_recv.at[6], small_s.at[5], small_r.at[5], x_side).wait_recv()
        small_recv[7] = small_recv[5] + small_recv[6]
        start(small_recv.at[7], small_recv.at[8], small_s.at[6], small_r.at[6], y_side)

    def small_z():
        copy(small_recv.at[7], small_recv.at[8], small_s.at[6], small_r.at[6], y_side).wait_recv()
        small_recv[z] = small_recv[7] + small_recv[8]
        for j in (1, 2, 3):
            start(small_recv.at[z], small_recv.at[z], small_s.at[j], small_r.at[j], z_side[j])

    def small_done():
        for j in (1, 2, 3):
            there = small_recv.at[z_of[j]]
            copy(there, there, small_s.at[j], small_r.at[j], z_side[j]).wait_recv()
        found = (small_recv[0] + small_recv[1]) + (small_recv[2] + small_recv[3])
        small_out[3] = found
        rates = step_rates()
        for first, kept, rate in (
            (GAIN_ROW, (gains, gains_first, gains_second), rates[1]),
            (BIAS_ROW, (biases, biases_first, biases_second), rates[2]),
            (TYPE_ROW, (type_table, type_first, type_second), rates[0]),
        ):
            rows = slice(first, first + kept[0].shape[0])
            updated = adam_update(*(ref[...] for ref in kept), found[rows], rate)
            for index, value in enumerate(updated):
                small_out[index, rows] = value

    def attn_out_rows():
        qkv_grad[0] = attn_out[:, 384:576]
        qkv_grad[1] = attn_out[:, 0:192]
        qkv_grad[2] = attn_out[:, 192:384]
        out_grad[...] = attn_out[:, 576:768].T

    own_attn()
    gather_on(ATTN, 0)
    own_rest()
    gather_z(ATTN)
    column_types()
    gather_on(UP, 0)
    first_norm()
    bias_along_z()
    masks()
    half_over()
    gather_far(UP, 0)
    gather_on(ATTN, 1)
    bias_along_x()
    gather_far(ATTN, 0)
    half_relay()
    spread_done(n1_all, 1)
    gather_on(ATTN, 2)
    gather_last(UP)
    give_cotangent()
    gather_z(UP)
    zeros_and_biases()
    gather_on(ATTN, 3)
    half_arrived()
    bias_along_y()
    gather_far(ATTN, 1)
    gather_far(ATTN, 2)
    gather_far(ATTN, 3)
    gather_on(DOWN, 0)
    gather_on(UP, 2)
    spread_done(g_all, 0)
    project(y)
    gather_on(UP, 1)
    gather_done(ATTN)
    project(1 - y)
    gather_z(DOWN)
    attend(y, 0)
    attend(y, 1)
    gather_far(DOWN, 0)
    attend(y, 2)
    gather_far(UP, 2)
    attend(1 - y, 0)
    gather_on(UP, 3)
    attend(1 - y, 1)
    gather_relay(UP)
    attend(1 - y, 2)
    gather_last(DOWN)
    gather_on(DOWN, 1)
    gather_far(UP, 1)
    gather_on(DOWN, 2)
    gather_last_done(UP)
    swap_sums(0, out_term)
    gather_far(UP, 3)
    swap_done(0)
    second_norm()
    bias_as_rows()
    gather_on(DOWN, 3)
    gather_far(DOWN, 1)
    spread_done(n2_all, 2)
    up_chunk(y, 0)
    up_chunk(y, 1)
    up_chunk(y, 2)
    gather_relay(DOWN)
    gather_far(DOWN, 2)
    gather_done(UP)
    up_chunk(1 - y, 0)
    up_chunk(1 - y, 1)
    gather_last_done(DOWN)
    up_chunk(1 - y, 2)
    gather_far(DOWN, 3)
    down_grad(1 - y)
    scatter_far(DOWN, 2)
    down_grad(y)
    scatter_far(DOWN, 1)
    du_chunk(y, 0)
    scatter_last(DOWN)
    du_chunk(y, 1)
    gather_done(DOWN)
    du_chunk(y, 2)
    du_chunk(1 - y, 0)
    du_chunk(1 - y, 1)
    du_chunk(1 - y, 2)
    scatter_far(DOWN, 3)
    scatter_near(DOWN, 1)
    up_grad(1 - y)
    scatter_far(UP, 2)
    scatter_near(DOWN, 2)
    scatter_far(UP, 3)
    scatter_far(UP, 1)
    swap_sums(2, du_term)
    scatter_relay(DOWN)
    scatter_near(DOWN, 3)
    swap_done(2)
    second_norm_back()
    up_grad(y)
    scatter_near(UP, 2)
    scatter_last_add(DOWN)
    spread_done(dh_all, 3)
    project_back(0)
    scatter_last(UP)
    project_back(1)
    attend_back(0, 0)
    scatter_near(UP, 3)
    attend_back(0, 1)
    attend_back(0, 2)
    send_far(0)
    attend_back(1, 0)
    attend_back(1, 1)
    attend_back(1, 2)
    send_far(1)
    scatter_z(DOWN, 3)
    scatter_near(UP, 1)
    scatter_far(DOWN, 0)
    scatter_z(UP, 3)
    swap_sums(1, mlp_term)
    scatter_z(DOWN, 2)
    swap_done(1)
    finish_act()
    add_far(1)
    add_far(0)
    attn_grad(1 - y)
    scatter_z(DOWN, 1)
    scatter_far(ATTN, 3)
    scatter_z(UP, 1)
    scatter_far(ATTN, 1)
    attn_grad(y)
    scatter_relay(UP)
    scatter_far(ATTN, 2)
    scatter_near(ATTN, 3)
    swap_sums(3, in_term)
    scatter_near(DOWN, 0)
    head_bias_sums()
    scatter_near(ATTN, 2)
    scatter_z(ATTN, 3)
    swap_done(3)
    scatter_z(UP, 2)
    scatter_near(ATTN, 1)
    scatter_z(DOWN, 0)
    scatter_last_add(UP)
    first_norm_back()
    small_core()
    scatter_z(ATTN, 2)
    small_x()
    scatter_done(DOWN)
    scatter_far(ATTN, 0)
    small_y()
    scatter_far(UP, 0)
    scatter_near(ATTN, 0)
    scatter_z(ATTN, 1)
    small_z()
    scatter_near(UP, 0)
    scatter_z(ATTN, 0)
    small_done()
    scatter_done(ATTN)
    attn_out_rows()
    scatter_z(UP, 0)
    scatter_done(UP)
    for one in pending:
        one.wait_send()
    for which, one in pending_if:
        @pl.when(which)
        def _(one=one):
            one.wait_send()

    @pl.when(holds_half)
    def _():
        over_y.wait_send()

    @pl.when(jnp.logical_not(holds_half))
    def _():
        relay.wait_send()


def run_layer(*operands):
    f32, bf16 = jnp.float32, jnp.bfloat16
    vmem, dma = pltpu.VMEM, pltpu.SemaphoreType.DMA
    scratch = [
        vmem((3, 2, 768, 768), bf16),
        vmem((3, 2, 768, 768), bf16),
        vmem((CHIP, 768), bf16),
        vmem((CHIP + HALF_PACK, 768), bf16),
        vmem((CHIP, 768), bf16),
        vmem((CHIP, 768), bf16),
        vmem((2, CHIP + HALF_PACK, 768), bf16),
        vmem((2, CHIP, 256), bf16),
        vmem((2, HALF_PACK, 384), bf16),
        vmem((6, 3, PACK, 256), bf16),
        vmem((3, PACK, 256), bf16),
        vmem((2, CHIP, 768), bf16),
        vmem((2, CHIP, 768), bf16),
        vmem((2, CHIP, 256), bf16),
        vmem((CHIP + HALF_PACK, HD), f32),
        vmem((CHIP + HALF_PACK, HD), f32),
        vmem((OWN, 768), f32),
        vmem((OWN, 768), f32),
        vmem((OWN, 768), f32),
        vmem((BLK, 768), f32),
        vmem((OWN, 768), bf16),
        vmem((4, OWN, 768), bf16),
        vmem((OWN, 128), f32),
        vmem((2, 1, 640), f32),
        vmem((16, 8, 128), f32),
        vmem((2, 8, 768), f32),
        vmem((SMALL_ROWS, 768), f32),
        vmem((9, SMALL_ROWS, 768), f32),
        vmem((3, 4, BLK, 768), bf16),
        vmem((3, 4, BLK, 768), bf16),
        vmem((3, 4, 80, 768), bf16),
        vmem((3, 4, 48, 768), bf16),
        vmem((3, 4, BLK, 768), bf16),
        vmem((2, 4, 2, 2 * Z_LAST, 768), bf16),
    ]
    scratch += [dma((3, 4))] * 24 + [dma((3, 8))] * 4
    scratch += [dma((4, 3))] * 4 + [dma((4,))] * 2 + [dma((6,))] * 2 + [dma((7,))] * 2
    whole = pl.BlockSpec(memory_space=vmem)
    return pl.pallas_call(
        layer_kernel,
        out_shape=(
            jax.ShapeDtypeStruct((OWN, 768), bf16),
            jax.ShapeDtypeStruct((OWN, 768), f32),
            jax.ShapeDtypeStruct((3, BLK, 192), f32),
            jax.ShapeDtypeStruct((192, BLK), f32),
            jax.ShapeDtypeStruct((BLK, 768), f32),
            jax.ShapeDtypeStruct((BLK, 768), f32),
            jax.ShapeDtypeStruct((4, SMALL_ROWS, 768), f32),
        ),
        in_specs=[whole] * len(operands),
        out_specs=(whole,) * 7,
        scratch_shapes=scratch,
        compiler_params=pltpu.CompilerParams(
            collective_id=0, has_side_effects=True, vmem_limit_bytes=63 * 2**20
        ),
    )(*operands)


def fits_kernel(mesh):
    return dict(mesh.shape) == {"wide": 8, "narrow": 4}


def fused_shards(
    tokens,
    type_ids,
    segment_ids,
    cotangent,
    type_table,
    type_first,
    type_second,
    norm_gains,
    gains_first,
    gains_second,
    biases,
    biases_first,
    biases_second,
    qkv_weight,
    qkv_first,
    qkv_second,
    out_weight,
    out_first,
    out_second,
    up_weight,
    up_first,
    up_second,
    up_bias,
    up_bias_first,
    up_bias_second,
    down_weight,
    down_first,
    down_second,
):
    wide, narrow = lax.axis_index("wide"), lax.axis_index("narrow")
    y, core = narrow // 2, narrow % 2
    activations, input_grad, grad_qkv, grad_out, grad_up, grad_down, small = run_layer(
        qkv_weight, out_weight, up_weight.T, down_weight, up_bias[None, :], tokens, type_ids[None, :],
        cotangent, segment_ids, type_table, norm_gains, biases, type_first, type_second, gains_first,
        gains_second, biases_first, biases_second,
    )
    grad_up = grad_up.T
    bias_part = lax.dynamic_slice_in_dim(small[3], UP_BIAS_ROW + 2 * core + y, 1)[0]
    grad_up_bias = jnp.concatenate(
        [
            lax.dynamic_slice_in_dim(bias_part, wide * Z_FIRST[UP], Z_FIRST[UP]),
            lax.dynamic_slice_in_dim(bias_part, LAST_AT + wide * Z_LAST, Z_LAST),
        ]
    )
    step_sizes = step_rates()
    updates = [
        small[0:3, TYPE_ROW : TYPE_ROW + 2],
        small[0:3, GAIN_ROW : GAIN_ROW + 2],
        small[0:3, BIAS_ROW : BIAS_ROW + 6],
        adam_update(qkv_weight, qkv_first, qkv_second, grad_qkv, step_sizes[3]),
        adam_update(out_weight, out_first, out_second, grad_out, step_sizes[4]),
        adam_update(up_weight, up_first, up_second, grad_up, step_sizes[5]),
        adam_update(up_bias, up_bias_first, up_bias_second, grad_up_bias, step_sizes[6]),
        adam_update(down_weight, down_first, down_second, grad_down, step_sizes[7]),
    ]
    updates = [value for update in updates for value in (update[0], update[1], update[2])]
    return (activations, input_grad, *updates)


def solution(mesh):
    placed = (
        P(("wide", "narrow"), None),
        P(("wide", "narrow")),
        P("wide", None),
        P(("wide", "narrow"), None),
        P(),
        P(),
        P(),
        P(),
        P(),
        P(),
        P(),
        P(),
        P(),
        P(None, "wide", "narrow"),
        P(None, "wide", "narrow"),
        P(None, "wide", "narrow"),
        P("narrow", "wide"),
        P("narrow", "wide"),
        P("narrow", "wide"),
        P(None, ("wide", "narrow")),
        P(None, ("wide", "narrow")),
        P(None, ("wide", "narrow")),
        P(("wide", "narrow")),
        P(("wide", "narrow")),
        P(("wide", "narrow")),
        P(("wide", "narrow"), None),
        P(("wide", "narrow"), None),
        P(("wide", "narrow"), None),
    )
    return jax.shard_map(
        fused_shards if fits_kernel(mesh) else shards,
        mesh=mesh,
        in_specs=placed,
        out_specs=(
            P(("wide", "narrow"), None),
            P(("wide", "narrow"), None),
            P(),
            P(),
            P(),
            P(),
            P(),
            P(),
            P(),
            P(),
            P(),
            P(None, "wide", "narrow"),
            P(None, "wide", "narrow"),
            P(None, "wide", "narrow"),
            P("narrow", "wide"),
            P("narrow", "wide"),
            P("narrow", "wide"),
            P(None, ("wide", "narrow")),
            P(None, ("wide", "narrow")),
            P(None, ("wide", "narrow")),
            P(("wide", "narrow")),
            P(("wide", "narrow")),
            P(("wide", "narrow")),
            P(("wide", "narrow"), None),
            P(("wide", "narrow"), None),
            P(("wide", "narrow"), None),
        ),
        check_vma=False,
    )
```

```python
import math

import jax
import jax.numpy as jnp
from jax import lax
from jax.experimental import pallas as pl
from jax.experimental.pallas import tpu as pltpu
from jax.sharding import PartitionSpec as P

D = 768
HD = 64
FF = 3072
STEP = 5


norm_eps = 1e-06
masked_score = -1e30


def in_blocks(value, dim, size):
    shape = value.shape
    tiles = value.reshape(*shape[:dim], size, shape[dim] // size, *shape[dim + 1 :])
    return jnp.moveaxis(tiles, dim, 0)


def sent_and_summed(value, axis, dim):
    tiles = in_blocks(value, dim, lax.axis_size(axis))
    arrived = lax.all_to_all(tiles, axis, split_axis=0, concat_axis=0, tiled=True)
    return arrived.astype(jnp.float32).sum(axis=0)


def norm_rows(values, gain, shift):
    center = jnp.mean(values, axis=-1, keepdims=True)
    spread = values - center
    variance = jnp.mean(spread * spread, axis=-1, keepdims=True)
    return spread * lax.rsqrt(variance + norm_eps) * gain + shift


def gelu_exact(values):
    return jax.nn.gelu(values, approximate=False)


def times_transposed(left_mat, right_mat):
    return lax.dot_general(
        left_mat, right_mat, (((1,), (1,)), ((), ())), preferred_element_type=jnp.float32
    )


def transposed_times(left_mat, right_mat):
    return lax.dot_general(
        left_mat, right_mat, (((0,), (0,)), ((), ())), preferred_element_type=jnp.float32
    )


def adam_update(weight_in, moment_one, moment_two, gradient, step_rate):
    moment_one = 0.5 * moment_one + 0.5 * gradient
    moment_two = 0.5 * moment_two + 0.5 * gradient * gradient
    correction = 1.0 - 0.5**STEP
    direction = moment_one / correction / (jnp.sqrt(moment_two / correction) + 1e-08)
    return (weight_in - step_rate * (direction + 0.01 * weight_in), moment_one, moment_two)


def step_rates():
    return (0.5, 0.4, 0.4, D ** (-0.5), 4.0 * D ** (-0.5), D ** (-0.5), 0.4, FF ** (-0.5))


def group_rows(values):
    return lax.all_gather(values, "narrow", axis=0, tiled=True)


def group_sums(term_fn, local_rows):
    return lax.psum_scatter(
        term_fn(jnp.int32(0), lax.axis_size("narrow") * local_rows).astype(jnp.bfloat16),
        "narrow",
        scatter_dimension=0,
        tiled=True,
    ).astype(jnp.float32)


def masked_scores(queries, key_rows, segment):
    raw_scores = jnp.einsum(
        "qhd,khd->hqk", queries, key_rows, preferred_element_type=jnp.float32
    ) * HD ** (-0.5)
    same_doc = segment[:, None] == segment[None, :]
    return jnp.where(same_doc[None, :, :], raw_scores, masked_score)


def pack_forward(pack_item):
    queries, key_rows, values, segment = pack_item
    scores = masked_scores(queries, key_rows, segment)
    highest = jnp.max(scores, axis=-1, keepdims=True)
    exponentials = jnp.exp(scores - highest)
    totals = jnp.sum(exponentials, axis=-1, keepdims=True)
    weights = exponentials / totals
    attended = jnp.einsum(
        "hqk,khd->qhd", weights.astype(jnp.bfloat16), values, preferred_element_type=jnp.float32
    )
    return (attended.astype(jnp.bfloat16), (highest + jnp.log(totals))[:, :, 0])


def pack_backward(pack_item):
    queries, key_rows, values, segment, log_totals, grad_attended = pack_item
    scores = masked_scores(queries, key_rows, segment)
    weights = jnp.exp(scores - log_totals[:, :, None])
    grad_values = jnp.einsum(
        "hqk,qhd->khd",
        weights.astype(jnp.bfloat16),
        grad_attended,
        preferred_element_type=jnp.float32,
    )
    grad_weights = jnp.einsum(
        "qhd,khd->hqk", grad_attended, values, preferred_element_type=jnp.float32
    )
    center = jnp.sum(weights * grad_weights, axis=-1, keepdims=True)
    grad_scores = (weights * (grad_weights - center)).astype(jnp.bfloat16)
    grad_queries = jnp.einsum(
        "hqk,khd->qhd", grad_scores, key_rows, preferred_element_type=jnp.float32
    ) * HD ** (-0.5)
    grad_keys = jnp.einsum(
        "hqk,qhd->khd", grad_scores, queries, preferred_element_type=jnp.float32
    ) * HD ** (-0.5)
    return (
        grad_queries.astype(jnp.bfloat16),
        grad_keys.astype(jnp.bfloat16),
        grad_values.astype(jnp.bfloat16),
    )


def shards(
    tokens,
    type_ids,
    segment_ids,
    cotangent,
    type_table,
    type_first,
    type_second,
    norm_gains,
    gains_first,
    gains_second,
    biases,
    biases_first,
    biases_second,
    qkv_weight,
    qkv_first,
    qkv_second,
    out_weight,
    out_first,
    out_second,
    up_weight,
    up_first,
    up_second,
    up_bias,
    up_bias_first,
    up_bias_second,
    down_weight,
    down_first,
    down_second,
):
    local_rows = tokens.shape[0]
    model_width = tokens.shape[1]
    head_cols = qkv_weight.shape[2]
    heads_here = head_cols // HD
    pack_count = segment_ids.shape[0]
    pack_rows = segment_ids.shape[1]
    group_count = pack_count * pack_rows
    narrow_index = lax.axis_index("narrow")
    qkv_low = qkv_weight.astype(jnp.bfloat16)
    out_low = out_weight.astype(jnp.bfloat16)
    up_low = up_weight.astype(jnp.bfloat16)
    up_bias_low = up_bias.astype(jnp.bfloat16)
    down_low = down_weight.astype(jnp.bfloat16)
    qkv_full, out_rows = (
        lax.all_gather(qkv_low, "wide", axis=1, tiled=True),
        lax.all_gather(out_low, "wide", axis=1, tiled=True),
    )
    up_cols, up_bias_cols, down_rows = (
        lax.all_gather(up_low, ("wide", "narrow"), axis=1, tiled=True),
        lax.all_gather(up_bias_low, ("wide", "narrow"), axis=0, tiled=True),
        lax.all_gather(down_low, ("wide", "narrow"), axis=0, tiled=True),
    )
    is_image = (type_ids == 1)[:, None]
    embedded = tokens.astype(jnp.float32) + jnp.where(
        is_image, type_table[1][None, :], type_table[0][None, :]
    )
    normed1_full, norm1_pull = jax.vjp(norm_rows, embedded, norm_gains[0], biases[0])
    normed1 = normed1_full.astype(jnp.bfloat16)
    group_normed = group_rows(normed1)
    head_offset = narrow_index * head_cols
    bias_query = lax.dynamic_slice_in_dim(biases[1], head_offset, head_cols)
    bias_value = lax.dynamic_slice_in_dim(biases[2], head_offset, head_cols)
    bias_stack = jnp.stack([bias_query, jnp.zeros_like(bias_query), bias_value])
    projected = jnp.einsum(
        "rd,sde->sre", group_normed, qkv_full, preferred_element_type=jnp.float32
    )
    qkv_rows = (projected + bias_stack[:, None, :]).astype(jnp.bfloat16)
    qkv_packs = qkv_rows.reshape(3, pack_count, pack_rows, heads_here, HD)
    attended, log_totals = lax.map(
        pack_forward, (qkv_packs[0], qkv_packs[1], qkv_packs[2], segment_ids)
    )
    attended = attended.reshape(group_count, head_cols)

    def out_term(first_row, row_span):
        return jnp.dot(attended, out_rows, preferred_element_type=jnp.float32)

    attn_proj = group_sums(out_term, local_rows)
    hidden1 = embedded + attn_proj + biases[3]
    normed2_full, norm2_pull = jax.vjp(norm_rows, hidden1, norm_gains[1], biases[4])
    normed2 = normed2_full.astype(jnp.bfloat16)
    mlp_input, mlp_back = (normed2, cotangent)
    pre_act = jnp.dot(mlp_input, up_cols, preferred_element_type=jnp.float32) + up_bias_cols.astype(
        jnp.float32
    )
    activated, gelu_pull = jax.vjp(gelu_exact, pre_act)
    act_low = activated.astype(jnp.bfloat16)
    mlp_out = jnp.dot(act_low, down_rows, preferred_element_type=jnp.float32)
    activations = (hidden1 + mlp_out + biases[5]).astype(jnp.bfloat16)
    grad_act = times_transposed(mlp_back, down_rows)
    (grad_pre,) = gelu_pull(grad_act)
    grad_pre_low = grad_pre.astype(jnp.bfloat16)
    grad_down = transposed_times(act_low, mlp_back)
    grad_up = transposed_times(mlp_input, grad_pre_low)
    grad_up_bias = jnp.sum(grad_pre_low.astype(jnp.float32), axis=0)
    grad_normed2 = times_transposed(grad_pre_low, up_cols)
    grad_hidden_part, grad_gain2, grad_shift2 = norm2_pull(grad_normed2)
    cotangent_full = cotangent.astype(jnp.float32)
    grad_hidden = cotangent_full + grad_hidden_part
    grad_hidden_low = grad_hidden.astype(jnp.bfloat16)
    group_back = group_rows(grad_hidden_low)
    grad_attended = times_transposed(group_back, out_rows).astype(jnp.bfloat16)
    grad_out_weight = transposed_times(attended, group_back)
    back_packs = grad_attended.reshape(pack_count, pack_rows, heads_here, HD)
    grad_queries, grad_keys, grad_values = lax.map(
        pack_backward,
        (qkv_packs[0], qkv_packs[1], qkv_packs[2], segment_ids, log_totals, back_packs),
    )
    grad_qkv_rows = jnp.stack([grad_queries, grad_keys, grad_values]).reshape(
        3, group_count, head_cols
    )
    grad_qkv_weight = jnp.einsum(
        "rd,sre->sde", group_normed, grad_qkv_rows, preferred_element_type=jnp.float32
    )
    head_sums = jnp.sum(grad_qkv_rows.astype(jnp.float32), axis=1)

    def in_term(first_row, row_span):
        return jnp.einsum(
            "sre,sde->rd", grad_qkv_rows, qkv_full, preferred_element_type=jnp.float32
        )

    grad_normed1 = group_sums(in_term, local_rows)
    grad_embed_part, grad_gain1, grad_shift1 = norm1_pull(grad_normed1)
    input_grad = grad_hidden + grad_embed_part
    zero_row = jnp.zeros((model_width,), jnp.float32)
    query_sums = lax.dynamic_update_slice_in_dim(zero_row, head_sums[0], head_offset, 0)
    value_sums = lax.dynamic_update_slice_in_dim(zero_row, head_sums[2], head_offset, 0)
    gain_part = jnp.stack([grad_gain1, grad_gain2])
    shift_part = jnp.stack(
        [
            grad_shift1,
            query_sums,
            value_sums,
            jnp.sum(grad_hidden, axis=0),
            grad_shift2,
            jnp.sum(cotangent_full, axis=0),
        ]
    )
    type_part = jnp.stack(
        [
            jnp.sum(jnp.where(is_image, 0.0, input_grad), axis=0),
            jnp.sum(jnp.where(is_image, input_grad, 0.0), axis=0),
        ]
    )
    grad_gains, grad_biases, grad_types = lax.psum(
        (gain_part, shift_part, type_part), ("wide", "narrow")
    )
    owned_qkv, owned_out = (
        sent_and_summed(grad_qkv_weight.astype(jnp.bfloat16), "wide", 1),
        sent_and_summed(grad_out_weight.astype(jnp.bfloat16), "wide", 1),
    )
    owned_up, owned_up_bias, owned_down = (
        lax.psum_scatter(grad_up, ("wide", "narrow"), scatter_dimension=1, tiled=True),
        lax.psum_scatter(grad_up_bias, ("wide", "narrow"), scatter_dimension=0, tiled=True),
        lax.psum_scatter(grad_down, ("wide", "narrow"), scatter_dimension=0, tiled=True),
    )
    step_sizes = step_rates()
    new_type = adam_update(type_table, type_first, type_second, grad_types, step_sizes[0])
    new_gains = adam_update(norm_gains, gains_first, gains_second, grad_gains, step_sizes[1])
    new_biases = adam_update(biases, biases_first, biases_second, grad_biases, step_sizes[2])
    new_qkv = adam_update(qkv_weight, qkv_first, qkv_second, owned_qkv, step_sizes[3])
    new_out = adam_update(out_weight, out_first, out_second, owned_out, step_sizes[4])
    new_up = adam_update(up_weight, up_first, up_second, owned_up, step_sizes[5])
    new_up_bias = adam_update(up_bias, up_bias_first, up_bias_second, owned_up_bias, step_sizes[6])
    new_down = adam_update(down_weight, down_first, down_second, owned_down, step_sizes[7])
    return (
        activations,
        input_grad,
        new_type[0],
        new_type[1],
        new_type[2],
        new_gains[0],
        new_gains[1],
        new_gains[2],
        new_biases[0],
        new_biases[1],
        new_biases[2],
        new_qkv[0],
        new_qkv[1],
        new_qkv[2],
        new_out[0],
        new_out[1],
        new_out[2],
        new_up[0],
        new_up[1],
        new_up[2],
        new_up_bias[0],
        new_up_bias[1],
        new_up_bias[2],
        new_down[0],
        new_down[1],
        new_down[2],
    )


def dot_nn(left_mat, right_mat):
    return lax.dot_general(
        left_mat, right_mat, (((1,), (0,)), ((), ())), preferred_element_type=jnp.float32
    )


def dot_nt(left_mat, right_mat):
    return lax.dot_general(
        left_mat, right_mat, (((1,), (1,)), ((), ())), preferred_element_type=jnp.float32
    )


def dot_tn(left_mat, right_mat):
    return lax.dot_general(
        left_mat, right_mat, (((0,), (0,)), ((), ())), preferred_element_type=jnp.float32
    )


def rows_at(block, size):
    return pl.ds(pl.multiple_of(block * size, size), size)


def row_stats(values):
    center = jnp.mean(values, axis=-1, keepdims=True)
    spread = values - center
    variance = jnp.mean(spread * spread, axis=-1, keepdims=True)
    scale = lax.rsqrt(variance + norm_eps)
    return spread * scale, scale


def column_sums(values):
    return jnp.sum(values, axis=0, keepdims=True)


ROW = 128
OWN = 384
CHIP = 768
HALF_PACK = 256
PACK = 512
BLK = 96
ATTN, UP, DOWN = 0, 1, 2
Z_FIRST = (96, 80, 80)
Z_LAST = 16
LAST_AT = 640
GATHER_BY_Y = (32, 48, 32)
SCATTER_BY_Y = (48, 32, 16)
GAIN_ROW, BIAS_ROW, TYPE_ROW, UP_BIAS_ROW, SMALL_ROWS = 0, 2, 8, 10, 16


def layer_kernel(
    qkv_weight, out_weight, up_rows, down_rows, up_bias, tokens, type_ids, cotangent, segment_ids, type_table,
    gains, biases, type_first, type_second, gains_first, gains_second, biases_first, biases_second,
    act_out, input_grad, qkv_grad, out_grad, up_out, down_out, small_out,
    full, part, g_all, n1_all, n2_all, dh_all, qkv, att, dkv_far, probs, mask, act, slope, datt,
    key_acc, value_acc, embedded, hidden1, own_sum, attn_out, swap_send, swap_recv, type_cols, qkv_bias,
    bias_slots, bias_row, small, small_recv, rx, ry, rdx, rdy, rz, rl,
    gz_s, gz_r, gx_s, gx_r, gy_s, gy_r, gfx_s, gfx_r, gfy_s, gfy_r,
    sz_s, sz_r, sx_s, sx_r, sy_s, sy_r, sdx_s, sdx_r, sdy_s, sdy_r,
    gl_s, gl_r, sl_s, sl_r, glz_s, glz_r, slz_s, slz_r,
    spread_s, spread_r, swap_s, swap_r, far_s, far_r, bias_s, bias_r, small_s, small_r,
):
    f32, bf16 = jnp.float32, jnp.bfloat16
    wide = lax.axis_index("wide")
    narrow = lax.axis_index("narrow")
    z, x = wide // 2, wide % 2
    y, core = narrow // 2, narrow % 2
    z_of = [z, z + 1 - 2 * (z % 2), (z + 2) % 4, 3 - z]
    sibling = (wide, y * 2 + (1 - core))
    x_side = (z * 2 + (1 - x), narrow)
    y_side = (wide, (1 - y) * 2 + core)
    z_side = [None] + [(z_of[j] * 2 + x, narrow) for j in (1, 2, 3)]

    def copy(src, dst, send, recv, to):
        return pltpu.make_async_remote_copy(
            src_ref=src, dst_ref=dst, send_sem=send, recv_sem=recv, device_id=to,
            device_id_type=pl.DeviceIdType.MESH,
        )

    pending = []
    pending_if = []
    totals = (attn_out, up_out, down_out)

    def start(*args):
        one = copy(*args)
        one.start()
        pending.append(one)
        return one

    barrier = pltpu.get_barrier_semaphore()
    for to in (sibling, x_side, y_side, z_side[1], z_side[2], z_side[3]):
        pl.semaphore_signal(barrier, inc=1, device_id=to, device_id_type=pl.DeviceIdType.MESH)
    pl.semaphore_wait(barrier, 6)

    inner = z * (3 - z) == 2
    outer = z * (3 - z) == 0

    def start_if(which, *args):
        one = copy(*args)

        @pl.when(which)
        def _():
            one.start()

        pending_if.append((which, one))

    def slot(ref, kind, yy, zz, xx, first=0, size=None):
        rows = Z_FIRST[kind]
        row = pl.multiple_of((zz * 2 + xx) * rows + first, 16)
        return ref.at[kind, yy, pl.ds(row, rows if size is None else size)]

    def last(ref, kind, yy, zz, xx, first=0, size=Z_LAST):
        row = pl.multiple_of(LAST_AT + (zz * 2 + xx) * Z_LAST + first, 16)
        return ref.at[kind, yy, pl.ds(row, size)]

    def last_pair(ref, kind, yy, zz):
        return last(ref, kind, yy, zz, 0, 0, 2 * Z_LAST)

    def gather_z(kind):
        mine = slot(full, kind, y, z, x)
        for j in (1, 2):
            start(mine, mine, gz_s.at[kind, j], gz_r.at[kind, j], z_side[j])
        start_if(inner, mine, mine, gz_s.at[kind, 3], gz_r.at[kind, 3], z_side[3])

    def gather_on(kind, j):
        block = slot(full, kind, y, z_of[j], x)
        if j:
            copy(block, block, gz_s.at[kind, j], gz_r.at[kind, j], z_side[j]).wait_recv()
        if j == 2:
            start_if(inner, block, block, gz_s.at[kind, 0], gz_r.at[kind, 3], z_side[1])
        start(block, block, gx_s.at[kind, j], gx_r.at[kind, j], x_side)
        start(block, block, gy_s.at[kind, j], gy_r.at[kind, j], y_side)
        if kind != ATTN and j == 0:
            block = last(full, kind, y, z, x)
            start(block, block, gl_s.at[kind, 0], gl_r.at[kind, 0], x_side)
            start(block, block, gl_s.at[kind, 1], gl_r.at[kind, 1], y_side)

    def gather_far(kind, j):
        zz = z_of[j]
        by_y, by_x = GATHER_BY_Y[kind], Z_FIRST[kind] - GATHER_BY_Y[kind]
        block = slot(full, kind, y, zz, 1 - x)
        copy(block, block, gx_s.at[kind, j], gx_r.at[kind, j], x_side).wait_recv()
        half = slot(full, kind, y, zz, 1 - x, 0, by_y)
        start(half, half, gfy_s.at[kind, j], gfy_r.at[kind, j], y_side)
        block = slot(full, kind, 1 - y, zz, x)
        copy(block, block, gy_s.at[kind, j], gy_r.at[kind, j], y_side).wait_recv()
        half = slot(full, kind, 1 - y, zz, x, by_y, by_x)
        start(half, half, gfx_s.at[kind, j], gfx_r.at[kind, j], x_side)
        if kind != ATTN and j == 0:
            block = last(full, kind, y, z, 1 - x)
            copy(block, block, gl_s.at[kind, 0], gl_r.at[kind, 0], x_side).wait_recv()
            block = last(full, kind, 1 - y, z, x)
            copy(block, block, gl_s.at[kind, 1], gl_r.at[kind, 1], y_side).wait_recv()
            start(block, block, gl_s.at[kind, 2], gl_r.at[kind, 2], x_side)

    def gather_last(kind):
        block = last(full, kind, 1 - y, z, 1 - x)
        copy(block, block, gl_s.at[kind, 2], gl_r.at[kind, 2], x_side).wait_recv()
        for yy in (0, 1):
            pair = last_pair(full, kind, yy, z)
            for j in (1, 2):
                start(pair, pair, glz_s.at[kind, 2 * j + yy], glz_r.at[kind, 2 * j + yy], z_side[j])
            start_if(inner, pair, pair, glz_s.at[kind, 6 + yy], glz_r.at[kind, 6 + yy], z_side[3])

    def last_arrived(kind, j):
        for yy in (0, 1):
            pair = last_pair(full, kind, yy, z_of[j])
            copy(pair, pair, glz_s.at[kind, 2 * j + yy], glz_r.at[kind, 2 * j + yy], z_side[j]).wait_recv()

    def gather_relay(kind):
        last_arrived(kind, 2)
        for yy in (0, 1):
            pair = last_pair(full, kind, yy, z_of[2])
            start_if(inner, pair, pair, glz_s.at[kind, yy], glz_r.at[kind, 6 + yy], z_side[1])

    def gather_last_done(kind):
        last_arrived(kind, 1)
        last_arrived(kind, 3)

    def gather_done(kind):
        by_y, by_x = GATHER_BY_Y[kind], Z_FIRST[kind] - GATHER_BY_Y[kind]
        for j in range(4):
            half = slot(full, kind, 1 - y, z_of[j], 1 - x, 0, by_y)
            copy(half, half, gfy_s.at[kind, j], gfy_r.at[kind, j], y_side).wait_recv()
            half = slot(full, kind, 1 - y, z_of[j], 1 - x, by_y, by_x)
            copy(half, half, gfx_s.at[kind, j], gfx_r.at[kind, j], x_side).wait_recv()

    def add_in(ref, arrived):
        ref[...] = (ref[...].astype(f32) + arrived[...].astype(f32)).astype(bf16)

    def scatter_last(kind):
        for yy in (0, 1):
            def target(j):
                return last_pair(part, kind, yy, z_of[j])

            def landing(j):
                return rl.at[kind - 1, j, yy]

            def sems(sent, landed):
                return slz_s.at[kind, 2 * sent + yy], slz_r.at[kind, 2 * landed + yy]

            start(target(1), landing(1), *sems(1, 1), z_side[1])
            start_if(outer, target(2), landing(2), *sems(2, 2), z_side[2])
            start_if(inner, target(3), landing(3), *sems(3, 3), z_side[3])
            start_if(outer, target(3), landing(0), *sems(3, 0), z_side[1])

    def scatter_relay(kind):
        @pl.when(inner)
        def _():
            for yy in (0, 1):
                here = last_pair(part, kind, yy, z_of[2])
                came = rl.at[kind - 1, 0, yy]
                copy(here, came, slz_s.at[kind, yy], slz_r.at[kind, yy], z_side[1]).wait_recv()
                add_in(here, came)

        for yy in (0, 1):
            here = last_pair(part, kind, yy, z_of[2])
            start_if(
                inner, here, rl.at[kind - 1, 2, yy], slz_s.at[kind, 4 + yy], slz_r.at[kind, 4 + yy], z_side[2]
            )

    def scatter_last_add(kind):
        for yy in (0, 1):
            here = last_pair(part, kind, yy, z)
            for j in (1, 2):
                came = rl.at[kind - 1, j, yy]
                copy(here, came, slz_s.at[kind, 2 * j + yy], slz_r.at[kind, 2 * j + yy], z_side[j]).wait_recv()
            total = here[...].astype(f32) + rl[kind - 1, 1, yy].astype(f32) + rl[kind - 1, 2, yy].astype(f32)
            here[...] = total.astype(bf16)

        @pl.when(inner)
        def _():
            for yy in (0, 1):
                here = last_pair(part, kind, yy, z)
                came = rl.at[kind - 1, 3, yy]
                copy(here, came, slz_s.at[kind, 6 + yy], slz_r.at[kind, 6 + yy], z_side[3]).wait_recv()
                add_in(here, came)

    def scatter_far(kind, j):
        by_y, by_x = SCATTER_BY_Y[kind], Z_FIRST[kind] - SCATTER_BY_Y[kind]
        half = slot(part, kind, 1 - y, z_of[j], 1 - x, 0, by_y)
        start(half, rdy.at[kind, j, pl.ds(0, by_y)], sdy_s.at[kind, j], sdy_r.at[kind, j], y_side)
        half = slot(part, kind, 1 - y, z_of[j], 1 - x, by_y, by_x)
        start(half, rdx.at[kind, j, pl.ds(0, by_x)], sdx_s.at[kind, j], sdx_r.at[kind, j], x_side)
        if kind != ATTN and j == 0:
            block = last(part, kind, 1 - y, z, 1 - x)
            start(block, rdx.at[kind, 0, pl.ds(64, Z_LAST)], sl_s.at[kind, 1], sl_r.at[kind, 1], x_side)

    def scatter_near(kind, j):
        zz = z_of[j]
        rows = Z_FIRST[kind]
        by_y, by_x = SCATTER_BY_Y[kind], rows - SCATTER_BY_Y[kind]
        half = slot(part, kind, y, zz, 1 - x, 0, by_y)
        came = rdy.at[kind, j, pl.ds(0, by_y)]
        copy(half, came, sdy_s.at[kind, j], sdy_r.at[kind, j], y_side).wait_recv()
        add_in(half, came)
        land = pl.ds(0, rows)
        start(slot(part, kind, y, zz, 1 - x), rx.at[kind, j, land], sx_s.at[kind, j], sx_r.at[kind, j], x_side)
        half = slot(part, kind, 1 - y, zz, x, by_y, by_x)
        came = rdx.at[kind, j, pl.ds(0, by_x)]
        copy(half, came, sdx_s.at[kind, j], sdx_r.at[kind, j], x_side).wait_recv()
        add_in(half, came)
        start(slot(part, kind, 1 - y, zz, x), ry.at[kind, j, land], sy_s.at[kind, j], sy_r.at[kind, j], y_side)
        if kind != ATTN and j == 0:
            land = pl.ds(rows, Z_LAST)
            start(last(part, kind, y, z, 1 - x), rx.at[kind, 0, land], sl_s.at[kind, 2], sl_r.at[kind, 2], x_side)
            block = last(part, kind, 1 - y, z, x)
            came = rdx.at[kind, 0, pl.ds(64, Z_LAST)]
            copy(block, came, sl_s.at[kind, 1], sl_r.at[kind, 1], x_side).wait_recv()
            add_in(block, came)
            start(last(part, kind, 1 - y, z, x), ry.at[kind, 0, land], sl_s.at[kind, 3], sl_r.at[kind, 3], y_side)

    def scatter_z(kind, j):
        land = pl.ds(0, Z_FIRST[kind])
        block = slot(part, kind, y, z_of[j], x)
        copy(block, rx.at[kind, j, land], sx_s.at[kind, j], sx_r.at[kind, j], x_side).wait_recv()
        copy(block, ry.at[kind, j, land], sy_s.at[kind, j], sy_r.at[kind, j], y_side).wait_recv()
        total = block[...].astype(f32) + rx[kind, j, land].astype(f32) + ry[kind, j, land].astype(f32)
        if j == 0:
            totals[kind][land] = total
            if kind != ATTN:
                land = pl.ds(Z_FIRST[kind], Z_LAST)
                block = last(part, kind, y, z, x)
                copy(block, rx.at[kind, 0, land], sl_s.at[kind, 2], sl_r.at[kind, 2], x_side).wait_recv()
                copy(block, ry.at[kind, 0, land], sl_s.at[kind, 3], sl_r.at[kind, 3], y_side).wait_recv()
                totals[kind][land] = (
                    block[...].astype(f32) + rx[kind, 0, land].astype(f32) + ry[kind, 0, land].astype(f32)
                )
            return
        block[...] = total.astype(bf16)
        came = rz.at[kind, j, land]
        if j == 1:
            start(block, came, sz_s.at[kind, j], sz_r.at[kind, j], z_side[j])
        elif j == 2:
            relayed = rz.at[kind, 0, land]

            @pl.when(inner)
            def _():
                copy(block, relayed, sz_s.at[kind, 0], sz_r.at[kind, 0], z_side[1]).wait_recv()
                add_in(block, relayed)

            start(block, came, sz_s.at[kind, j], sz_r.at[kind, j], z_side[j])
        else:
            start_if(inner, block, came, sz_s.at[kind, 3], sz_r.at[kind, 3], z_side[3])
            start_if(outer, block, rz.at[kind, 0, land], sz_s.at[kind, 3], sz_r.at[kind, 0], z_side[1])

    def scatter_done(kind):
        land = pl.ds(0, Z_FIRST[kind])
        for j in (1, 2):
            came = rz.at[kind, j, land]
            copy(came, came, sz_s.at[kind, j], sz_r.at[kind, j], z_side[j]).wait_recv()
        totals[kind][land] += rz[kind, 1, land].astype(f32) + rz[kind, 2, land].astype(f32)

        @pl.when(inner)
        def _():
            came = rz.at[kind, 3, land]
            copy(came, came, sz_s.at[kind, 3], sz_r.at[kind, 3], z_side[3]).wait_recv()
            totals[kind][land] += came[...].astype(f32)

    def place(which, block):
        return rows_at((3 * which + block + 4 * y) % 6, ROW)

    def hand_over(ref, use, block):
        here = ref.at[place(core, block)]
        return copy(here, here, spread_s.at[use, block], spread_r.at[use, block], sibling)

    def spread_done(ref, use):
        for block in range(3):
            there = ref.at[place(1 - core, block)]
            copy(there, there, spread_s.at[use, block], spread_r.at[use, block], sibling).wait_recv()
            pending.append(hand_over(ref, use, block))

    def swap_sums(use, term):
        def for_sibling(block, carry):
            rows = rows_at(block, ROW)
            swap_send[rows] = term(place(1 - core, block)).astype(bf16)
            copy(
                swap_send.at[rows], swap_recv.at[use, rows], swap_s.at[use, block],
                swap_r.at[use, block], sibling,
            ).start()
            return carry

        def for_self(block, carry):
            own_sum[rows_at(block, ROW)] = term(place(core, block))
            return carry

        lax.fori_loop(0, 3, for_sibling, 0)
        lax.fori_loop(0, 3, for_self, 0)

    def swap_done(use):
        for block in range(3):
            rows = pl.ds(block * ROW, ROW)
            one = copy(
                swap_send.at[rows], swap_recv.at[use, rows], swap_s.at[use, block],
                swap_r.at[use, block], sibling,
            )
            one.wait_recv()
            one.wait_send()

    def swapped(use, rows):
        return own_sum[rows] + swap_recv[use, rows].astype(f32)

    def own_attn():
        slot(full, ATTN, y, z, x)[...] = jnp.concatenate(
            [qkv_weight[1], qkv_weight[2], qkv_weight[0], out_weight[...].T], axis=1
        ).astype(bf16)

    def own_rest():
        for kind, rows in ((UP, up_rows), (DOWN, down_rows)):
            early = Z_FIRST[kind]
            slot(full, kind, y, z, x)[...] = rows[0:early].astype(bf16)
            last(full, kind, y, z, x)[...] = rows[early:BLK].astype(bf16)

    def as_column(row):
        return jnp.broadcast_to(row, (ROW, ROW)).T

    def column_types():
        types = type_ids[...].astype(f32)
        for block in range(3):
            rows = pl.ds(block * ROW, ROW)
            type_cols[rows] = as_column(types[:, block * ROW : block * ROW + ROW])

    def give_cotangent():
        def body(block, carry):
            g_all[place(core, block)] = cotangent[rows_at(block, ROW)]
            hand_over(g_all, 0, block).start()
            return carry

        lax.fori_loop(0, 3, body, 0)

    def first_norm():
        def body(block, carry):
            rows = rows_at(block, ROW)
            values = tokens[rows].astype(f32) + jnp.where(
                type_cols[rows, 0:1] > 0, type_table[1:2, :], type_table[0:1, :]
            )
            embedded[rows] = values
            xhat, _ = row_stats(values)
            n1_all[place(core, block)] = (xhat * gains[0:1, :] + biases[0:1, :]).astype(bf16)
            hand_over(n1_all, 1, block).start()
            return carry

        lax.fori_loop(0, 3, body, 0)

    half_rows = pl.ds(PACK, HALF_PACK)
    far_rows = pl.ds(CHIP, HALF_PACK)
    over_y = copy(n1_all.at[half_rows], n1_all.at[far_rows], far_s.at[0], far_r.at[0], y_side)
    relay = copy(n1_all.at[far_rows], n1_all.at[far_rows], far_s.at[1], far_r.at[1], sibling)
    holds_half = (core + y) == 1

    def half_over():
        @pl.when(holds_half)
        def _():
            over_y.start()

    def half_relay():
        @pl.when(jnp.logical_not(holds_half))
        def _():
            over_y.wait_recv()
            relay.start()

    def half_arrived():
        @pl.when(holds_half)
        def _():
            relay.wait_recv()

    bias_first = (y * 2 + x) * 4

    def bias_hop(first, size, index, to):
        ref = bias_slots.at[pl.ds(first, size)]
        return start(ref, ref, bias_s.at[index], bias_r.at[index], to)

    def bias_wait(first, size, index, to):
        ref = bias_slots.at[pl.ds(first, size)]
        copy(ref, ref, bias_s.at[index], bias_r.at[index], to).wait_recv()

    def bias_along_z():
        bias_slots[bias_first + z] = jnp.broadcast_to(
            jnp.concatenate(
                [up_bias[...].astype(bf16).astype(f32), jnp.zeros((1, 128 - BLK), f32)], axis=1
            ),
            (8, 128),
        )
        for j in (1, 2, 3):
            bias_hop(bias_first + z, 1, j, z_side[j])

    def bias_along_x():
        for j in (1, 2, 3):
            bias_wait(bias_first + z_of[j], 1, j, z_side[j])
        bias_hop(bias_first, 4, 4, x_side)

    def bias_along_y():
        bias_wait((y * 2 + 1 - x) * 4, 4, 4, x_side)
        bias_hop(y * 8, 8, 5, y_side)

    def bias_as_rows():
        bias_wait((1 - y) * 8, 8, 5, y_side)
        for yy in (0, 1):
            for xx in (0, 1):
                for zz in range(4):
                    which, block = zz * 2 + xx, (yy * 2 + xx) * 4 + zz
                    early = Z_FIRST[UP]
                    first = which * early
                    bias_row[yy, :, first : first + early] = bias_slots[block, :, 0:early]
                    first = LAST_AT + which * Z_LAST
                    bias_row[yy, :, first : first + Z_LAST] = bias_slots[block, :, early:BLK]

    def masks():
        documents = segment_ids[...].astype(f32)
        early = y == 0
        whole_doc = jnp.where(early, documents[0:1], documents[2:3])
        near_doc = jnp.where(early, documents[1:2, 0:256], documents[1:2, 256:512])
        far_doc = jnp.where(early, documents[1:2, 256:512], documents[1:2, 0:256])
        query_rows = (whole_doc[:, 0:256], whole_doc[:, 256:512], near_doc)
        key_rows_of = (whole_doc, jnp.concatenate([near_doc, far_doc], axis=1))
        for side, tiles in ((0, (0, 1)), (1, (2,))):
            for chunk in range(4):
                keys = slice(chunk * ROW, chunk * ROW + ROW)
                column = as_column(key_rows_of[side][:, keys])[:, 0:1]
                for tile in tiles:
                    mask[tile, keys] = jnp.where(
                        column == query_rows[tile], 0.0, masked_score
                    ).astype(bf16)

    def zeros_and_biases():
        small[...] = jnp.zeros_like(small)
        for yy in (0, 1):
            att[yy, :, 0:HD] = jnp.zeros((CHIP, HD), bf16)
            qkv[yy, :, 576:768] = jnp.zeros((CHIP + HALF_PACK, 192), bf16)
            first = yy * 384
            chosen = [
                jnp.where(
                    core == 0,
                    biases[i : i + 1, first : first + 192],
                    biases[i : i + 1, first + 192 : first + 384],
                )
                for i in (2, 1)
            ]
            zeros = jnp.zeros((1, 192), f32)
            qkv_bias[yy] = jnp.concatenate([zeros] + chosen + [zeros[:, 0:64]], axis=1)

    lane = lax.broadcasted_iota(jnp.int32, (1, 640), 1)
    shrink = jnp.where(lane >= 384, HD ** (-0.5), 1.0).astype(f32)

    def project(yy):
        def body(tile, carry):
            rows = rows_at(tile, 256)
            found = dot_nn(n1_all[rows], full[ATTN, yy, :, 0:640]) + qkv_bias[yy]
            qkv[yy, rows, 0:576] = (found * shrink)[:, 0:576].astype(bf16)
            return carry

        lax.fori_loop(0, 4, body, 0)

    def head_rows(yy, head, rows, keys):
        queries = qkv[yy, rows, 384 + HD * head : 448 + HD * head]
        key_rows = qkv[yy, keys, HD * head : HD * head + HD]
        values = qkv[yy, keys, 192 + HD * head : 256 + HD * head]
        return queries, key_rows, values

    def attend(yy, head):
        def body(tile, carry):
            rows = rows_at(tile, 256)
            queries, key_rows, values = head_rows(yy, head, rows, rows_at(tile // 2, PACK))
            scores = dot_nt(key_rows, queries) + mask[tile].astype(f32)
            exponentials = jnp.exp(scores - jnp.max(scores, axis=0, keepdims=True))
            totals = jnp.sum(exponentials, axis=0, keepdims=True)
            weights = (exponentials * (1.0 / totals)).astype(bf16)
            probs[yy * 3 + head, tile] = weights
            att[yy, rows, HD + HD * head : 2 * HD + HD * head] = dot_tn(values, weights).T.astype(bf16)
            return carry

        lax.fori_loop(0, 3, body, 0)

    def out_term(rows):
        return dot_nt(att[0, rows], full[ATTN, 0, :, 512:768]) + dot_nt(
            att[1, rows], full[ATTN, 1, :, 512:768]
        )

    def second_norm():
        def body(block, carry):
            rows = rows_at(block, ROW)
            values = embedded[rows] + swapped(0, rows) + biases[3:4, :]
            hidden1[rows] = values
            xhat, _ = row_stats(values)
            n2_all[place(core, block)] = (xhat * gains[1:2, :] + biases[4:5, :]).astype(bf16)
            hand_over(n2_all, 2, block).start()
            return carry

        lax.fori_loop(0, 3, body, 0)

    def up_chunk(yy, chunk):
        lanes = slice(chunk * 256, chunk * 256 + 256)
        shift = bias_row[yy, 0:1, lanes]

        def body(tile, carry):
            rows = rows_at(tile, 256)
            before = dot_nt(n2_all[rows], full[UP, yy, lanes]) + shift
            normal = 0.5 + 0.5 * lax.erf(before * (0.5**0.5))
            act[yy, rows, lanes] = (before * normal).astype(bf16)
            bell = jnp.exp(-0.5 * before * before) * ((2.0 * math.pi) ** -0.5)
            slope[yy, rows, lanes] = (normal + before * bell).astype(bf16)
            return carry

        lax.fori_loop(0, 3, body, 0)

    def down_grad(yy):
        for chunk in range(3):
            lanes = slice(chunk * 256, chunk * 256 + 256)
            part[DOWN, yy, lanes] = dot_tn(act[yy, :, lanes], g_all[...]).astype(bf16)

    def du_chunk(yy, chunk):
        lanes = slice(chunk * 256, chunk * 256 + 256)

        def body(tile, carry):
            rows = rows_at(tile, 256)
            grad = dot_nt(g_all[rows], full[DOWN, yy, lanes]) * slope[yy, rows, lanes].astype(f32)
            grad = grad.astype(bf16)
            slope[yy, rows, lanes] = grad
            return carry + column_sums(grad.astype(f32))

        total = lax.fori_loop(0, 3, body, jnp.zeros((1, 256), f32))
        for cc in (0, 1):
            for side in (0, 1):
                row = UP_BIAS_ROW + 2 * cc + side
                small[row : row + 1, lanes] = jnp.where(
                    jnp.logical_and(core == cc, yy == side), total, small[row : row + 1, lanes]
                )

    def mlp_term(rows):
        return dot_nn(act[0, rows], full[DOWN, 0]) + dot_nn(act[1, rows], full[DOWN, 1])

    def du_term(rows):
        return dot_nn(slope[0, rows], full[UP, 0]) + dot_nn(slope[1, rows], full[UP, 1])

    def up_grad(yy):
        for chunk in range(3):
            lanes = slice(chunk * 256, chunk * 256 + 256)
            part[UP, yy, lanes] = dot_tn(slope[yy, :, lanes], n2_all[...]).astype(bf16)

    def second_norm_back():
        def body(block, carry):
            rows = rows_at(block, ROW)
            grad = swapped(2, rows)
            xhat, scale = row_stats(hidden1[rows])
            scaled = grad * gains[1:2, :]
            back = (
                scaled
                - jnp.mean(scaled, axis=-1, keepdims=True)
                - xhat * jnp.mean(scaled * xhat, axis=-1, keepdims=True)
            ) * scale
            given = cotangent[rows].astype(f32)
            total = given + back
            input_grad[rows] = total
            dh_all[place(core, block)] = total.astype(bf16)
            hand_over(dh_all, 3, block).start()
            small[1:2, :] += column_sums(grad * xhat)
            small[6:7, :] += column_sums(grad)
            small[5:6, :] += column_sums(total)
            small[7:8, :] += column_sums(given)
            return carry

        lax.fori_loop(0, 3, body, 0)

    def project_back(yy):
        def body(tile, carry):
            rows = rows_at(tile, 256)
            datt[yy, rows] = dot_nn(dh_all[rows], full[ATTN, yy, :, 512:768]).astype(bf16)
            return carry

        lax.fori_loop(0, 3, body, 0)

    def attend_back(yy, head):
        key_acc[...] = jnp.zeros_like(key_acc)
        value_acc[...] = jnp.zeros_like(value_acc)

        def body(tile, carry):
            rows = rows_at(tile, 256)
            keys = rows_at(tile // 2, PACK)
            queries, key_rows, values = head_rows(yy, head, rows, keys)
            grad = datt[yy, rows, HD + HD * head : 2 * HD + HD * head]
            weights = probs[yy * 3 + head, tile]
            weights_full = weights.astype(f32)
            back = dot_nt(values, grad) * weights_full
            center = jnp.sum(back, axis=0, keepdims=True)
            grad_scores = (back - weights_full * center).astype(bf16)
            grad_queries = dot_tn(key_rows, grad_scores) * HD ** (-0.5)
            value_acc[keys] += dot_nn(weights, grad)
            key_acc[keys] += dot_nn(grad_scores, queries)
            qkv[yy, rows, 384 + HD * head : 448 + HD * head] = grad_queries.T.astype(bf16)
            return carry

        lax.fori_loop(0, 3, body, 0, unroll=True)
        qkv[yy, :, HD * head : HD * head + HD] = key_acc[...].astype(bf16)
        qkv[yy, :, 192 + HD * head : 256 + HD * head] = value_acc[...].astype(bf16)

    def send_far(yy):
        start(qkv.at[yy, far_rows, 0:384], dkv_far.at[yy], far_s.at[2 + yy], far_r.at[2 + yy], y_side)

    def add_far(yy):
        copy(
            qkv.at[yy, far_rows, 0:384], dkv_far.at[yy], far_s.at[2 + yy], far_r.at[2 + yy], y_side
        ).wait_recv()
        qkv[yy, half_rows, 0:384] = (
            qkv[yy, half_rows, 0:384].astype(f32) + dkv_far[yy].astype(f32)
        ).astype(bf16)

    def finish_act():
        def body(block, carry):
            rows = rows_at(block, ROW)
            act_out[rows] = (hidden1[rows] + swapped(1, rows) + biases[5:6, :]).astype(bf16)
            return carry

        lax.fori_loop(0, 3, body, 0)

    def attn_grad(yy):
        for chunk in range(3):
            lanes = slice(chunk * 256, chunk * 256 + 256)
            n1_part = n1_all[0:CHIP, lanes]
            part[ATTN, yy, lanes, 0:512] = dot_tn(n1_part, qkv[yy, 0:CHIP, 0:512]).astype(bf16)
            part[ATTN, yy, lanes, 512:768] = (
                dot_tn(n1_part, qkv[yy, 0:CHIP, 512:768]) + dot_tn(dh_all[:, lanes], att[yy])
            ).astype(bf16)

    def in_term(rows):
        return dot_nt(qkv[0, rows], full[ATTN, 0]) + dot_nt(qkv[1, rows], full[ATTN, 1])

    def head_bias_sums():
        for yy in (0, 1):
            sums = column_sums(qkv[yy, 0:CHIP, 192:576].astype(f32))
            for cc in (0, 1):
                first = yy * 384 + cc * 192
                small[4:5, first : first + 192] = jnp.where(core == cc, sums[:, 0:192], 0.0)
                small[3:4, first : first + 192] = jnp.where(core == cc, sums[:, 192:384], 0.0)

    def first_norm_back():
        def body(block, carry):
            rows = rows_at(block, ROW)
            grad = swapped(3, rows)
            xhat, scale = row_stats(embedded[rows])
            scaled = grad * gains[0:1, :]
            back = (
                scaled
                - jnp.mean(scaled, axis=-1, keepdims=True)
                - xhat * jnp.mean(scaled * xhat, axis=-1, keepdims=True)
            ) * scale
            total = input_grad[rows] + back
            input_grad[rows] = total
            small[0:1, :] += column_sums(grad * xhat)
            small[2:3, :] += column_sums(grad)
            image = type_cols[rows, 0:1] > 0
            small[8:9, :] += column_sums(jnp.where(image, 0.0, total))
            small[9:10, :] += column_sums(jnp.where(image, total, 0.0))
            return carry

        lax.fori_loop(0, 3, body, 0)

    def small_core():
        start(small, small_recv.at[4], small_s.at[4], small_r.at[4], sibling)

    def small_x():
        copy(small, small_recv.at[4], small_s.at[4], small_r.at[4], sibling).wait_recv()
        small_recv[5] = small[...] + small_recv[4]
        start(small_recv.at[5], small_recv.at[6], small_s.at[5], small_r.at[5], x_side)

    def small_y():
        copy(small_recv.at[5], small_recv.at[6], small_s.at[5], small_r.at[5], x_side).wait_recv()
        small_recv[7] = small_recv[5] + small_recv[6]
        start(small_recv.at[7], small_recv.at[8], small_s.at[6], small_r.at[6], y_side)

    def small_z():
        copy(small_recv.at[7], small_recv.at[8], small_s.at[6], small_r.at[6], y_side).wait_recv()
        small_recv[z] = small_recv[7] + small_recv[8]
        for j in (1, 2, 3):
            start(small_recv.at[z], small_recv.at[z], small_s.at[j], small_r.at[j], z_side[j])

    def small_done():
        for j in (1, 2, 3):
            there = small_recv.at[z_of[j]]
            copy(there, there, small_s.at[j], small_r.at[j], z_side[j]).wait_recv()
        found = (small_recv[0] + small_recv[1]) + (small_recv[2] + small_recv[3])
        small_out[3] = found
        rates = step_rates()
        for first, kept, rate in (
            (GAIN_ROW, (gains, gains_first, gains_second), rates[1]),
            (BIAS_ROW, (biases, biases_first, biases_second), rates[2]),
            (TYPE_ROW, (type_table, type_first, type_second), rates[0]),
        ):
            rows = slice(first, first + kept[0].shape[0])
            updated = adam_update(*(ref[...] for ref in kept), found[rows], rate)
            for index, value in enumerate(updated):
                small_out[index, rows] = value

    def attn_out_rows():
        qkv_grad[0] = attn_out[:, 384:576]
        qkv_grad[1] = attn_out[:, 0:192]
        qkv_grad[2] = attn_out[:, 192:384]
        out_grad[...] = attn_out[:, 576:768].T

    own_attn()
    gather_on(ATTN, 0)
    own_rest()
    gather_z(ATTN)
    column_types()
    gather_on(UP, 0)
    first_norm()
    bias_along_z()
    masks()
    half_over()
    gather_far(UP, 0)
    gather_on(ATTN, 1)
    bias_along_x()
    gather_far(ATTN, 0)
    half_relay()
    spread_done(n1_all, 1)
    gather_on(ATTN, 2)
    gather_last(UP)
    give_cotangent()
    gather_z(UP)
    zeros_and_biases()
    gather_on(ATTN, 3)
    half_arrived()
    bias_along_y()
    gather_far(ATTN, 1)
    gather_far(ATTN, 2)
    gather_far(ATTN, 3)
    gather_on(DOWN, 0)
    gather_on(UP, 2)
    spread_done(g_all, 0)
    project(y)
    gather_on(UP, 1)
    gather_done(ATTN)
    project(1 - y)
    gather_z(DOWN)
    attend(y, 0)
    attend(y, 1)
    gather_far(DOWN, 0)
    attend(y, 2)
    gather_far(UP, 2)
    attend(1 - y, 0)
    gather_on(UP, 3)
    attend(1 - y, 1)
    gather_relay(UP)
    attend(1 - y, 2)
    gather_last(DOWN)
    gather_on(DOWN, 1)
    gather_far(UP, 1)
    gather_on(DOWN, 2)
    gather_last_done(UP)
    swap_sums(0, out_term)
    gather_far(UP, 3)
    swap_done(0)
    second_norm()
    bias_as_rows()
    gather_on(DOWN, 3)
    gather_far(DOWN, 1)
    spread_done(n2_all, 2)
    up_chunk(y, 0)
    up_chunk(y, 1)
    up_chunk(y, 2)
    gather_relay(DOWN)
    gather_far(DOWN, 2)
    gather_done(UP)
    up_chunk(1 - y, 0)
    up_chunk(1 - y, 1)
    gather_last_done(DOWN)
    up_chunk(1 - y, 2)
    gather_far(DOWN, 3)
    down_grad(1 - y)
    scatter_far(DOWN, 2)
    down_grad(y)
    scatter_far(DOWN, 1)
    du_chunk(y, 0)
    scatter_last(DOWN)
    du_chunk(y, 1)
    gather_done(DOWN)
    du_chunk(y, 2)
    du_chunk(1 - y, 0)
    du_chunk(1 - y, 1)
    du_chunk(1 - y, 2)
    scatter_far(DOWN, 3)
    scatter_near(DOWN, 1)
    up_grad(1 - y)
    scatter_far(UP, 2)
    scatter_near(DOWN, 2)
    scatter_far(UP, 3)
    scatter_far(UP, 1)
    swap_sums(2, du_term)
    scatter_relay(DOWN)
    scatter_near(DOWN, 3)
    swap_done(2)
    second_norm_back()
    up_grad(y)
    scatter_near(UP, 2)
    scatter_last_add(DOWN)
    spread_done(dh_all, 3)
    project_back(0)
    scatter_last(UP)
    project_back(1)
    attend_back(0, 0)
    scatter_near(UP, 3)
    attend_back(0, 1)
    attend_back(0, 2)
    send_far(0)
    attend_back(1, 0)
    attend_back(1, 1)
    attend_back(1, 2)
    send_far(1)
    scatter_z(DOWN, 3)
    scatter_near(UP, 1)
    scatter_far(DOWN, 0)
    scatter_z(UP, 3)
    swap_sums(1, mlp_term)
    scatter_z(DOWN, 2)
    swap_done(1)
    finish_act()
    add_far(1)
    add_far(0)
    attn_grad(1 - y)
    scatter_z(DOWN, 1)
    scatter_far(ATTN, 3)
    scatter_z(UP, 1)
    scatter_far(ATTN, 1)
    attn_grad(y)
    scatter_relay(UP)
    scatter_far(ATTN, 2)
    scatter_near(ATTN, 3)
    swap_sums(3, in_term)
    scatter_near(DOWN, 0)
    head_bias_sums()
    scatter_near(ATTN, 2)
    scatter_z(ATTN, 3)
    swap_done(3)
    scatter_z(UP, 2)
    scatter_near(ATTN, 1)
    scatter_z(DOWN, 0)
    scatter_last_add(UP)
    first_norm_back()
    small_core()
    scatter_z(ATTN, 2)
    small_x()
    scatter_done(DOWN)
    scatter_far(ATTN, 0)
    small_y()
    scatter_far(UP, 0)
    scatter_near(ATTN, 0)
    scatter_z(ATTN, 1)
    small_z()
    scatter_near(UP, 0)
    scatter_z(ATTN, 0)
    small_done()
    scatter_done(ATTN)
    attn_out_rows()
    scatter_z(UP, 0)
    scatter_done(UP)
    for one in pending:
        one.wait_send()
    for which, one in pending_if:
        @pl.when(which)
        def _(one=one):
            one.wait_send()

    @pl.when(holds_half)
    def _():
        over_y.wait_send()

    @pl.when(jnp.logical_not(holds_half))
    def _():
        relay.wait_send()


def run_layer(*operands):
    f32, bf16 = jnp.float32, jnp.bfloat16
    vmem, dma = pltpu.VMEM, pltpu.SemaphoreType.DMA
    scratch = [
        vmem((3, 2, 768, 768), bf16),
        vmem((3, 2, 768, 768), bf16),
        vmem((CHIP, 768), bf16),
        vmem((CHIP + HALF_PACK, 768), bf16),
        vmem((CHIP, 768), bf16),
        vmem((CHIP, 768), bf16),
        vmem((2, CHIP + HALF_PACK, 768), bf16),
        vmem((2, CHIP, 256), bf16),
        vmem((2, HALF_PACK, 384), bf16),
        vmem((6, 3, PACK, 256), bf16),
        vmem((3, PACK, 256), bf16),
        vmem((2, CHIP, 768), bf16),
        vmem((2, CHIP, 768), bf16),
        vmem((2, CHIP, 256), bf16),
        vmem((CHIP + HALF_PACK, HD), f32),
        vmem((CHIP + HALF_PACK, HD), f32),
        vmem((OWN, 768), f32),
        vmem((OWN, 768), f32),
        vmem((OWN, 768), f32),
        vmem((BLK, 768), f32),
        vmem((OWN, 768), bf16),
        vmem((4, OWN, 768), bf16),
        vmem((OWN, 128), f32),
        vmem((2, 1, 640), f32),
        vmem((16, 8, 128), f32),
        vmem((2, 8, 768), f32),
        vmem((SMALL_ROWS, 768), f32),
        vmem((9, SMALL_ROWS, 768), f32),
        vmem((3, 4, BLK, 768), bf16),
        vmem((3, 4, BLK, 768), bf16),
        vmem((3, 4, 80, 768), bf16),
        vmem((3, 4, 48, 768), bf16),
        vmem((3, 4, BLK, 768), bf16),
        vmem((2, 4, 2, 2 * Z_LAST, 768), bf16),
    ]
    scratch += [dma((3, 4))] * 24 + [dma((3, 8))] * 4
    scratch += [dma((4, 3))] * 4 + [dma((4,))] * 2 + [dma((6,))] * 2 + [dma((7,))] * 2
    whole = pl.BlockSpec(memory_space=vmem)
    return pl.pallas_call(
        layer_kernel,
        out_shape=(
            jax.ShapeDtypeStruct((OWN, 768), bf16),
            jax.ShapeDtypeStruct((OWN, 768), f32),
            jax.ShapeDtypeStruct((3, BLK, 192), f32),
            jax.ShapeDtypeStruct((192, BLK), f32),
            jax.ShapeDtypeStruct((BLK, 768), f32),
            jax.ShapeDtypeStruct((BLK, 768), f32),
            jax.ShapeDtypeStruct((4, SMALL_ROWS, 768), f32),
        ),
        in_specs=[whole] * len(operands),
        out_specs=(whole,) * 7,
        scratch_shapes=scratch,
        compiler_params=pltpu.CompilerParams(
            collective_id=0, has_side_effects=True, vmem_limit_bytes=63 * 2**20
        ),
    )(*operands)


def fits_kernel(mesh):
    return dict(mesh.shape) == {"wide": 8, "narrow": 4}


def fused_shards(
    tokens,
    type_ids,
    segment_ids,
    cotangent,
    type_table,
    type_first,
    type_second,
    norm_gains,
    gains_first,
    gains_second,
    biases,
    biases_first,
    biases_second,
    qkv_weight,
    qkv_first,
    qkv_second,
    out_weight,
    out_first,
    out_second,
    up_weight,
    up_first,
    up_second,
    up_bias,
    up_bias_first,
    up_bias_second,
    down_weight,
    down_first,
    down_second,
):
    wide, narrow = lax.axis_index("wide"), lax.axis_index("narrow")
    y, core = narrow // 2, narrow % 2
    activations, input_grad, grad_qkv, grad_out, grad_up, grad_down, small = run_layer(
        qkv_weight, out_weight, up_weight.T, down_weight, up_bias[None, :], tokens, type_ids[None, :],
        cotangent, segment_ids, type_table, norm_gains, biases, type_first, type_second, gains_first,
        gains_second, biases_first, biases_second,
    )
    grad_up = grad_up.T
    bias_part = lax.dynamic_slice_in_dim(small[3], UP_BIAS_ROW + 2 * core + y, 1)[0]
    grad_up_bias = jnp.concatenate(
        [
            lax.dynamic_slice_in_dim(bias_part, wide * Z_FIRST[UP], Z_FIRST[UP]),
            lax.dynamic_slice_in_dim(bias_part, LAST_AT + wide * Z_LAST, Z_LAST),
        ]
    )
    step_sizes = step_rates()
    updates = [
        small[0:3, TYPE_ROW : TYPE_ROW + 2],
        small[0:3, GAIN_ROW : GAIN_ROW + 2],
        small[0:3, BIAS_ROW : BIAS_ROW + 6],
        adam_update(qkv_weight, qkv_first, qkv_second, grad_qkv, step_sizes[3]),
        adam_update(out_weight, out_first, out_second, grad_out, step_sizes[4]),
        adam_update(up_weight, up_first, up_second, grad_up, step_sizes[5]),
        adam_update(up_bias, up_bias_first, up_bias_second, grad_up_bias, step_sizes[6]),
        adam_update(down_weight, down_first, down_second, grad_down, step_sizes[7]),
    ]
    updates = [value for update in updates for value in (update[0], update[1], update[2])]
    return (activations, input_grad, *updates)


def solution(mesh):
    placed = (
        P(("wide", "narrow"), None),
        P(("wide", "narrow")),
        P("wide", None),
        P(("wide", "narrow"), None),
        P(),
        P(),
        P(),
        P(),
        P(),
        P(),
        P(),
        P(),
        P(),
        P(None, "wide", "narrow"),
        P(None, "wide", "narrow"),
        P(None, "wide", "narrow"),
        P("narrow", "wide"),
        P("narrow", "wide"),
        P("narrow", "wide"),
        P(None, ("wide", "narrow")),
        P(None, ("wide", "narrow")),
        P(None, ("wide", "narrow")),
        P(("wide", "narrow")),
        P(("wide", "narrow")),
        P(("wide", "narrow")),
        P(("wide", "narrow"), None),
        P(("wide", "narrow"), None),
        P(("wide", "narrow"), None),
    )
    return jax.shard_map(
        fused_shards if fits_kernel(mesh) else shards,
        mesh=mesh,
        in_specs=placed,
        out_specs=(
            P(("wide", "narrow"), None),
            P(("wide", "narrow"), None),
            P(),
            P(),
            P(),
            P(),
            P(),
            P(),
            P(),
            P(),
            P(),
            P(None, "wide", "narrow"),
            P(None, "wide", "narrow"),
            P(None, "wide", "narrow"),
            P("narrow", "wide"),
            P("narrow", "wide"),
            P("narrow", "wide"),
            P(None, ("wide", "narrow")),
            P(None, ("wide", "narrow")),
            P(None, ("wide", "narrow")),
            P(("wide", "narrow")),
            P(("wide", "narrow")),
            P(("wide", "narrow")),
            P(("wide", "narrow"), None),
            P(("wide", "narrow"), None),
            P(("wide", "narrow"), None),
        ),
        check_vma=False,
    )
```
